256 devices in a mesh: dp: 8 (over y, core), fsdp: 32 (over x, z).
Axes of the slice: x: 4, y: 4, z: 8, core: 2. Of those that a mesh axis runs over, the one named last changes fastest.
Arguments:
- kva_parts: bfloat16 [8, 576, 7168], P('dp', 'fsdp'), may hold values from -60 to 60
- kvb_parts: bfloat16 [8, 16384, 512], P('dp', 'fsdp'), may hold values from -60 to 60
- kva_moment: float32 [576, 7168], P('fsdp'), may hold values from -60 to 60
- kvb_moment: float32 [16384, 512], P('fsdp'), may hold values from -60 to 60
Outputs:
- kva_moment_new: float32 [576, 7168], P('fsdp')
- kvb_moment_new: float32 [16384, 512], P('fsdp')
- kva_update: bfloat16 [576, 7168], P('fsdp')
- kvb_update: bfloat16 [16384, 512], P('fsdp')
The draws below stay inside these ranges and needn't reach their ends.
All inputs are finite; a program needn't handle non-finite values.
Results may differ from the reference program's by a relative error of at most 0.035.
Values may be sent and summed in bfloat16 or wider, within the bound.
No kernel may reach another device: no remote copies, remote signals or barrier semaphores. Data moves between devices by JAX's collectives and lax.ppermute only.
A program may use at most 64 MiB of HBM per device.

```python
import math
import jax
import jax.numpy as jnp
from jax import lax

D = 7168
KV_RANK = 512
ITERS = 3
KVA_ROWS = 576
KVB_ROWS = 16384
N_DP = 8


def scales_for(key, salt, rows, cols):
    key = jax.random.fold_in(key, salt)
    row_key, col_key = jax.random.split(key)
    ramp = jnp.exp(jnp.log(3.0) * jnp.arange(rows, dtype=jnp.float32) / (rows - 1))
    row_scale = jnp.exp(jax.random.uniform(row_key, (rows,), jnp.float32, 0.0, jnp.log(4.0))) * ramp
    col_scale = jnp.exp(jax.random.uniform(col_key, (cols,), jnp.float32, 0.0, jnp.log(10.0)))
    return row_scale[:, None] * col_scale[None, :] / 8.0


def draw_kva_parts(key, part):
    scale = scales_for(key, 1, KVA_ROWS, D)
    key = jax.random.fold_in(key, 11)
    noise_key = jax.random.fold_in(key, 0)
    noise = jax.random.truncated_normal(noise_key, -4.0, 4.0, (N_DP, KVA_ROWS, D), jnp.float32)
    return (0.4 * noise * scale).astype(jnp.bfloat16)


def draw_kvb_parts(key, part):
    scale = scales_for(key, 2, KVB_ROWS, KV_RANK)
    key = jax.random.fold_in(key, 12)
    noise_key = jax.random.fold_in(key, 0)
    noise = jax.random.truncated_normal(noise_key, -4.0, 4.0, (N_DP, KVB_ROWS, KV_RANK), jnp.float32)
    return (0.4 * noise * scale).astype(jnp.bfloat16)


def draw_kva_moment(key, part):
    scale = scales_for(key, 1, KVA_ROWS, D)
    key = jax.random.fold_in(key, 13)
    return jax.random.truncated_normal(key, -4.0, 4.0, (KVA_ROWS, D), jnp.float32) * scale


def draw_kvb_moment(key, part):
    scale = scales_for(key, 2, KVB_ROWS, KV_RANK)
    key = jax.random.fold_in(key, 14)
    return jax.random.truncated_normal(key, -4.0, 4.0, (KVB_ROWS, KV_RANK), jnp.float32) * scale


def setup_inputs(seed: int = 0) -> dict:
    streams_of = jax.random.split(jax.random.key(seed), 5)
    kva_parts = draw_kva_parts(jax.random.fold_in(streams_of[4], 71), 0)
    kvb_parts = draw_kvb_parts(jax.random.fold_in(streams_of[4], 71), 0)
    kva_moment = draw_kva_moment(jax.random.fold_in(streams_of[4], 71), 0)
    kvb_moment = draw_kvb_moment(jax.random.fold_in(streams_of[4], 71), 0)
    return dict(kva_parts=kva_parts, kvb_parts=kvb_parts, kva_moment=kva_moment, kvb_moment=kvb_moment)


first_coeff = 3.4445
second_coeff = -4.775
third_coeff = 2.0315
decay_rate = 0.95
norm_epsilon = 1e-07

def polynomial(gram):
    square = jnp.dot(gram, gram, preferred_element_type=jnp.float32)
    return (second_coeff * gram.astype(jnp.float32) + third_coeff * square).astype(jnp.bfloat16)

def reference(kva_parts, kvb_parts, kva_moment, kvb_moment):
    grad_a = lax.optimization_barrier(jnp.sum(kva_parts.astype(jnp.float32), axis=0))
    grad_b = lax.optimization_barrier(jnp.sum(kvb_parts.astype(jnp.float32), axis=0))
    moment_a = decay_rate * kva_moment + grad_a
    moment_b = decay_rate * kvb_moment + grad_b
    push_a = grad_a + decay_rate * moment_a
    push_b = grad_b + decay_rate * moment_b
    short_a = (push_a / (jnp.sqrt(jnp.sum(push_a * push_a)) + norm_epsilon)).astype(jnp.bfloat16)
    long_b = (push_b / (jnp.sqrt(jnp.sum(push_b * push_b)) + norm_epsilon)).astype(jnp.bfloat16)
    scale_a = math.sqrt(max(KVA_ROWS, D))
    scale_b = math.sqrt(max(KVB_ROWS, KV_RANK))
    for step in range(ITERS):
        gram_a = lax.dot_general(short_a, short_a, (((1,), (1,)), ((), ())), preferred_element_type=jnp.float32).astype(jnp.bfloat16)
        gram_b = lax.dot_general(long_b, long_b, (((0,), (0,)), ((), ())), preferred_element_type=jnp.float32).astype(jnp.bfloat16)
        poly_a = polynomial(gram_a)
        poly_b = polynomial(gram_b)
        next_a = first_coeff * short_a.astype(jnp.float32) + jnp.dot(poly_a, short_a, preferred_element_type=jnp.float32)
        next_b = first_coeff * long_b.astype(jnp.float32) + jnp.dot(long_b, poly_b, preferred_element_type=jnp.float32)
        if step + 1 < ITERS:
            short_a = next_a.astype(jnp.bfloat16)
            long_b = next_b.astype(jnp.bfloat16)
        else:
            short_a = (next_a * scale_a).astype(jnp.bfloat16)
            long_b = (next_b * scale_b).astype(jnp.bfloat16)
    return (moment_a, moment_b, short_a, long_b)
```

```python
import functools
import math

import jax
import jax.numpy as jnp
from jax import lax
from jax.experimental import pallas as pl
from jax.experimental.pallas import tpu as pltpu
from jax.sharding import Mesh, PartitionSpec as P

D = 7168
KV_RANK = 512
KVA_ROWS = 576
KVB_ROWS = 16384
DP = ("y", "c")
FSDP = ("x", "z")
N_DP = 8
N_FSDP = 32
CHUNK = D // N_DP
GROUPS = CHUNK // 128
MAIN = 16
WIDE = CHUNK + 128

c1 = 3.4445
c2 = -4.775
c3 = 2.0315
decay_rate = 0.95
norm_epsilon = 1e-07
f32 = jnp.float32
bf16 = jnp.bfloat16
VMEM_LIMIT = 48 * 1024 * 1024


def call(body, out_shape, n_scalar=0, n_in=1, scratch=()):
    return pl.pallas_call(
        body,
        out_shape=out_shape,
        in_specs=[pl.BlockSpec(memory_space=pltpu.SMEM)] * n_scalar
        + [pl.BlockSpec(memory_space=pltpu.VMEM)] * n_in,
        out_specs=jax.tree.map(lambda _: pl.BlockSpec(memory_space=pltpu.VMEM), out_shape),
        scratch_shapes=list(scratch),
        compiler_params=pltpu.CompilerParams(vmem_limit_bytes=VMEM_LIMIT),
    )


def shape(dims, dtype):
    return jax.ShapeDtypeStruct(dims, dtype)


def tail_tile(rows):
    pieces = [rows[:, 128 * k : 128 * k + 128] for k in range(GROUPS)]
    return jnp.concatenate(pieces + [jnp.zeros((2, 128), f32)], axis=0)


def pack_body(x_ref, o_ref):
    for d in range(N_DP):
        lanes = slice(d * CHUNK, (d + 1) * CHUNK)
        o_ref[d, :, :CHUNK] = x_ref[0, :MAIN, lanes]
        o_ref[d, :, CHUNK:] = tail_tile(x_ref[0, MAIN:, lanes].astype(f32)).astype(bf16)


def push_a_body(d_ref, parts_ref, m_ref, g_ref, x_ref):
    start = pl.multiple_of(d_ref[0] * CHUNK, 128)
    grad = parts_ref[0].astype(f32)
    for r in range(1, N_DP):
        grad += parts_ref[r].astype(f32)
    g_ref[...] = grad.astype(bf16)
    m_main = m_ref[:MAIN, pl.ds(start, CHUNK)]
    m_tail = tail_tile(m_ref[MAIN:, pl.ds(start, CHUNK)])
    moment = decay_rate * jnp.concatenate([m_main, m_tail], axis=1) + grad
    push = (grad + decay_rate * moment).astype(bf16)
    for r in range(N_FSDP):
        x_ref[r] = push


def moment_a_body(g_ref, m_ref, o_ref):
    for d in range(N_DP):
        lanes = slice(d * CHUNK, (d + 1) * CHUNK)
        o_ref[:MAIN, lanes] = decay_rate * m_ref[:MAIN, lanes] + g_ref[d, :, :CHUNK].astype(f32)
        tail = g_ref[d, :, CHUNK:].astype(f32)
        for k in range(GROUPS):
            piece = slice(d * CHUNK + 128 * k, d * CHUNK + 128 * k + 128)
            o_ref[MAIN:, piece] = decay_rate * m_ref[MAIN:, piece] + tail[2 * k : 2 * k + 2]


def gram_a_body(x_ref, g_ref, full_ref):
    full_ref[: N_FSDP * MAIN] = x_ref[:, :, :CHUNK].reshape(N_FSDP * MAIN, CHUNK)
    tail = x_ref[:, :, CHUNK:].reshape(N_FSDP * MAIN, 128)
    rows = 2 * N_FSDP
    r = lax.broadcasted_iota(jnp.int32, (rows, N_FSDP * MAIN), 0)
    c = lax.broadcasted_iota(jnp.int32, (rows, N_FSDP * MAIN), 1)
    first = MAIN * lax.shift_right_logical(r, 1) + (r & 1)
    for k in range(GROUPS):
        pick = jnp.where(c == first + 2 * k, 1.0, 0.0).astype(bf16)
        full_ref[N_FSDP * MAIN :, 128 * k : 128 * k + 128] = jnp.dot(
            pick, tail, preferred_element_type=f32
        ).astype(bf16)
    x = full_ref[...]
    g_ref[...] = lax.dot_general(
        x, x, (((1,), (1,)), ((), ())), preferred_element_type=f32
    ).astype(bf16)


def gram_b_body(d_ref, y_ref, o_ref, scratch):
    y = y_ref[...]
    scratch[...] = lax.dot_general(y, y, (((0,), (0,)), ((), ())), preferred_element_type=f32)
    rows = KV_RANK // N_DP
    piece = scratch[pl.ds(pl.multiple_of(d_ref[0] * rows, rows), rows), :].astype(bf16)
    for r in range(o_ref.shape[0]):
        o_ref[r] = piece


def mm(a, b):
    return jnp.dot(a.astype(bf16), b.astype(bf16), preferred_element_type=f32)


def gram_scale(gram):
    n = gram.shape[0]
    r = lax.broadcasted_iota(jnp.int32, (n, n), 0)
    c = lax.broadcasted_iota(jnp.int32, (n, n), 1)
    squares = jnp.sum(jnp.where(r == c, gram, 0.0))
    return 1.0 / (jnp.sqrt(squares) + norm_epsilon)


def two_steps(g0):
    d0 = c2 * g0 + c3 * mm(g0, g0)
    t0 = c1 * g0 + mm(d0, g0)
    g1 = c1 * t0 + mm(d0, t0)
    d1 = c2 * g1 + c3 * mm(g1, g1)
    d01 = c1 * (d0 + d1) + mm(d1, d0)
    t1 = c1 * g1 + mm(d1, g1)
    g2 = c1 * t1 + mm(d1, t1)
    return d01, g2


def finish_b_body(g_ref, y_ref, o_ref):
    gram = g_ref[...].astype(f32)
    s = gram_scale(gram)
    d01, g2 = two_steps(gram * (s * s))
    d2 = c2 * g2 + c3 * mm(g2, g2)
    rest = c1 * d01 + c1 * c1 * d2 + mm(d2, d01)
    y = y_ref[...]
    total = s * math.sqrt(max(KVB_ROWS, KV_RANK))
    out = (c1 * c1 * c1) * y.astype(f32) + mm(y, rest)
    o_ref[...] = (out * total).astype(bf16)


def finish_a_body(f_ref, g_ref, x_ref, o_ref, d01_ref, g2_ref):
    f = f_ref[0]
    gram = g_ref[...].astype(f32)
    s = gram_scale(gram)
    d01, g2 = two_steps(gram * (s * s))
    d01_ref[...] = d01
    g2_ref[...] = g2
    main = pl.ds(pl.multiple_of(f * MAIN, MAIN), MAIN)
    base = N_FSDP * MAIN + 8 * lax.shift_right_logical(f, 2)
    tail = pl.ds(pl.multiple_of(base, 8), 8)

    def rows(ref):
        return jnp.concatenate([ref[main, :], ref[tail, :]], axis=0)

    g2_rows = rows(g2_ref)
    d2 = c2 * g2_rows + c3 * mm(g2_rows, g2)
    rest = c1 * rows(d01_ref) + c1 * c1 * d2 + mm(d2, d01)
    x_rows = jnp.concatenate([x_ref[main, :].astype(f32), x_ref[pl.ds(pl.multiple_of(N_FSDP * MAIN + 16 * lax.shift_right_logical(f, 3), 16), 16), :].astype(f32)], axis=0)
    total = s * math.sqrt(max(KVA_ROWS, D))
    moved = mm(rest, x_ref[...])
    out = ((c1 * c1 * c1) * x_rows[:MAIN] + moved[:MAIN]) * total
    o_main = out.astype(bf16)
    q = f & 3
    h = f & 7
    x_tail = x_rows[MAIN : MAIN + 2]
    for j in range(1, 8):
        x_tail = jnp.where(h == j, x_rows[MAIN + 2 * j : MAIN + 2 * j + 2], x_tail)
    m_tail = moved[MAIN : MAIN + 2]
    for j in range(1, 4):
        m_tail = jnp.where(q == j, moved[MAIN + 2 * j : MAIN + 2 * j + 2], m_tail)
    o_tail = tail_tile(((c1 * c1 * c1) * x_tail + m_tail) * total).astype(bf16)
    for r in range(N_DP):
        o_ref[r, :, :CHUNK] = o_main
        o_ref[r, :, CHUNK:] = o_tail


def unpack_body(u_ref, o_ref):
    for d in range(N_DP):
        o_ref[:MAIN, d * CHUNK : (d + 1) * CHUNK] = u_ref[d, :, :CHUNK]
        tail = u_ref[d, :, CHUNK:].astype(f32)
        for k in range(GROUPS):
            piece = slice(d * CHUNK + 128 * k, d * CHUNK + 128 * k + 128)
            o_ref[MAIN:, piece] = tail[2 * k : 2 * k + 2].astype(bf16)


def exchange(x, axis):
    return lax.all_to_all(x, axis, split_axis=0, concat_axis=0, tiled=True)


def gather(x, axis, n):
    return exchange(jnp.broadcast_to(x[None], (n,) + x.shape), axis)


def total_of(x):
    return jnp.sum(x.astype(f32), axis=0)


def local(kva_parts, kvb_parts, kva_moment, kvb_moment):
    d = (lax.axis_index(DP)).astype(jnp.int32).reshape(1)
    f = (lax.axis_index(FSDP)).astype(jnp.int32).reshape(1)

    packed = call(pack_body, shape((N_DP, MAIN, WIDE), bf16))(kva_parts)
    grad_a, push_a = call(
        push_a_body,
        (shape((MAIN, WIDE), bf16), shape((N_FSDP, MAIN, WIDE), bf16)),
        1,
        2,
    )(d, exchange(packed, DP), kva_moment)
    all_a = exchange(push_a, FSDP)

    grad_b = total_of(exchange(kvb_parts.reshape(N_DP, -1, KV_RANK), DP)).astype(bf16)
    grad_b = gather(grad_b, DP, N_DP).reshape(-1, KV_RANK).astype(f32)
    moment_b = decay_rate * kvb_moment + grad_b
    long_b = (grad_b + decay_rate * moment_b).astype(bf16)
    moment_a = call(moment_a_body, shape(kva_moment.shape, f32), 0, 2)(
        gather(grad_a, DP, N_DP), kva_moment
    )

    piece_b = call(
        gram_b_body,
        shape((8, KV_RANK // N_DP, KV_RANK), bf16),
        1,
        1,
        [pltpu.VMEM((KV_RANK, KV_RANK), f32)],
    )(d, long_b)
    piece_b = total_of(exchange(piece_b, "z")).astype(bf16)
    piece_b = total_of(gather(piece_b, "x", 4)).astype(bf16)
    gram_b = gather(piece_b, DP, N_DP).reshape(KV_RANK, KV_RANK)

    gram_a, short_a = call(
        gram_a_body, (shape((KVA_ROWS, KVA_ROWS), bf16), shape((KVA_ROWS, CHUNK), bf16))
    )(all_a)
    gram_a = total_of(exchange(gram_a.reshape(N_DP, -1, KVA_ROWS), DP)).astype(bf16)
    gram_a = gather(gram_a, DP, N_DP).reshape(KVA_ROWS, KVA_ROWS)

    update_a = call(
        finish_a_body,
        shape((N_DP, MAIN, WIDE), bf16),
        1,
        2,
        [pltpu.VMEM((KVA_ROWS, KVA_ROWS), f32)] * 2,
    )(f, gram_a, short_a)
    update_a = call(unpack_body, shape(kva_moment.shape, bf16))(exchange(update_a, DP))
    update_b = call(finish_b_body, shape(long_b.shape, bf16), 0, 2)(gram_b, long_b)
    return (moment_a, moment_b, update_a, update_b)


def solution(mesh):
    fine = Mesh(mesh.devices.reshape(4, 2, 4, 8), DP + FSDP)
    return jax.shard_map(
        local,
        mesh=fine,
        in_specs=(P(DP, FSDP, None), P(DP, FSDP, None), P(FSDP, None), P(FSDP, None)),
        out_specs=(P(FSDP, None), P(FSDP, None), P(FSDP, None), P(FSDP, None)),
        check_vma=False,
    )
```

```python
import functools
import math

import jax
import jax.numpy as jnp
from jax import lax
from jax.experimental import pallas as pl
from jax.experimental.pallas import tpu as pltpu
from jax.sharding import Mesh, PartitionSpec as P

D = 7168
KV_RANK = 512
KVA_ROWS = 576
KVB_ROWS = 16384
DP = ("y", "c")
FSDP = ("x", "z")
N_DP = 8
N_FSDP = 32
CHUNK = D // N_DP
GROUPS = CHUNK // 128
MAIN = 16
WIDE = CHUNK + 128
ROWS_B = KVB_ROWS // N_FSDP // N_DP
HALF_B = ROWS_B // 2
BLOCKS = 5

c1 = 3.4445
c2 = -4.775
c3 = 2.0315
decay_rate = 0.95
norm_epsilon = 1e-07
f32 = jnp.float32
bf16 = jnp.bfloat16
VMEM_LIMIT = 48 * 1024 * 1024


def call(body, out_shape, n_scalar=0, n_in=1, scratch=()):
    return pl.pallas_call(
        body,
        out_shape=out_shape,
        in_specs=[pl.BlockSpec(memory_space=pltpu.SMEM)] * n_scalar
        + [pl.BlockSpec(memory_space=pltpu.VMEM)] * n_in,
        out_specs=jax.tree.map(lambda _: pl.BlockSpec(memory_space=pltpu.VMEM), out_shape),
        scratch_shapes=list(scratch),
        compiler_params=pltpu.CompilerParams(vmem_limit_bytes=VMEM_LIMIT),
    )


def shape(dims, dtype):
    return jax.ShapeDtypeStruct(dims, dtype)


def tail_tile(rows):
    pieces = [rows[:, 128 * k : 128 * k + 128] for k in range(GROUPS)]
    return jnp.concatenate(pieces + [jnp.zeros((2, 128), f32)], axis=0)


def pack_body(a_ref, o_ref):
    for d in range(N_DP):
        lanes = slice(d * CHUNK, (d + 1) * CHUNK)
        o_ref[d, :, :CHUNK] = a_ref[0, :MAIN, lanes]
        o_ref[d, :, CHUNK:] = tail_tile(a_ref[0, MAIN:, lanes].astype(f32)).astype(bf16)


def split_b_body(d_ref, b_ref, *o_refs):
    for k in range(N_DP):
        rank = (d_ref[0] + k) & (N_DP - 1)
        o_refs[k][...] = b_ref[0, pl.ds(pl.multiple_of(rank * ROWS_B, ROWS_B), ROWS_B)]


def push_a_body(d_ref, parts_ref, m_ref, g_ref, x_ref):
    start = pl.multiple_of(d_ref[0] * CHUNK, 128)
    grad = parts_ref[0].astype(f32)
    for r in range(1, N_DP):
        grad += parts_ref[r].astype(f32)
    g_ref[...] = grad.astype(bf16)
    m_main = m_ref[:MAIN, pl.ds(start, CHUNK)]
    m_tail = tail_tile(m_ref[MAIN:, pl.ds(start, CHUNK)])
    moment = decay_rate * jnp.concatenate([m_main, m_tail], axis=1) + grad
    push = (grad + decay_rate * moment).astype(bf16)
    for r in range(N_FSDP):
        x_ref[r] = push


def join_body(g_ref, *refs):
    o_ref = refs[-1]
    o_ref[:MAIN] = g_ref[...]
    grad = refs[0][...].astype(f32)
    for r in refs[1:-1]:
        grad += r[...].astype(f32)
    grad = grad.astype(bf16)
    for h in range(2):
        o_ref[MAIN:, h * KV_RANK : (h + 1) * KV_RANK] = grad[h * HALF_B : (h + 1) * HALF_B]


def moment_a_body(g_ref, m_ref, o_ref):
    for d in range(N_DP):
        lanes = slice(d * CHUNK, (d + 1) * CHUNK)
        o_ref[:MAIN, lanes] = decay_rate * m_ref[:MAIN, lanes] + g_ref[d, :MAIN, :CHUNK].astype(f32)
        tail = g_ref[d, :MAIN, CHUNK:].astype(f32)
        for k in range(GROUPS):
            piece = slice(d * CHUNK + 128 * k, d * CHUNK + 128 * k + 128)
            o_ref[MAIN:, piece] = decay_rate * m_ref[MAIN:, piece] + tail[2 * k : 2 * k + 2]


def moment_b_body(d_ref, g_ref, m_ref, o_ref, y_ref, p_ref, scratch):
    for d in range(N_DP):
        for h in range(2):
            first = d * 2 * HALF_B + h * HALF_B
            rows = slice(first, first + HALF_B)
            grad = g_ref[d, MAIN:, h * KV_RANK : (h + 1) * KV_RANK].astype(f32)
            moment = decay_rate * m_ref[rows] + grad
            o_ref[rows] = moment
            y_ref[rows] = (grad + decay_rate * moment).astype(bf16)
    y = y_ref[...]
    scratch[...] = lax.dot_general(y, y, (((0,), (0,)), ((), ())), preferred_element_type=f32)
    rows = KV_RANK // N_DP
    p_ref[...] = scratch[pl.ds(pl.multiple_of(d_ref[0] * rows, rows), rows), :].astype(bf16)


def gram_a_body(x_ref, g_ref, full_ref, gram_ref):
    full_ref[: N_FSDP * MAIN] = x_ref[:, :, :CHUNK].reshape(N_FSDP * MAIN, CHUNK)
    tail = x_ref[:, :, CHUNK:].reshape(N_FSDP * MAIN, 128)
    rows = 2 * N_FSDP
    r = lax.broadcasted_iota(jnp.int32, (rows, N_FSDP * MAIN), 0)
    c = lax.broadcasted_iota(jnp.int32, (rows, N_FSDP * MAIN), 1)
    first = MAIN * lax.shift_right_logical(r, 1) + (r & 1)
    for k in range(GROUPS):
        pick = jnp.where(c == first + 2 * k, 1.0, 0.0).astype(bf16)
        full_ref[N_FSDP * MAIN :, 128 * k : 128 * k + 128] = jnp.dot(
            pick, tail, preferred_element_type=f32
        ).astype(bf16)
    x = full_ref[...]
    gram_ref[...] = jnp.zeros_like(gram_ref)
    gram_ref[:KVA_ROWS, :KVA_ROWS] = lax.dot_general(
        x, x, (((1,), (1,)), ((), ())), preferred_element_type=f32
    )
    for i in range(BLOCKS):
        for h in range(2):
            rows = slice(128 * i + 64 * h, 128 * i + 64 * h + 64)
            for j in range(3):
                k = (i + j) % BLOCKS
                g_ref[h, 64 * i : 64 * i + 64, 128 * j : 128 * j + 128] = gram_ref[
                    rows, 128 * k : 128 * k + 128
                ].astype(bf16)


def whole_gram(t_ref, gram_ref):
    for i in range(BLOCKS):
        for j in range(3):
            k = (i + j) % BLOCKS
            block = jnp.concatenate(
                [t_ref[h, 64 * i : 64 * i + 64, 128 * j : 128 * j + 128] for h in range(2)], axis=0
            ).astype(f32)
            gram_ref[128 * i : 128 * i + 128, 128 * k : 128 * k + 128] = block
            if j:
                gram_ref[128 * k : 128 * k + 128, 128 * i : 128 * i + 128] = block.T
    return gram_ref[:KVA_ROWS, :KVA_ROWS]


def mm(a, b):
    return jnp.dot(a.astype(bf16), b.astype(bf16), preferred_element_type=f32)


def gram_scale(gram):
    n = gram.shape[0]
    r = lax.broadcasted_iota(jnp.int32, (n, n), 0)
    c = lax.broadcasted_iota(jnp.int32, (n, n), 1)
    squares = jnp.sum(jnp.where(r == c, gram, 0.0))
    return 1.0 / (jnp.sqrt(squares) + norm_epsilon)


def two_steps(g0):
    d0 = c2 * g0 + c3 * mm(g0, g0)
    t0 = c1 * g0 + mm(d0, g0)
    g1 = c1 * t0 + mm(d0, t0)
    d1 = c2 * g1 + c3 * mm(g1, g1)
    d01 = c1 * (d0 + d1) + mm(d1, d0)
    t1 = c1 * g1 + mm(d1, g1)
    g2 = c1 * t1 + mm(d1, t1)
    return d01, g2


def finish_b_body(g_ref, y_ref, o_ref):
    gram = g_ref[...].astype(f32)
    s = gram_scale(gram)
    d01, g2 = two_steps(gram * (s * s))
    d2 = c2 * g2 + c3 * mm(g2, g2)
    rest = c1 * d01 + c1 * c1 * d2 + mm(d2, d01)
    y = y_ref[...]
    total = s * math.sqrt(max(KVB_ROWS, KV_RANK))
    out = (c1 * c1 * c1) * y.astype(f32) + mm(y, rest)
    o_ref[...] = (out * total).astype(bf16)


def finish_a_body(f_ref, g_ref, x_ref, o_ref, gram_ref, d01_ref, g2_ref):
    f = f_ref[0]
    gram = whole_gram(g_ref, gram_ref)
    s = gram_scale(gram)
    d01, g2 = two_steps(gram * (s * s))
    d01_ref[...] = d01
    g2_ref[...] = g2
    main = pl.ds(pl.multiple_of(f * MAIN, MAIN), MAIN)
    base = N_FSDP * MAIN + 8 * lax.shift_right_logical(f, 2)
    tail = pl.ds(pl.multiple_of(base, 8), 8)

    def rows(ref):
        return jnp.concatenate([ref[main, :], ref[tail, :]], axis=0)

    g2_rows = rows(g2_ref)
    d2 = c2 * g2_rows + c3 * mm(g2_rows, g2)
    rest = c1 * rows(d01_ref) + c1 * c1 * d2 + mm(d2, d01)
    x_rows = jnp.concatenate([x_ref[main, :].astype(f32), x_ref[pl.ds(pl.multiple_of(N_FSDP * MAIN + 16 * lax.shift_right_logical(f, 3), 16), 16), :].astype(f32)], axis=0)
    total = s * math.sqrt(max(KVA_ROWS, D))
    moved = mm(rest, x_ref[...])
    out = ((c1 * c1 * c1) * x_rows[:MAIN] + moved[:MAIN]) * total
    o_main = out.astype(bf16)
    q = f & 3
    h = f & 7
    x_tail = x_rows[MAIN : MAIN + 2]
    for j in range(1, 8):
        x_tail = jnp.where(h == j, x_rows[MAIN + 2 * j : MAIN + 2 * j + 2], x_tail)
    m_tail = moved[MAIN : MAIN + 2]
    for j in range(1, 4):
        m_tail = jnp.where(q == j, moved[MAIN + 2 * j : MAIN + 2 * j + 2], m_tail)
    o_tail = tail_tile(((c1 * c1 * c1) * x_tail + m_tail) * total).astype(bf16)
    for r in range(N_DP):
        o_ref[r, :, :CHUNK] = o_main
        o_ref[r, :, CHUNK:] = o_tail


def unpack_body(u_ref, o_ref):
    for d in range(N_DP):
        o_ref[:MAIN, d * CHUNK : (d + 1) * CHUNK] = u_ref[d, :, :CHUNK]
        tail = u_ref[d, :, CHUNK:].astype(f32)
        for k in range(GROUPS):
            piece = slice(d * CHUNK + 128 * k, d * CHUNK + 128 * k + 128)
            o_ref[MAIN:, piece] = tail[2 * k : 2 * k + 2].astype(bf16)


def exchange(x, axis):
    return lax.all_to_all(x, axis, split_axis=0, concat_axis=0, tiled=True)


def total_of(x):
    return jnp.sum(x.astype(f32), axis=0)


def shift(x, axis, n, k):
    return lax.ppermute(x, axis, [(i, (i + k) % n) for i in range(n)])


def sum_over(x, axis, n):
    total = x.astype(f32)
    for y in [shift(x, axis, n, k) for k in range(1, n)]:
        total += y.astype(f32)
    return total.astype(bf16)


def local(kva_parts, kvb_parts, kva_moment, kvb_moment):
    d = lax.axis_index(DP).astype(jnp.int32).reshape(1)
    f = lax.axis_index(FSDP).astype(jnp.int32).reshape(1)
    rows_b = KV_RANK // N_DP
    tall = MAIN + HALF_B

    packed = call(pack_body, shape((N_DP, MAIN, WIDE), bf16))(kva_parts)
    terms_b = call(split_b_body, [shape((ROWS_B, KV_RANK), bf16)] * N_DP, 1, 1)(d, kvb_parts)
    terms_b = [terms_b[0]] + [shift(terms_b[k], DP, N_DP, k) for k in range(1, N_DP)]
    grads, push_a = call(
        push_a_body,
        (shape((MAIN, WIDE), bf16), shape((N_FSDP, MAIN, WIDE), bf16)),
        1,
        2,
    )(d, exchange(packed, DP), kva_moment)
    all_a = exchange(push_a, FSDP)

    grads = call(join_body, shape((tall, WIDE), bf16), 0, 1 + N_DP)(grads, *terms_b)
    grads = lax.all_gather(grads, DP)
    moment_a = call(moment_a_body, shape(kva_moment.shape, f32), 0, 2)(grads, kva_moment)
    moment_b, long_b, piece_b = call(
        moment_b_body,
        (
            shape(kvb_moment.shape, f32),
            shape(kvb_moment.shape, bf16),
            shape((rows_b, KV_RANK), bf16),
        ),
        1,
        2,
        [pltpu.VMEM((KV_RANK, KV_RANK), f32)],
    )(d, grads, kvb_moment)
    piece_b = sum_over(piece_b, "z", 8)
    piece_b = sum_over(piece_b, "x", 4)
    gram_b = lax.all_gather(piece_b, DP).reshape(KV_RANK, KV_RANK)

    gram_a, short_a = call(
        gram_a_body,
        (shape((2, 64 * BLOCKS, 384), bf16), shape((KVA_ROWS, CHUNK), bf16)),
        0,
        1,
        [pltpu.VMEM((128 * BLOCKS, 128 * BLOCKS), f32)],
    )(all_a)
    gram_a = lax.all_gather(gram_a, "c")
    gram_a = lax.dynamic_index_in_dim(gram_a, lax.axis_index("c"), axis=1, keepdims=False)
    gram_a = sum_over(total_of(gram_a).astype(bf16), "y", 4)
    gram_a = lax.all_gather(gram_a, "c")

    update_a = call(
        finish_a_body,
        shape((N_DP, MAIN, WIDE), bf16),
        1,
        2,
        [pltpu.VMEM((128 * BLOCKS, 128 * BLOCKS), f32)]
        + [pltpu.VMEM((KVA_ROWS, KVA_ROWS), f32)] * 2,
    )(f, gram_a, short_a)
    update_a = call(unpack_body, shape(kva_moment.shape, bf16))(exchange(update_a, DP))
    update_b = call(finish_b_body, shape(long_b.shape, bf16), 0, 2)(gram_b, long_b)
    return (moment_a, moment_b, update_a, update_b)


def solution(mesh):
    fine = Mesh(mesh.devices.reshape(4, 2, 4, 8), DP + FSDP)
    return jax.shard_map(
        local,
        mesh=fine,
        in_specs=(P(DP, FSDP, None), P(DP, FSDP, None), P(FSDP, None), P(FSDP, None)),
        out_specs=(P(FSDP, None), P(FSDP, None), P(FSDP, None), P(FSDP, None)),
        check_vma=False,
    )
```

```python
import functools
import math

import jax
import jax.numpy as jnp
from jax import lax
from jax.experimental import pallas as pl
from jax.experimental.pallas import tpu as pltpu
from jax.sharding import Mesh, PartitionSpec as P

D = 7168
KV_RANK = 512
KVA_ROWS = 576
KVB_ROWS = 16384
DP = ("y", "c")
FSDP = ("x", "z")
N_DP = 8
N_FSDP = 32
CHUNK = D // N_DP
GROUPS = CHUNK // 128
MAIN = 16
WIDE = CHUNK + 128
BLOCKS = 5

c1 = 3.4445
c2 = -4.775
c3 = 2.0315
decay_rate = 0.95
norm_epsilon = 1e-07
f32 = jnp.float32
bf16 = jnp.bfloat16
VMEM_LIMIT = 48 * 1024 * 1024


def call(body, out_shape, n_scalar=0, n_in=1, scratch=()):
    return pl.pallas_call(
        body,
        out_shape=out_shape,
        in_specs=[pl.BlockSpec(memory_space=pltpu.SMEM)] * n_scalar
        + [pl.BlockSpec(memory_space=pltpu.VMEM)] * n_in,
        out_specs=jax.tree.map(lambda _: pl.BlockSpec(memory_space=pltpu.VMEM), out_shape),
        scratch_shapes=list(scratch),
        compiler_params=pltpu.CompilerParams(vmem_limit_bytes=VMEM_LIMIT),
    )


def shape(dims, dtype):
    return jax.ShapeDtypeStruct(dims, dtype)


def tail_tile(rows):
    pieces = [rows[:, 128 * k : 128 * k + 128] for k in range(GROUPS)]
    return jnp.concatenate(pieces + [jnp.zeros((2, 128), f32)], axis=0)


def pack_body(c_ref, a_ref, b_ref, o_ref, send_ref):
    rows = send_ref.shape[0]
    send_ref[...] = b_ref[0, pl.ds(pl.multiple_of((1 - c_ref[0]) * rows, rows), rows)]
    for d in range(N_DP):
        lanes = slice(d * CHUNK, (d + 1) * CHUNK)
        o_ref[d, :, :CHUNK] = a_ref[0, :MAIN, lanes]
        o_ref[d, :, CHUNK:] = tail_tile(a_ref[0, MAIN:, lanes].astype(f32)).astype(bf16)


def push_a_body(d_ref, parts_ref, m_ref, g_ref, x_ref):
    start = pl.multiple_of(d_ref[0] * CHUNK, 128)
    grad = parts_ref[0].astype(f32)
    for r in range(1, N_DP):
        grad += parts_ref[r].astype(f32)
    g_ref[...] = grad.astype(bf16)
    m_main = m_ref[:MAIN, pl.ds(start, CHUNK)]
    m_tail = tail_tile(m_ref[MAIN:, pl.ds(start, CHUNK)])
    moment = decay_rate * jnp.concatenate([m_main, m_tail], axis=1) + grad
    push = (grad + decay_rate * moment).astype(bf16)
    for r in range(N_FSDP):
        x_ref[r] = push


def moment_a_body(g_ref, m_ref, o_ref):
    for d in range(N_DP):
        lanes = slice(d * CHUNK, (d + 1) * CHUNK)
        o_ref[:MAIN, lanes] = decay_rate * m_ref[:MAIN, lanes] + g_ref[d, :, :CHUNK].astype(f32)
        tail = g_ref[d, :, CHUNK:].astype(f32)
        for k in range(GROUPS):
            piece = slice(d * CHUNK + 128 * k, d * CHUNK + 128 * k + 128)
            o_ref[MAIN:, piece] = decay_rate * m_ref[MAIN:, piece] + tail[2 * k : 2 * k + 2]


def half_b_body(c_ref, b_ref, x_ref, o_ref):
    rows = o_ref.shape[0]
    half = b_ref[0, pl.ds(pl.multiple_of(c_ref[0] * rows, rows), rows)]
    o_ref[...] = (half.astype(f32) + x_ref[...].astype(f32)).astype(bf16)


def moment_b_body(d_ref, g_ref, m_ref, o_ref, y_ref, p_ref, scratch):
    grad = g_ref[...].astype(f32)
    moment = decay_rate * m_ref[...] + grad
    o_ref[...] = moment
    y = (grad + decay_rate * moment).astype(bf16)
    y_ref[...] = y
    scratch[...] = lax.dot_general(y, y, (((0,), (0,)), ((), ())), preferred_element_type=f32)
    rows = KV_RANK // N_DP
    p_ref[...] = scratch[pl.ds(pl.multiple_of(d_ref[0] * rows, rows), rows), :].astype(bf16)


def gram_a_body(x_ref, g_ref, full_ref, gram_ref):
    full_ref[: N_FSDP * MAIN] = x_ref[:, :, :CHUNK].reshape(N_FSDP * MAIN, CHUNK)
    tail = x_ref[:, :, CHUNK:].reshape(N_FSDP * MAIN, 128)
    rows = 2 * N_FSDP
    r = lax.broadcasted_iota(jnp.int32, (rows, N_FSDP * MAIN), 0)
    c = lax.broadcasted_iota(jnp.int32, (rows, N_FSDP * MAIN), 1)
    first = MAIN * lax.shift_right_logical(r, 1) + (r & 1)
    for k in range(GROUPS):
        pick = jnp.where(c == first + 2 * k, 1.0, 0.0).astype(bf16)
        full_ref[N_FSDP * MAIN :, 128 * k : 128 * k + 128] = jnp.dot(
            pick, tail, preferred_element_type=f32
        ).astype(bf16)
    x = full_ref[...]
    gram_ref[...] = jnp.zeros_like(gram_ref)
    gram_ref[:KVA_ROWS, :KVA_ROWS] = lax.dot_general(
        x, x, (((1,), (1,)), ((), ())), preferred_element_type=f32
    )
    for i in range(BLOCKS):
        for h in range(2):
            rows = slice(128 * i + 64 * h, 128 * i + 64 * h + 64)
            for j in range(3):
                k = (i + j) % BLOCKS
                g_ref[h, 64 * i : 64 * i + 64, 128 * j : 128 * j + 128] = gram_ref[
                    rows, 128 * k : 128 * k + 128
                ].astype(bf16)


def whole_gram(t_ref, gram_ref):
    for i in range(BLOCKS):
        for j in range(3):
            k = (i + j) % BLOCKS
            block = jnp.concatenate(
                [t_ref[h, 64 * i : 64 * i + 64, 128 * j : 128 * j + 128] for h in range(2)], axis=0
            ).astype(f32)
            gram_ref[128 * i : 128 * i + 128, 128 * k : 128 * k + 128] = block
            if j:
                gram_ref[128 * k : 128 * k + 128, 128 * i : 128 * i + 128] = block.T
    return gram_ref[:KVA_ROWS, :KVA_ROWS]


def mm(a, b):
    return jnp.dot(a.astype(bf16), b.astype(bf16), preferred_element_type=f32)


def gram_scale(gram):
    n = gram.shape[0]
    r = lax.broadcasted_iota(jnp.int32, (n, n), 0)
    c = lax.broadcasted_iota(jnp.int32, (n, n), 1)
    squares = jnp.sum(jnp.where(r == c, gram, 0.0))
    return 1.0 / (jnp.sqrt(squares) + norm_epsilon)


def two_steps(g0):
    d0 = c2 * g0 + c3 * mm(g0, g0)
    t0 = c1 * g0 + mm(d0, g0)
    g1 = c1 * t0 + mm(d0, t0)
    d1 = c2 * g1 + c3 * mm(g1, g1)
    d01 = c1 * (d0 + d1) + mm(d1, d0)
    t1 = c1 * g1 + mm(d1, g1)
    g2 = c1 * t1 + mm(d1, t1)
    return d01, g2


def finish_b_body(i_ref, g0_ref, g1_ref, g2_ref, g3_ref, y_ref, o_ref, gram_ref):
    rows = KV_RANK // 4
    for k, g_ref in enumerate((g0_ref, g1_ref, g2_ref, g3_ref)):
        first = pl.multiple_of(((i_ref[0] - k) & 3) * rows, rows)
        gram_ref[pl.ds(first, rows), :] = g_ref[...].astype(f32)
    gram = gram_ref[...]
    s = gram_scale(gram)
    d01, g2 = two_steps(gram * (s * s))
    d2 = c2 * g2 + c3 * mm(g2, g2)
    rest = c1 * d01 + c1 * c1 * d2 + mm(d2, d01)
    y = y_ref[...]
    total = s * math.sqrt(max(KVB_ROWS, KV_RANK))
    out = (c1 * c1 * c1) * y.astype(f32) + mm(y, rest)
    o_ref[...] = (out * total).astype(bf16)


def finish_a_body(f_ref, g_ref, x_ref, o_ref, gram_ref, d01_ref, g2_ref):
    f = f_ref[0]
    gram = whole_gram(g_ref, gram_ref)
    s = gram_scale(gram)
    d01, g2 = two_steps(gram * (s * s))
    d01_ref[...] = d01
    g2_ref[...] = g2
    main = pl.ds(pl.multiple_of(f * MAIN, MAIN), MAIN)
    base = N_FSDP * MAIN + 8 * lax.shift_right_logical(f, 2)
    tail = pl.ds(pl.multiple_of(base, 8), 8)

    def rows(ref):
        return jnp.concatenate([ref[main, :], ref[tail, :]], axis=0)

    g2_rows = rows(g2_ref)
    d2 = c2 * g2_rows + c3 * mm(g2_rows, g2)
    rest = c1 * rows(d01_ref) + c1 * c1 * d2 + mm(d2, d01)
    x_rows = jnp.concatenate([x_ref[main, :].astype(f32), x_ref[pl.ds(pl.multiple_of(N_FSDP * MAIN + 16 * lax.shift_right_logical(f, 3), 16), 16), :].astype(f32)], axis=0)
    total = s * math.sqrt(max(KVA_ROWS, D))
    moved = mm(rest, x_ref[...])
    out = ((c1 * c1 * c1) * x_rows[:MAIN] + moved[:MAIN]) * total
    o_main = out.astype(bf16)
    q = f & 3
    h = f & 7
    x_tail = x_rows[MAIN : MAIN + 2]
    for j in range(1, 8):
        x_tail = jnp.where(h == j, x_rows[MAIN + 2 * j : MAIN + 2 * j + 2], x_tail)
    m_tail = moved[MAIN : MAIN + 2]
    for j in range(1, 4):
        m_tail = jnp.where(q == j, moved[MAIN + 2 * j : MAIN + 2 * j + 2], m_tail)
    o_tail = tail_tile(((c1 * c1 * c1) * x_tail + m_tail) * total).astype(bf16)
    for r in range(N_DP):
        o_ref[r, :, :CHUNK] = o_main
        o_ref[r, :, CHUNK:] = o_tail


def unpack_body(u_ref, o_ref):
    for d in range(N_DP):
        o_ref[:MAIN, d * CHUNK : (d + 1) * CHUNK] = u_ref[d, :, :CHUNK]
        tail = u_ref[d, :, CHUNK:].astype(f32)
        for k in range(GROUPS):
            piece = slice(d * CHUNK + 128 * k, d * CHUNK + 128 * k + 128)
            o_ref[MAIN:, piece] = tail[2 * k : 2 * k + 2].astype(bf16)


def exchange(x, axis):
    return lax.all_to_all(x, axis, split_axis=0, concat_axis=0, tiled=True)


def total_of(x):
    return jnp.sum(x.astype(f32), axis=0)


def shift(x, axis, n, k):
    return lax.ppermute(x, axis, [(i, (i + k) % n) for i in range(n)])


def others(x, axis, n):
    return [x] + [shift(x, axis, n, k) for k in range(1, n)]


def sum_over(x, axis, n):
    terms = [y.astype(f32) for y in others(x, axis, n)]
    while len(terms) > 1:
        half = len(terms) // 2
        terms = [terms[k] + terms[k + half] for k in range(half)]
    return terms[0].astype(bf16)


def local(kva_parts, kvb_parts, kva_moment, kvb_moment):
    y = lax.axis_index("y").astype(jnp.int32).reshape(1)
    c = lax.axis_index("c").astype(jnp.int32).reshape(1)
    f = lax.axis_index(FSDP).astype(jnp.int32).reshape(1)
    d = y * 2 + c
    rows_b = KV_RANK // N_DP

    half = shape((kvb_parts.shape[1] // 2, KV_RANK), bf16)
    packed, send_b = call(pack_body, (shape((N_DP, MAIN, WIDE), bf16), half), 1, 2)(
        c, kva_parts, kvb_parts
    )
    terms_a = exchange(packed, DP)
    grad_b = call(half_b_body, half, 1, 2)(c, kvb_parts, shift(send_b, "c", 2, 1))
    terms_a, grad_b = lax.optimization_barrier((terms_a, grad_b))
    grad_a, push_a = call(
        push_a_body,
        (shape((MAIN, WIDE), bf16), shape((N_FSDP, MAIN, WIDE), bf16)),
        1,
        2,
    )(d, terms_a, kva_moment)
    all_a = exchange(push_a, FSDP)

    grad_b = lax.all_gather(sum_over(grad_b, "y", 4), "c", tiled=True)
    moment_b, long_b, piece_b = call(
        moment_b_body,
        (
            shape(kvb_moment.shape, f32),
            shape(kvb_moment.shape, bf16),
            shape((rows_b, KV_RANK), bf16),
        ),
        1,
        2,
        [pltpu.VMEM((KV_RANK, KV_RANK), f32)],
    )(d, grad_b, kvb_moment)
    piece_b = sum_over(piece_b, "z", 8)
    piece_b = sum_over(piece_b, "x", 4)
    piece_b = lax.all_gather(piece_b, "c", tiled=True)
    pieces_b = others(piece_b, "y", 4)

    gram_a, short_a = call(
        gram_a_body,
        (shape((2, 64 * BLOCKS, 384), bf16), shape((KVA_ROWS, CHUNK), bf16)),
        0,
        1,
        [pltpu.VMEM((128 * BLOCKS, 128 * BLOCKS), f32)],
    )(all_a)
    gram_a = lax.all_gather(gram_a, "c")
    gram_a = lax.dynamic_index_in_dim(gram_a, lax.axis_index("c"), axis=1, keepdims=False)
    gram_a = sum_over(total_of(gram_a).astype(bf16), "y", 4)
    gram_a = lax.all_gather(gram_a, "c")

    grad_a = exchange(jnp.broadcast_to(grad_a[None], (N_DP,) + grad_a.shape), DP)
    moment_a = call(moment_a_body, shape(kva_moment.shape, f32), 0, 2)(grad_a, kva_moment)

    update_a = call(
        finish_a_body,
        shape((N_DP, MAIN, WIDE), bf16),
        1,
        2,
        [pltpu.VMEM((128 * BLOCKS, 128 * BLOCKS), f32)]
        + [pltpu.VMEM((KVA_ROWS, KVA_ROWS), f32)] * 2,
    )(f, gram_a, short_a)
    update_a = call(unpack_body, shape(kva_moment.shape, bf16))(exchange(update_a, DP))
    update_b = call(
        finish_b_body, shape(long_b.shape, bf16), 1, 5, [pltpu.VMEM((KV_RANK, KV_RANK), f32)]
    )(y, *pieces_b, long_b)
    return (moment_a, moment_b, update_a, update_b)


def solution(mesh):
    fine = Mesh(mesh.devices.reshape(4, 2, 4, 8), DP + FSDP)
    return jax.shard_map(
        local,
        mesh=fine,
        in_specs=(P(DP, FSDP, None), P(DP, FSDP, None), P(FSDP, None), P(FSDP, None)),
        out_specs=(P(FSDP, None), P(FSDP, None), P(FSDP, None), P(FSDP, None)),
        check_vma=False,
    )
```

```python
import functools
import math

import jax
import jax.numpy as jnp
from jax import lax
from jax.experimental import pallas as pl
from jax.experimental.pallas import tpu as pltpu
from jax.sharding import Mesh, PartitionSpec as P

D = 7168
KV_RANK = 512
KVA_ROWS = 576
KVB_ROWS = 16384
DP = ("y", "c")
FSDP = ("x", "z")
N_DP = 8
N_FSDP = 32
CHUNK = D // N_DP
GROUPS = CHUNK // 128
MAIN = 16
WIDE = CHUNK + 128
BLOCKS = 5

c1 = 3.4445
c2 = -4.775
c3 = 2.0315
decay_rate = 0.95
norm_epsilon = 1e-07
f32 = jnp.float32
bf16 = jnp.bfloat16
VMEM_LIMIT = 48 * 1024 * 1024


def call(body, out_shape, n_scalar=0, n_in=1, scratch=(), space=pltpu.VMEM):
    return pl.pallas_call(
        body,
        out_shape=out_shape,
        in_specs=[pl.BlockSpec(memory_space=pltpu.SMEM)] * n_scalar
        + [pl.BlockSpec(memory_space=space)] * n_in,
        out_specs=jax.tree.map(lambda _: pl.BlockSpec(memory_space=pltpu.VMEM), out_shape),
        scratch_shapes=list(scratch),
        compiler_params=pltpu.CompilerParams(vmem_limit_bytes=VMEM_LIMIT),
    )


def shape(dims, dtype):
    return jax.ShapeDtypeStruct(dims, dtype)


def tail_tile(rows):
    pieces = [rows[:, 128 * k : 128 * k + 128] for k in range(GROUPS)]
    return jnp.concatenate(pieces + [jnp.zeros((2, 128), f32)], axis=0)


def pack_body(c_ref, a_ref, b_ref, o_ref, send_ref, held_ref, sems):
    rows = send_ref.shape[0]
    other = pl.ds(pl.multiple_of((1 - c_ref[0]) * rows, rows), rows)
    copy_a = pltpu.make_async_copy(a_ref, held_ref, sems.at[0])
    copy_b = pltpu.make_async_copy(b_ref.at[0, other], send_ref, sems.at[1])
    copy_a.start()
    copy_b.start()
    copy_a.wait()
    for d in range(N_DP):
        lanes = slice(d * CHUNK, (d + 1) * CHUNK)
        o_ref[d, :, :CHUNK] = held_ref[0, :MAIN, lanes]
        o_ref[d, :, CHUNK:] = tail_tile(held_ref[0, MAIN:, lanes].astype(f32)).astype(bf16)
    copy_b.wait()


def push_a_body(d_ref, parts_ref, m_ref, g_ref, x_ref):
    start = pl.multiple_of(d_ref[0] * CHUNK, 128)
    grad = parts_ref[0].astype(f32)
    for r in range(1, N_DP):
        grad += parts_ref[r].astype(f32)
    g_ref[...] = grad.astype(bf16)
    m_main = m_ref[:MAIN, pl.ds(start, CHUNK)]
    m_tail = tail_tile(m_ref[MAIN:, pl.ds(start, CHUNK)])
    moment = decay_rate * jnp.concatenate([m_main, m_tail], axis=1) + grad
    push = (grad + decay_rate * moment).astype(bf16)
    for r in range(N_FSDP):
        x_ref[r] = push


def moment_a_body(g_ref, m_ref, o_ref):
    for d in range(N_DP):
        lanes = slice(d * CHUNK, (d + 1) * CHUNK)
        o_ref[:MAIN, lanes] = decay_rate * m_ref[:MAIN, lanes] + g_ref[d, :, :CHUNK].astype(f32)
        tail = g_ref[d, :, CHUNK:].astype(f32)
        for k in range(GROUPS):
            piece = slice(d * CHUNK + 128 * k, d * CHUNK + 128 * k + 128)
            o_ref[MAIN:, piece] = decay_rate * m_ref[MAIN:, piece] + tail[2 * k : 2 * k + 2]


def half_b_body(c_ref, b_ref, x_ref, o_ref):
    rows = o_ref.shape[0]
    half = b_ref[0, pl.ds(pl.multiple_of(c_ref[0] * rows, rows), rows)]
    o_ref[...] = (half.astype(f32) + x_ref[...].astype(f32)).astype(bf16)


def moment_b_body(d_ref, g_ref, m_ref, o_ref, y_ref, p_ref, scratch):
    grad = g_ref[...].astype(f32)
    moment = decay_rate * m_ref[...] + grad
    o_ref[...] = moment
    y = (grad + decay_rate * moment).astype(bf16)
    y_ref[...] = y
    scratch[...] = lax.dot_general(y, y, (((0,), (0,)), ((), ())), preferred_element_type=f32)
    rows = KV_RANK // N_DP
    p_ref[...] = scratch[pl.ds(pl.multiple_of(d_ref[0] * rows, rows), rows), :].astype(bf16)


def gram_a_body(x_ref, g_ref, full_ref, gram_ref):
    full_ref[: N_FSDP * MAIN] = x_ref[:, :, :CHUNK].reshape(N_FSDP * MAIN, CHUNK)
    tail = x_ref[:, :, CHUNK:].reshape(N_FSDP * MAIN, 128)
    rows = 2 * N_FSDP
    r = lax.broadcasted_iota(jnp.int32, (rows, N_FSDP * MAIN), 0)
    c = lax.broadcasted_iota(jnp.int32, (rows, N_FSDP * MAIN), 1)
    first = MAIN * lax.shift_right_logical(r, 1) + (r & 1)
    for k in range(GROUPS):
        pick = jnp.where(c == first + 2 * k, 1.0, 0.0).astype(bf16)
        full_ref[N_FSDP * MAIN :, 128 * k : 128 * k + 128] = jnp.dot(
            pick, tail, preferred_element_type=f32
        ).astype(bf16)
    x = full_ref[...]
    gram_ref[...] = jnp.zeros_like(gram_ref)
    gram_ref[:KVA_ROWS, :KVA_ROWS] = lax.dot_general(
        x, x, (((1,), (1,)), ((), ())), preferred_element_type=f32
    )
    for i in range(BLOCKS):
        for h in range(2):
            rows = slice(128 * i + 64 * h, 128 * i + 64 * h + 64)
            for j in range(3):
                k = (i + j) % BLOCKS
                g_ref[h, 64 * i : 64 * i + 64, 128 * j : 128 * j + 128] = gram_ref[
                    rows, 128 * k : 128 * k + 128
                ].astype(bf16)


def whole_gram(t_ref, gram_ref):
    for i in range(BLOCKS):
        for j in range(3):
            k = (i + j) % BLOCKS
            block = jnp.concatenate(
                [t_ref[h, 64 * i : 64 * i + 64, 128 * j : 128 * j + 128] for h in range(2)], axis=0
            ).astype(f32)
            gram_ref[128 * i : 128 * i + 128, 128 * k : 128 * k + 128] = block
            if j:
                gram_ref[128 * k : 128 * k + 128, 128 * i : 128 * i + 128] = block.T
    return gram_ref[:KVA_ROWS, :KVA_ROWS]


def mm(a, b):
    return jnp.dot(a.astype(bf16), b.astype(bf16), preferred_element_type=f32)


def gram_scale(gram):
    n = gram.shape[0]
    r = lax.broadcasted_iota(jnp.int32, (n, n), 0)
    c = lax.broadcasted_iota(jnp.int32, (n, n), 1)
    squares = jnp.sum(jnp.where(r == c, gram, 0.0))
    return 1.0 / (jnp.sqrt(squares) + norm_epsilon)


def two_steps(g0):
    d0 = c2 * g0 + c3 * mm(g0, g0)
    t0 = c1 * g0 + mm(d0, g0)
    g1 = c1 * t0 + mm(d0, t0)
    d1 = c2 * g1 + c3 * mm(g1, g1)
    d01 = c1 * (d0 + d1) + mm(d1, d0)
    t1 = c1 * g1 + mm(d1, g1)
    g2 = c1 * t1 + mm(d1, t1)
    return d01, g2


def finish_b_body(i_ref, g0_ref, g1_ref, g2_ref, g3_ref, y_ref, o_ref, gram_ref):
    rows = KV_RANK // 4
    for k, g_ref in enumerate((g0_ref, g1_ref, g2_ref, g3_ref)):
        first = pl.multiple_of(((i_ref[0] - k) & 3) * rows, rows)
        gram_ref[pl.ds(first, rows), :] = g_ref[...].astype(f32)
    gram = gram_ref[...]
    s = gram_scale(gram)
    d01, g2 = two_steps(gram * (s * s))
    d2 = c2 * g2 + c3 * mm(g2, g2)
    rest = c1 * d01 + c1 * c1 * d2 + mm(d2, d01)
    y = y_ref[...]
    total = s * math.sqrt(max(KVB_ROWS, KV_RANK))
    out = (c1 * c1 * c1) * y.astype(f32) + mm(y, rest)
    o_ref[...] = (out * total).astype(bf16)


def finish_a_body(f_ref, g_ref, x_ref, o_ref, gram_ref, d01_ref, g2_ref):
    f = f_ref[0]
    gram = whole_gram(g_ref, gram_ref)
    s = gram_scale(gram)
    d01, g2 = two_steps(gram * (s * s))
    d01_ref[...] = d01
    g2_ref[...] = g2
    main = pl.ds(pl.multiple_of(f * MAIN, MAIN), MAIN)
    base = N_FSDP * MAIN + 8 * lax.shift_right_logical(f, 2)
    tail = pl.ds(pl.multiple_of(base, 8), 8)

    def rows(ref):
        return jnp.concatenate([ref[main, :], ref[tail, :]], axis=0)

    g2_rows = rows(g2_ref)
    d2 = c2 * g2_rows + c3 * mm(g2_rows, g2)
    rest = c1 * rows(d01_ref) + c1 * c1 * d2 + mm(d2, d01)
    x_rows = jnp.concatenate([x_ref[main, :].astype(f32), x_ref[pl.ds(pl.multiple_of(N_FSDP * MAIN + 16 * lax.shift_right_logical(f, 3), 16), 16), :].astype(f32)], axis=0)
    total = s * math.sqrt(max(KVA_ROWS, D))
    moved = mm(rest, x_ref[...])
    out = ((c1 * c1 * c1) * x_rows[:MAIN] + moved[:MAIN]) * total
    o_main = out.astype(bf16)
    q = f & 3
    h = f & 7
    x_tail = x_rows[MAIN : MAIN + 2]
    for j in range(1, 8):
        x_tail = jnp.where(h == j, x_rows[MAIN + 2 * j : MAIN + 2 * j + 2], x_tail)
    m_tail = moved[MAIN : MAIN + 2]
    for j in range(1, 4):
        m_tail = jnp.where(q == j, moved[MAIN + 2 * j : MAIN + 2 * j + 2], m_tail)
    o_tail = tail_tile(((c1 * c1 * c1) * x_tail + m_tail) * total).astype(bf16)
    for r in range(N_DP):
        o_ref[r, :, :CHUNK] = o_main
        o_ref[r, :, CHUNK:] = o_tail


def unpack_body(u_ref, o_ref):
    for d in range(N_DP):
        o_ref[:MAIN, d * CHUNK : (d + 1) * CHUNK] = u_ref[d, :, :CHUNK]
        tail = u_ref[d, :, CHUNK:].astype(f32)
        for k in range(GROUPS):
            piece = slice(d * CHUNK + 128 * k, d * CHUNK + 128 * k + 128)
            o_ref[MAIN:, piece] = tail[2 * k : 2 * k + 2].astype(bf16)


def exchange(x, axis):
    return lax.all_to_all(x, axis, split_axis=0, concat_axis=0, tiled=True)


def total_of(x):
    return jnp.sum(x.astype(f32), axis=0)


def shift(x, axis, n, k):
    return lax.ppermute(x, axis, [(i, (i + k) % n) for i in range(n)])


def others(x, axis, n, step=1):
    return [x] + [shift(x, axis, n, k) for k in range(step, n, step)]


def sum_over(x, axis, n, step=1):
    terms = [y.astype(f32) for y in others(x, axis, n, step)]
    while len(terms) > 1:
        half = len(terms) // 2
        terms = [terms[k] + terms[k + half] for k in range(half)]
    return terms[0].astype(bf16)


def sum_pair(x, axis, n):
    other = lax.ppermute(x, axis, [(i, i ^ 1) for i in range(n)])
    return (x.astype(f32) + other.astype(f32)).astype(bf16)


def local(kva_parts, kvb_parts, kva_moment, kvb_moment):
    y = lax.axis_index("y").astype(jnp.int32).reshape(1)
    c = lax.axis_index("c").astype(jnp.int32).reshape(1)
    f = lax.axis_index(FSDP).astype(jnp.int32).reshape(1)
    d = y * 2 + c
    rows_b = KV_RANK // N_DP

    half = shape((kvb_parts.shape[1] // 2, KV_RANK), bf16)
    packed, send_b = call(
        pack_body,
        (shape((N_DP, MAIN, WIDE), bf16), half),
        1,
        2,
        [pltpu.VMEM(kva_parts.shape, bf16), pltpu.SemaphoreType.DMA((2,))],
        pl.ANY,
    )(c, kva_parts, kvb_parts)
    terms_a = exchange(packed, DP)
    grad_b = call(half_b_body, half, 1, 2)(c, kvb_parts, shift(send_b, "c", 2, 1))
    terms_a, grad_b = lax.optimization_barrier((terms_a, grad_b))
    grad_a, push_a = call(
        push_a_body,
        (shape((MAIN, WIDE), bf16), shape((N_FSDP, MAIN, WIDE), bf16)),
        1,
        2,
    )(d, terms_a, kva_moment)
    all_a = exchange(push_a, FSDP)

    grad_b = lax.all_gather(sum_over(grad_b, "y", 4), "c", tiled=True)
    moment_b, long_b, piece_b = call(
        moment_b_body,
        (
            shape(kvb_moment.shape, f32),
            shape(kvb_moment.shape, bf16),
            shape((rows_b, KV_RANK), bf16),
        ),
        1,
        2,
        [pltpu.VMEM((KV_RANK, KV_RANK), f32)],
    )(d, grad_b, kvb_moment)
    piece_b = sum_over(sum_pair(piece_b, "z", 8), "z", 8, 2)
    piece_b = sum_over(piece_b, "x", 4)
    piece_b, grad_a = lax.optimization_barrier((piece_b, grad_a))
    piece_b = lax.all_gather(piece_b, "c", tiled=True)

    gram_a, short_a = call(
        gram_a_body,
        (shape((2, 64 * BLOCKS, 384), bf16), shape((KVA_ROWS, CHUNK), bf16)),
        0,
        1,
        [pltpu.VMEM((128 * BLOCKS, 128 * BLOCKS), f32)],
    )(all_a)
    gram_a = lax.all_gather(gram_a, "c")
    gram_a = lax.dynamic_index_in_dim(gram_a, lax.axis_index("c"), axis=1, keepdims=False)
    gram_a = sum_over(total_of(gram_a).astype(bf16), "y", 4)
    gram_a = lax.all_gather(gram_a, "c")

    grad_a = exchange(jnp.broadcast_to(grad_a[None], (N_DP,) + grad_a.shape), DP)
    moment_a = call(moment_a_body, shape(kva_moment.shape, f32), 0, 2)(grad_a, kva_moment)

    pieces_b = others(piece_b, "y", 4)
    update_a = call(
        finish_a_body,
        shape((N_DP, MAIN, WIDE), bf16),
        1,
        2,
        [pltpu.VMEM((128 * BLOCKS, 128 * BLOCKS), f32)]
        + [pltpu.VMEM((KVA_ROWS, KVA_ROWS), f32)] * 2,
    )(f, gram_a, short_a)
    update_a, pieces_b = lax.optimization_barrier((update_a, pieces_b))
    update_a = call(unpack_body, shape(kva_moment.shape, bf16))(exchange(update_a, DP))
    update_b = call(
        finish_b_body, shape(long_b.shape, bf16), 1, 5, [pltpu.VMEM((KV_RANK, KV_RANK), f32)]
    )(y, *pieces_b, long_b)
    return (moment_a, moment_b, update_a, update_b)


def solution(mesh):
    fine = Mesh(mesh.devices.reshape(4, 2, 4, 8), DP + FSDP)
    return jax.shard_map(
        local,
        mesh=fine,
        in_specs=(P(DP, FSDP, None), P(DP, FSDP, None), P(FSDP, None), P(FSDP, None)),
        out_specs=(P(FSDP, None), P(FSDP, None), P(FSDP, None), P(FSDP, None)),
        check_vma=False,
    )
```

```python
import functools
import math

import jax
import jax.numpy as jnp
from jax import lax
from jax.experimental import pallas as pl
from jax.experimental.pallas import tpu as pltpu
from jax.sharding import Mesh, PartitionSpec as P

D = 7168
KV_RANK = 512
KVA_ROWS = 576
KVB_ROWS = 16384
DP = ("y", "c")
FSDP = ("x", "z")
N_DP = 8
N_FSDP = 32
CHUNK = D // N_DP
GROUPS = CHUNK // 128
MAIN = 16
WIDE = CHUNK + 128
BLOCKS = 5

c1 = 3.4445
c2 = -4.775
c3 = 2.0315
decay_rate = 0.95
norm_epsilon = 1e-07
f32 = jnp.float32
bf16 = jnp.bfloat16
VMEM_LIMIT = 48 * 1024 * 1024


def call(body, out_shape, n_scalar=0, n_in=1, scratch=(), space=pltpu.VMEM):
    return pl.pallas_call(
        body,
        out_shape=out_shape,
        in_specs=[pl.BlockSpec(memory_space=pltpu.SMEM)] * n_scalar
        + [pl.BlockSpec(memory_space=space)] * n_in,
        out_specs=jax.tree.map(lambda _: pl.BlockSpec(memory_space=pltpu.VMEM), out_shape),
        scratch_shapes=list(scratch),
        compiler_params=pltpu.CompilerParams(vmem_limit_bytes=VMEM_LIMIT),
    )


def shape(dims, dtype):
    return jax.ShapeDtypeStruct(dims, dtype)


def tail_tile(rows):
    pieces = [rows[:, 128 * k : 128 * k + 128] for k in range(GROUPS)]
    return jnp.concatenate(pieces + [jnp.zeros((2, 128), f32)], axis=0)


def pack_body(c_ref, a_ref, b_ref, o_ref, send_ref, held_ref, sems):
    rows = send_ref.shape[0]
    other = pl.ds(pl.multiple_of((1 - c_ref[0]) * rows, rows), rows)
    copy_a = pltpu.make_async_copy(a_ref, held_ref, sems.at[0])
    copy_b = pltpu.make_async_copy(b_ref.at[0, other], send_ref, sems.at[1])
    copy_a.start()
    copy_b.start()
    copy_a.wait()
    for d in range(N_DP):
        lanes = slice(d * CHUNK, (d + 1) * CHUNK)
        o_ref[d, :, :CHUNK] = held_ref[0, :MAIN, lanes]
        o_ref[d, :, CHUNK:] = tail_tile(held_ref[0, MAIN:, lanes].astype(f32)).astype(bf16)
    copy_b.wait()


def push_a_body(d_ref, parts_ref, m_ref, g_ref, x_ref):
    start = pl.multiple_of(d_ref[0] * CHUNK, 128)
    grad = parts_ref[0].astype(f32)
    for r in range(1, N_DP):
        grad += parts_ref[r].astype(f32)
    g_ref[...] = grad.astype(bf16)
    m_main = m_ref[:MAIN, pl.ds(start, CHUNK)]
    m_tail = tail_tile(m_ref[MAIN:, pl.ds(start, CHUNK)])
    moment = decay_rate * jnp.concatenate([m_main, m_tail], axis=1) + grad
    push = (grad + decay_rate * moment).astype(bf16)
    for r in range(N_FSDP):
        x_ref[r] = push


def moment_a_body(i_ref, g0_ref, g1_ref, g2_ref, g3_ref, m_ref, o_ref):
    for k, g_ref in enumerate((g0_ref, g1_ref, g2_ref, g3_ref)):
        for c in range(2):
            start = (((i_ref[0] - k) & 3) * 2 + c) * CHUNK
            lanes = pl.ds(pl.multiple_of(start, 128), CHUNK)
            main = g_ref[c, :, :CHUNK].astype(f32)
            o_ref[:MAIN, lanes] = decay_rate * m_ref[:MAIN, lanes] + main
            tail = g_ref[c, :, CHUNK:].astype(f32)
            for j in range(GROUPS):
                piece = pl.ds(pl.multiple_of(start + 128 * j, 128), 128)
                o_ref[MAIN:, piece] = decay_rate * m_ref[MAIN:, piece] + tail[2 * j : 2 * j + 2]


def half_b_body(c_ref, b_ref, x_ref, o_ref):
    rows = o_ref.shape[0]
    half = b_ref[0, pl.ds(pl.multiple_of(c_ref[0] * rows, rows), rows)]
    o_ref[...] = (half.astype(f32) + x_ref[...].astype(f32)).astype(bf16)


def moment_b_body(d_ref, g_ref, m_ref, o_ref, y_ref, p_ref, scratch):
    grad = g_ref[...].astype(f32)
    moment = decay_rate * m_ref[...] + grad
    o_ref[...] = moment
    y = (grad + decay_rate * moment).astype(bf16)
    y_ref[...] = y
    scratch[...] = lax.dot_general(y, y, (((0,), (0,)), ((), ())), preferred_element_type=f32)
    rows = KV_RANK // N_DP
    p_ref[...] = scratch[pl.ds(pl.multiple_of(d_ref[0] * rows, rows), rows), :].astype(bf16)


def gram_a_body(x_ref, g_ref, full_ref, gram_ref):
    full_ref[: N_FSDP * MAIN] = x_ref[:, :, :CHUNK].reshape(N_FSDP * MAIN, CHUNK)
    tail = x_ref[:, :, CHUNK:].reshape(N_FSDP * MAIN, 128)
    rows = 2 * N_FSDP
    r = lax.broadcasted_iota(jnp.int32, (rows, N_FSDP * MAIN), 0)
    c = lax.broadcasted_iota(jnp.int32, (rows, N_FSDP * MAIN), 1)
    first = MAIN * lax.shift_right_logical(r, 1) + (r & 1)
    for k in range(GROUPS):
        pick = jnp.where(c == first + 2 * k, 1.0, 0.0).astype(bf16)
        full_ref[N_FSDP * MAIN :, 128 * k : 128 * k + 128] = jnp.dot(
            pick, tail, preferred_element_type=f32
        ).astype(bf16)
    x = full_ref[...]
    gram_ref[...] = jnp.zeros_like(gram_ref)
    gram_ref[:KVA_ROWS, :KVA_ROWS] = lax.dot_general(
        x, x, (((1,), (1,)), ((), ())), preferred_element_type=f32
    )
    for i in range(BLOCKS):
        for h in range(2):
            rows = slice(128 * i + 64 * h, 128 * i + 64 * h + 64)
            for j in range(3):
                k = (i + j) % BLOCKS
                g_ref[h, 64 * i : 64 * i + 64, 128 * j : 128 * j + 128] = gram_ref[
                    rows, 128 * k : 128 * k + 128
                ].astype(bf16)


def whole_gram(t_ref, gram_ref):
    for i in range(BLOCKS):
        for j in range(3):
            k = (i + j) % BLOCKS
            block = jnp.concatenate(
                [t_ref[h, 64 * i : 64 * i + 64, 128 * j : 128 * j + 128] for h in range(2)], axis=0
            ).astype(f32)
            gram_ref[128 * i : 128 * i + 128, 128 * k : 128 * k + 128] = block
            if j:
                gram_ref[128 * k : 128 * k + 128, 128 * i : 128 * i + 128] = block.T
    return gram_ref[:KVA_ROWS, :KVA_ROWS]


def mm(a, b):
    return jnp.dot(a.astype(bf16), b.astype(bf16), preferred_element_type=f32)


def gram_scale(gram):
    n = gram.shape[0]
    r = lax.broadcasted_iota(jnp.int32, (n, n), 0)
    c = lax.broadcasted_iota(jnp.int32, (n, n), 1)
    squares = jnp.sum(jnp.where(r == c, gram, 0.0))
    return 1.0 / (jnp.sqrt(squares) + norm_epsilon)


def two_steps(g0):
    d0 = c2 * g0 + c3 * mm(g0, g0)
    t0 = c1 * g0 + mm(d0, g0)
    g1 = c1 * t0 + mm(d0, t0)
    d1 = c2 * g1 + c3 * mm(g1, g1)
    d01 = c1 * (d0 + d1) + mm(d1, d0)
    t1 = c1 * g1 + mm(d1, g1)
    g2 = c1 * t1 + mm(d1, t1)
    return d01, g2


def finish_b_body(i_ref, g0_ref, g1_ref, g2_ref, g3_ref, y_ref, o_ref, gram_ref):
    rows = KV_RANK // 4
    for k, g_ref in enumerate((g0_ref, g1_ref, g2_ref, g3_ref)):
        first = pl.multiple_of(((i_ref[0] - k) & 3) * rows, rows)
        gram_ref[pl.ds(first, rows), :] = g_ref[...].astype(f32)
    gram = gram_ref[...]
    s = gram_scale(gram)
    d01, g2 = two_steps(gram * (s * s))
    d2 = c2 * g2 + c3 * mm(g2, g2)
    rest = c1 * d01 + c1 * c1 * d2 + mm(d2, d01)
    y = y_ref[...]
    total = s * math.sqrt(max(KVB_ROWS, KV_RANK))
    out = (c1 * c1 * c1) * y.astype(f32) + mm(y, rest)
    o_ref[...] = (out * total).astype(bf16)


def finish_a_body(f_ref, g_ref, x_ref, o_ref, gram_ref, d01_ref, g2_ref):
    f = f_ref[0]
    gram = whole_gram(g_ref, gram_ref)
    s = gram_scale(gram)
    d01, g2 = two_steps(gram * (s * s))
    d01_ref[...] = d01
    g2_ref[...] = g2
    main = pl.ds(pl.multiple_of(f * MAIN, MAIN), MAIN)
    base = N_FSDP * MAIN + 8 * lax.shift_right_logical(f, 2)
    tail = pl.ds(pl.multiple_of(base, 8), 8)

    def rows(ref):
        return jnp.concatenate([ref[main, :], ref[tail, :]], axis=0)

    g2_rows = rows(g2_ref)
    d2 = c2 * g2_rows + c3 * mm(g2_rows, g2)
    rest = c1 * rows(d01_ref) + c1 * c1 * d2 + mm(d2, d01)
    x_rows = jnp.concatenate([x_ref[main, :].astype(f32), x_ref[pl.ds(pl.multiple_of(N_FSDP * MAIN + 16 * lax.shift_right_logical(f, 3), 16), 16), :].astype(f32)], axis=0)
    total = s * math.sqrt(max(KVA_ROWS, D))
    moved = mm(rest, x_ref[...])
    out = ((c1 * c1 * c1) * x_rows[:MAIN] + moved[:MAIN]) * total
    o_main = out.astype(bf16)
    q = f & 3
    h = f & 7
    x_tail = x_rows[MAIN : MAIN + 2]
    for j in range(1, 8):
        x_tail = jnp.where(h == j, x_rows[MAIN + 2 * j : MAIN + 2 * j + 2], x_tail)
    m_tail = moved[MAIN : MAIN + 2]
    for j in range(1, 4):
        m_tail = jnp.where(q == j, moved[MAIN + 2 * j : MAIN + 2 * j + 2], m_tail)
    o_tail = tail_tile(((c1 * c1 * c1) * x_tail + m_tail) * total).astype(bf16)
    for r in range(N_DP):
        o_ref[r, :, :CHUNK] = o_main
        o_ref[r, :, CHUNK:] = o_tail


def unpack_body(u_ref, o_ref):
    for d in range(N_DP):
        o_ref[:MAIN, d * CHUNK : (d + 1) * CHUNK] = u_ref[d, :, :CHUNK]
        tail = u_ref[d, :, CHUNK:].astype(f32)
        for k in range(GROUPS):
            piece = slice(d * CHUNK + 128 * k, d * CHUNK + 128 * k + 128)
            o_ref[MAIN:, piece] = tail[2 * k : 2 * k + 2].astype(bf16)


def exchange(x, axis):
    return lax.all_to_all(x, axis, split_axis=0, concat_axis=0, tiled=True)


def total_of(x):
    return jnp.sum(x.astype(f32), axis=0)


def shift(x, axis, n, k):
    return lax.ppermute(x, axis, [(i, (i + k) % n) for i in range(n)])


def others(x, axis, n, step=1):
    return [x] + [shift(x, axis, n, k) for k in range(step, n, step)]


def sum_over(x, axis, n, step=1):
    return pair_sums(others(x, axis, n, step))


def pair_sums(terms):
    terms = [y.astype(f32) for y in terms]
    while len(terms) > 1:
        half = len(terms) // 2
        terms = [terms[k] + terms[k + half] for k in range(half)]
    return terms[0].astype(bf16)


def sum_pair(x, axis, n):
    other = lax.ppermute(x, axis, [(i, i ^ 1) for i in range(n)])
    return (x.astype(f32) + other.astype(f32)).astype(bf16)


def local(kva_parts, kvb_parts, kva_moment, kvb_moment):
    y = lax.axis_index("y").astype(jnp.int32).reshape(1)
    c = lax.axis_index("c").astype(jnp.int32).reshape(1)
    f = lax.axis_index(FSDP).astype(jnp.int32).reshape(1)
    d = y * 2 + c
    rows_b = KV_RANK // N_DP

    half = shape((kvb_parts.shape[1] // 2, KV_RANK), bf16)
    packed, send_b = call(
        pack_body,
        (shape((N_DP, MAIN, WIDE), bf16), half),
        1,
        2,
        [pltpu.VMEM(kva_parts.shape, bf16), pltpu.SemaphoreType.DMA((2,))],
        pl.ANY,
    )(c, kva_parts, kvb_parts)
    terms_a = exchange(packed, DP)
    grad_b = call(half_b_body, half, 1, 2)(c, kvb_parts, shift(send_b, "c", 2, 1))
    grads_b = others(grad_b, "y", 4)
    terms_a, grads_b[1] = lax.optimization_barrier((terms_a, grads_b[1]))
    grad_a, push_a = call(
        push_a_body,
        (shape((MAIN, WIDE), bf16), shape((N_FSDP, MAIN, WIDE), bf16)),
        1,
        2,
    )(d, terms_a, kva_moment)
    all_a = exchange(push_a, FSDP)

    grad_b = lax.all_gather(pair_sums(grads_b), "c", tiled=True)
    moment_b, long_b, piece_b = call(
        moment_b_body,
        (
            shape(kvb_moment.shape, f32),
            shape(kvb_moment.shape, bf16),
            shape((rows_b, KV_RANK), bf16),
        ),
        1,
        2,
        [pltpu.VMEM((KV_RANK, KV_RANK), f32)],
    )(d, grad_b, kvb_moment)
    piece_b = sum_over(piece_b, "z", 8, 2)

    grads_a = others(lax.all_gather(grad_a, "c"), "y", 4)
    moment_a = call(moment_a_body, shape(kva_moment.shape, f32), 1, 5)(y, *grads_a, kva_moment)
    all_a, moment_a = lax.optimization_barrier((all_a, moment_a))

    gram_a, short_a = call(
        gram_a_body,
        (shape((2, 64 * BLOCKS, 384), bf16), shape((KVA_ROWS, CHUNK), bf16)),
        0,
        1,
        [pltpu.VMEM((128 * BLOCKS, 128 * BLOCKS), f32)],
    )(all_a)
    gram_a = lax.all_gather(gram_a, "c")
    gram_a = lax.dynamic_index_in_dim(gram_a, lax.axis_index("c"), axis=1, keepdims=False)
    gram_a = total_of(gram_a).astype(bf16)
    gram_a, piece_b = lax.optimization_barrier((gram_a, piece_b))
    grams_a = others(gram_a, "y", 4)
    piece_b = sum_pair(piece_b, "z", 8)
    piece_b, grams_a[1], grams_a[3] = lax.optimization_barrier((piece_b, grams_a[1], grams_a[3]))
    gram_a = lax.all_gather(pair_sums(grams_a), "c")

    piece_b = sum_over(piece_b, "x", 4)
    piece_b = lax.all_gather(piece_b, "c", tiled=True)

    pieces_b = others(piece_b, "y", 4)
    update_a = call(
        finish_a_body,
        shape((N_DP, MAIN, WIDE), bf16),
        1,
        2,
        [pltpu.VMEM((128 * BLOCKS, 128 * BLOCKS), f32)]
        + [pltpu.VMEM((KVA_ROWS, KVA_ROWS), f32)] * 2,
    )(f, gram_a, short_a)
    update_a, pieces_b = lax.optimization_barrier((update_a, pieces_b))
    update_a = call(unpack_body, shape(kva_moment.shape, bf16))(exchange(update_a, DP))
    update_b = call(
        finish_b_body, shape(long_b.shape, bf16), 1, 5, [pltpu.VMEM((KV_RANK, KV_RANK), f32)]
    )(y, *pieces_b, long_b)
    return (moment_a, moment_b, update_a, update_b)


def solution(mesh):
    fine = Mesh(mesh.devices.reshape(4, 2, 4, 8), DP + FSDP)
    return jax.shard_map(
        local,
        mesh=fine,
        in_specs=(P(DP, FSDP, None), P(DP, FSDP, None), P(FSDP, None), P(FSDP, None)),
        out_specs=(P(FSDP, None), P(FSDP, None), P(FSDP, None), P(FSDP, None)),
        check_vma=False,
    )
```

```python
import functools
import math

import jax
import jax.numpy as jnp
from jax import lax
from jax.experimental import pallas as pl
from jax.experimental.pallas import tpu as pltpu
from jax.sharding import Mesh, PartitionSpec as P

D = 7168
KV_RANK = 512
KVA_ROWS = 576
KVB_ROWS = 16384
DP = ("y", "c")
FSDP = ("x", "z")
N_DP = 8
N_FSDP = 32
CHUNK = D // N_DP
GROUPS = CHUNK // 128
MAIN = 16
WIDE = CHUNK + 128
BLOCKS = 5

c1 = 3.4445
c2 = -4.775
c3 = 2.0315
decay_rate = 0.95
norm_epsilon = 1e-07
f32 = jnp.float32
bf16 = jnp.bfloat16
VMEM_LIMIT = 48 * 1024 * 1024


def call(body, out_shape, n_scalar=0, n_in=1, scratch=(), space=pltpu.VMEM, limit=VMEM_LIMIT):
    return pl.pallas_call(
        body,
        out_shape=out_shape,
        in_specs=[pl.BlockSpec(memory_space=pltpu.SMEM)] * n_scalar
        + [pl.BlockSpec(memory_space=space)] * n_in,
        out_specs=jax.tree.map(lambda _: pl.BlockSpec(memory_space=pltpu.VMEM), out_shape),
        scratch_shapes=list(scratch),
        compiler_params=pltpu.CompilerParams(vmem_limit_bytes=limit),
    )


def shape(dims, dtype):
    return jax.ShapeDtypeStruct(dims, dtype)


def tail_tile(rows):
    pieces = [rows[:, 128 * k : 128 * k + 128] for k in range(GROUPS)]
    return jnp.concatenate(pieces + [jnp.zeros((2, 128), f32)], axis=0)


def pack_body(c_ref, a_ref, b_ref, o_ref, send_ref, held_ref, sems):
    rows = send_ref.shape[0]
    other = pl.ds(pl.multiple_of((1 - c_ref[0]) * rows, rows), rows)
    copy_a = pltpu.make_async_copy(a_ref, held_ref, sems.at[0])
    copy_b = pltpu.make_async_copy(b_ref.at[0, other], send_ref, sems.at[1])
    copy_a.start()
    copy_b.start()
    copy_a.wait()
    for d in range(N_DP):
        lanes = slice(d * CHUNK, (d + 1) * CHUNK)
        o_ref[d, :, :CHUNK] = held_ref[0, :MAIN, lanes]
        o_ref[d, :, CHUNK:] = tail_tile(held_ref[0, MAIN:, lanes].astype(f32)).astype(bf16)
    copy_b.wait()


def push_a_body(d_ref, parts_ref, m_ref, g_ref, x_ref):
    start = pl.multiple_of(d_ref[0] * CHUNK, 128)
    grad = parts_ref[0].astype(f32)
    for r in range(1, N_DP):
        grad += parts_ref[r].astype(f32)
    g_ref[...] = grad.astype(bf16)
    m_main = m_ref[:MAIN, pl.ds(start, CHUNK)]
    m_tail = tail_tile(m_ref[MAIN:, pl.ds(start, CHUNK)])
    moment = decay_rate * jnp.concatenate([m_main, m_tail], axis=1) + grad
    push = (grad + decay_rate * moment).astype(bf16)
    for r in range(N_FSDP):
        x_ref[r] = push


def moment_a_body(i_ref, g0_ref, g1_ref, g2_ref, g3_ref, m_ref, o_ref):
    for k, g_ref in enumerate((g0_ref, g1_ref, g2_ref, g3_ref)):
        for c in range(2):
            start = (((i_ref[0] - k) & 3) * 2 + c) * CHUNK
            lanes = pl.ds(pl.multiple_of(start, 128), CHUNK)
            main = g_ref[c, :, :CHUNK].astype(f32)
            o_ref[:MAIN, lanes] = decay_rate * m_ref[:MAIN, lanes] + main
            tail = g_ref[c, :, CHUNK:].astype(f32)
            for j in range(GROUPS):
                piece = pl.ds(pl.multiple_of(start + 128 * j, 128), 128)
                o_ref[MAIN:, piece] = decay_rate * m_ref[MAIN:, piece] + tail[2 * j : 2 * j + 2]


def half_b_body(c_ref, b_ref, x_ref, o_ref):
    rows = o_ref.shape[0]
    half = b_ref[0, pl.ds(pl.multiple_of(c_ref[0] * rows, rows), rows)]
    o_ref[...] = (half.astype(f32) + x_ref[...].astype(f32)).astype(bf16)


def moment_b_body(d_ref, g_ref, m_ref, o_ref, y_ref, p_ref, scratch):
    grad = g_ref[...].astype(f32)
    moment = decay_rate * m_ref[...] + grad
    o_ref[...] = moment
    y = (grad + decay_rate * moment).astype(bf16)
    y_ref[...] = y
    scratch[...] = lax.dot_general(y, y, (((0,), (0,)), ((), ())), preferred_element_type=f32)
    rows = KV_RANK // N_DP
    p_ref[...] = scratch[pl.ds(pl.multiple_of(d_ref[0] * rows, rows), rows), :].astype(bf16)


def gram_a_body(x_ref, g_ref, full_ref, gram_ref):
    full_ref[: N_FSDP * MAIN] = x_ref[:, :, :CHUNK].reshape(N_FSDP * MAIN, CHUNK)
    tail = x_ref[:, :, CHUNK:].reshape(N_FSDP * MAIN, 128)
    rows = 2 * N_FSDP
    r = lax.broadcasted_iota(jnp.int32, (rows, N_FSDP * MAIN), 0)
    c = lax.broadcasted_iota(jnp.int32, (rows, N_FSDP * MAIN), 1)
    first = MAIN * lax.shift_right_logical(r, 1) + (r & 1)
    for k in range(GROUPS):
        pick = jnp.where(c == first + 2 * k, 1.0, 0.0).astype(bf16)
        full_ref[N_FSDP * MAIN :, 128 * k : 128 * k + 128] = jnp.dot(
            pick, tail, preferred_element_type=f32
        ).astype(bf16)
    x = full_ref[...]
    gram_ref[...] = jnp.zeros_like(gram_ref)
    gram_ref[:KVA_ROWS, :KVA_ROWS] = lax.dot_general(
        x, x, (((1,), (1,)), ((), ())), preferred_element_type=f32
    )
    for i in range(BLOCKS):
        for h in range(2):
            rows = slice(128 * i + 64 * h, 128 * i + 64 * h + 64)
            for j in range(3):
                k = (i + j) % BLOCKS
                g_ref[h, 64 * i : 64 * i + 64, 128 * j : 128 * j + 128] = gram_ref[
                    rows, 128 * k : 128 * k + 128
                ].astype(bf16)


def whole_gram(t_ref, gram_ref):
    for i in range(BLOCKS):
        for j in range(3):
            k = (i + j) % BLOCKS
            block = jnp.concatenate(
                [t_ref[h, 64 * i : 64 * i + 64, 128 * j : 128 * j + 128] for h in range(2)], axis=0
            ).astype(f32)
            gram_ref[128 * i : 128 * i + 128, 128 * k : 128 * k + 128] = block
            if j:
                gram_ref[128 * k : 128 * k + 128, 128 * i : 128 * i + 128] = block.T
    return gram_ref[:KVA_ROWS, :KVA_ROWS]


def mm(a, b):
    return jnp.dot(a.astype(bf16), b.astype(bf16), preferred_element_type=f32)


def gram_scale(gram):
    n = gram.shape[0]
    r = lax.broadcasted_iota(jnp.int32, (n, n), 0)
    c = lax.broadcasted_iota(jnp.int32, (n, n), 1)
    squares = jnp.sum(jnp.where(r == c, gram, 0.0))
    return 1.0 / (jnp.sqrt(squares) + norm_epsilon)


def two_steps(g0):
    d0 = c2 * g0 + c3 * mm(g0, g0)
    t0 = c1 * g0 + mm(d0, g0)
    g1 = c1 * t0 + mm(d0, t0)
    d1 = c2 * g1 + c3 * mm(g1, g1)
    d01 = c1 * (d0 + d1) + mm(d1, d0)
    t1 = c1 * g1 + mm(d1, g1)
    g2 = c1 * t1 + mm(d1, t1)
    return d01, g2


def finish_b_body(i_ref, g0_ref, g1_ref, g2_ref, g3_ref, y_ref, o_ref, gram_ref):
    rows = KV_RANK // 4
    for k, g_ref in enumerate((g0_ref, g1_ref, g2_ref, g3_ref)):
        first = pl.multiple_of(((i_ref[0] - k) & 3) * rows, rows)
        gram_ref[pl.ds(first, rows), :] = g_ref[...].astype(f32)
    gram = gram_ref[...]
    s = gram_scale(gram)
    d01, g2 = two_steps(gram * (s * s))
    d2 = c2 * g2 + c3 * mm(g2, g2)
    rest = c1 * d01 + c1 * c1 * d2 + mm(d2, d01)
    y = y_ref[...]
    total = s * math.sqrt(max(KVB_ROWS, KV_RANK))
    out = (c1 * c1 * c1) * y.astype(f32) + mm(y, rest)
    o_ref[...] = (out * total).astype(bf16)


def finish_a_body(f_ref, g_ref, x_ref, o_ref, gram_ref, d01_ref, g2_ref):
    f = f_ref[0]
    gram = whole_gram(g_ref, gram_ref)
    s = gram_scale(gram)
    d01, g2 = two_steps(gram * (s * s))
    d01_ref[...] = d01
    g2_ref[...] = g2
    main = pl.ds(pl.multiple_of(f * MAIN, MAIN), MAIN)
    base = N_FSDP * MAIN + 8 * lax.shift_right_logical(f, 2)
    tail = pl.ds(pl.multiple_of(base, 8), 8)

    def rows(ref):
        return jnp.concatenate([ref[main, :], ref[tail, :]], axis=0)

    g2_rows = rows(g2_ref)
    d2 = c2 * g2_rows + c3 * mm(g2_rows, g2)
    rest = c1 * rows(d01_ref) + c1 * c1 * d2 + mm(d2, d01)
    x_rows = jnp.concatenate([x_ref[main, :].astype(f32), x_ref[pl.ds(pl.multiple_of(N_FSDP * MAIN + 16 * lax.shift_right_logical(f, 3), 16), 16), :].astype(f32)], axis=0)
    total = s * math.sqrt(max(KVA_ROWS, D))
    moved = mm(rest, x_ref[...])
    out = ((c1 * c1 * c1) * x_rows[:MAIN] + moved[:MAIN]) * total
    o_main = out.astype(bf16)
    q = f & 3
    h = f & 7
    x_tail = x_rows[MAIN : MAIN + 2]
    for j in range(1, 8):
        x_tail = jnp.where(h == j, x_rows[MAIN + 2 * j : MAIN + 2 * j + 2], x_tail)
    m_tail = moved[MAIN : MAIN + 2]
    for j in range(1, 4):
        m_tail = jnp.where(q == j, moved[MAIN + 2 * j : MAIN + 2 * j + 2], m_tail)
    o_tail = tail_tile(((c1 * c1 * c1) * x_tail + m_tail) * total).astype(bf16)
    for r in range(N_DP):
        o_ref[r, :, :CHUNK] = o_main
        o_ref[r, :, CHUNK:] = o_tail


def unpack_body(u_ref, o_ref):
    for d in range(N_DP):
        o_ref[:MAIN, d * CHUNK : (d + 1) * CHUNK] = u_ref[d, :, :CHUNK]
        tail = u_ref[d, :, CHUNK:].astype(f32)
        for k in range(GROUPS):
            piece = slice(d * CHUNK + 128 * k, d * CHUNK + 128 * k + 128)
            o_ref[MAIN:, piece] = tail[2 * k : 2 * k + 2].astype(bf16)


def exchange(x, axis):
    return lax.all_to_all(x, axis, split_axis=0, concat_axis=0, tiled=True)


def total_of(x):
    return jnp.sum(x.astype(f32), axis=0)


def shift(x, axis, n, k):
    return lax.ppermute(x, axis, [(i, (i + k) % n) for i in range(n)])


def others(x, axis, n, step=1):
    return [x] + [shift(x, axis, n, k) for k in range(step, n, step)]


def sum_over(x, axis, n, step=1):
    return pair_sums(others(x, axis, n, step))


def pair_sums(terms):
    terms = [y.astype(f32) for y in terms]
    while len(terms) > 1:
        half = len(terms) // 2
        terms = [terms[k] + terms[k + half] for k in range(half)]
    return terms[0].astype(bf16)


def sum_pair(x, axis, n):
    other = lax.ppermute(x, axis, [(i, i ^ 1) for i in range(n)])
    return (x.astype(f32) + other.astype(f32)).astype(bf16)


def local(kva_parts, kvb_parts, kva_moment, kvb_moment):
    y = lax.axis_index("y").astype(jnp.int32).reshape(1)
    c = lax.axis_index("c").astype(jnp.int32).reshape(1)
    f = lax.axis_index(FSDP).astype(jnp.int32).reshape(1)
    d = y * 2 + c
    rows_b = KV_RANK // N_DP

    half = shape((kvb_parts.shape[1] // 2, KV_RANK), bf16)
    packed, send_b = call(
        pack_body,
        (shape((N_DP, MAIN, WIDE), bf16), half),
        1,
        2,
        [pltpu.VMEM(kva_parts.shape, bf16), pltpu.SemaphoreType.DMA((2,))],
        pl.ANY,
        67_000_000,
    )(c, kva_parts, kvb_parts)
    terms_a = exchange(packed, DP)
    grad_b = call(half_b_body, half, 1, 2)(c, kvb_parts, shift(send_b, "c", 2, 1))
    grads_b = others(grad_b, "y", 4)
    terms_a, grads_b = lax.optimization_barrier((terms_a, grads_b))
    grad_a, push_a = call(
        push_a_body,
        (shape((MAIN, WIDE), bf16), shape((N_FSDP, MAIN, WIDE), bf16)),
        1,
        2,
    )(d, terms_a, kva_moment)
    all_a = exchange(push_a, FSDP)

    grad_b = lax.all_gather(pair_sums(grads_b), "c", tiled=True)
    moment_b, long_b, piece_b = call(
        moment_b_body,
        (
            shape(kvb_moment.shape, f32),
            shape(kvb_moment.shape, bf16),
            shape((rows_b, KV_RANK), bf16),
        ),
        1,
        2,
        [pltpu.VMEM((KV_RANK, KV_RANK), f32)],
    )(d, grad_b, kvb_moment)
    piece_b, grad_a = lax.optimization_barrier((piece_b, grad_a))
    piece_b = sum_pair(sum_over(piece_b, "x", 4), "z", 8)

    grads_a = others(lax.all_gather(grad_a, "c"), "y", 4)
    moment_a = call(moment_a_body, shape(kva_moment.shape, f32), 1, 5)(y, *grads_a, kva_moment)
    all_a, moment_a = lax.optimization_barrier((all_a, moment_a))

    gram_a, short_a = call(
        gram_a_body,
        (shape((2, 64 * BLOCKS, 384), bf16), shape((KVA_ROWS, CHUNK), bf16)),
        0,
        1,
        [pltpu.VMEM((128 * BLOCKS, 128 * BLOCKS), f32)],
    )(all_a)
    gram_a = lax.all_gather(gram_a, "c")
    gram_a = lax.dynamic_index_in_dim(gram_a, lax.axis_index("c"), axis=1, keepdims=False)
    gram_a = total_of(gram_a).astype(bf16)
    gram_a, piece_b = lax.optimization_barrier((gram_a, piece_b))
    gram_a = sum_over(gram_a, "y", 4)
    piece_b = sum_over(piece_b, "z", 8, 2)
    gram_a, piece_b = lax.optimization_barrier((gram_a, piece_b))
    gram_a = lax.all_gather(gram_a, "c")
    piece_b = lax.all_gather(piece_b, "c", tiled=True)

    pieces_b = others(piece_b, "y", 4)
    update_a = call(
        finish_a_body,
        shape((N_DP, MAIN, WIDE), bf16),
        1,
        2,
        [pltpu.VMEM((128 * BLOCKS, 128 * BLOCKS), f32)]
        + [pltpu.VMEM((KVA_ROWS, KVA_ROWS), f32)] * 2,
    )(f, gram_a, short_a)
    update_a, pieces_b = lax.optimization_barrier((update_a, pieces_b))
    update_a = call(unpack_body, shape(kva_moment.shape, bf16))(exchange(update_a, DP))
    update_b = call(
        finish_b_body, shape(long_b.shape, bf16), 1, 5, [pltpu.VMEM((KV_RANK, KV_RANK), f32)]
    )(y, *pieces_b, long_b)
    return (moment_a, moment_b, update_a, update_b)


def solution(mesh):
    fine = Mesh(mesh.devices.reshape(4, 2, 4, 8), DP + FSDP)
    return jax.shard_map(
        local,
        mesh=fine,
        in_specs=(P(DP, FSDP, None), P(DP, FSDP, None), P(FSDP, None), P(FSDP, None)),
        out_specs=(P(FSDP, None), P(FSDP, None), P(FSDP, None), P(FSDP, None)),
        check_vma=False,
    )
```

```python
import functools
import math

import jax
import jax.numpy as jnp
from jax import lax
from jax.experimental import pallas as pl
from jax.experimental.pallas import tpu as pltpu
from jax.sharding import Mesh, PartitionSpec as P

D = 7168
KV_RANK = 512
KVA_ROWS = 576
KVB_ROWS = 16384
DP = ("y", "c")
FSDP = ("x", "z")
N_DP = 8
N_FSDP = 32
CHUNK = D // N_DP
GROUPS = CHUNK // 128
MAIN = 16
WIDE = CHUNK + 128
BLOCKS = 5

c1 = 3.4445
c2 = -4.775
c3 = 2.0315
decay_rate = 0.95
norm_epsilon = 1e-07
f32 = jnp.float32
bf16 = jnp.bfloat16
VMEM_LIMIT = 48 * 1024 * 1024
HINT = 40_000_000_000


def call(body, out_shape, n_scalar=0, n_in=1, scratch=(), space=pltpu.VMEM, limit=VMEM_LIMIT, flops=0):
    return pl.pallas_call(
        body,
        out_shape=out_shape,
        in_specs=[pl.BlockSpec(memory_space=pltpu.SMEM)] * n_scalar
        + [pl.BlockSpec(memory_space=space)] * n_in,
        out_specs=jax.tree.map(lambda _: pl.BlockSpec(memory_space=pltpu.VMEM), out_shape),
        scratch_shapes=list(scratch),
        compiler_params=pltpu.CompilerParams(vmem_limit_bytes=limit),
        cost_estimate=pl.CostEstimate(flops=flops, bytes_accessed=0, transcendentals=0)
        if flops
        else None,
    )


def shape(dims, dtype):
    return jax.ShapeDtypeStruct(dims, dtype)


def tail_tile(rows):
    pieces = [rows[:, 128 * k : 128 * k + 128] for k in range(GROUPS)]
    return jnp.concatenate(pieces + [jnp.zeros((2, 128), f32)], axis=0)


def pack_body(c_ref, a_ref, b_ref, o_ref, send_ref, held_ref, sems):
    rows = send_ref.shape[0]
    other = pl.ds(pl.multiple_of((1 - c_ref[0]) * rows, rows), rows)
    copy_a = pltpu.make_async_copy(a_ref, held_ref, sems.at[0])
    copy_b = pltpu.make_async_copy(b_ref.at[0, other], send_ref, sems.at[1])
    copy_a.start()
    copy_b.start()
    copy_a.wait()
    for d in range(N_DP):
        lanes = slice(d * CHUNK, (d + 1) * CHUNK)
        o_ref[d, :, :CHUNK] = held_ref[0, :MAIN, lanes]
        o_ref[d, :, CHUNK:] = tail_tile(held_ref[0, MAIN:, lanes].astype(f32)).astype(bf16)
    copy_b.wait()


def push_a_body(d_ref, parts_ref, m_ref, g_ref, x_ref):
    start = pl.multiple_of(d_ref[0] * CHUNK, 128)
    grad = parts_ref[0].astype(f32)
    for r in range(1, N_DP):
        grad += parts_ref[r].astype(f32)
    g_ref[...] = grad.astype(bf16)
    m_main = m_ref[:MAIN, pl.ds(start, CHUNK)]
    m_tail = tail_tile(m_ref[MAIN:, pl.ds(start, CHUNK)])
    moment = decay_rate * jnp.concatenate([m_main, m_tail], axis=1) + grad
    push = (grad + decay_rate * moment).astype(bf16)
    for r in range(N_FSDP):
        x_ref[r] = push


def moment_a_body(i_ref, g0_ref, g1_ref, g2_ref, g3_ref, m_ref, o_ref):
    for k, g_ref in enumerate((g0_ref, g1_ref, g2_ref, g3_ref)):
        for c in range(2):
            start = (((i_ref[0] - k) & 3) * 2 + c) * CHUNK
            lanes = pl.ds(pl.multiple_of(start, 128), CHUNK)
            main = g_ref[c, :, :CHUNK].astype(f32)
            o_ref[:MAIN, lanes] = decay_rate * m_ref[:MAIN, lanes] + main
            tail = g_ref[c, :, CHUNK:].astype(f32)
            for j in range(GROUPS):
                piece = pl.ds(pl.multiple_of(start + 128 * j, 128), 128)
                o_ref[MAIN:, piece] = decay_rate * m_ref[MAIN:, piece] + tail[2 * j : 2 * j + 2]


def half_b_body(c_ref, b_ref, x_ref, o_ref):
    rows = o_ref.shape[0]
    half = b_ref[0, pl.ds(pl.multiple_of(c_ref[0] * rows, rows), rows)]
    o_ref[...] = (half.astype(f32) + x_ref[...].astype(f32)).astype(bf16)


def moment_b_body(d_ref, g_ref, m_ref, o_ref, y_ref, p_ref, scratch):
    grad = g_ref[...].astype(f32)
    moment = decay_rate * m_ref[...] + grad
    o_ref[...] = moment
    y = (grad + decay_rate * moment).astype(bf16)
    y_ref[...] = y
    scratch[...] = lax.dot_general(y, y, (((0,), (0,)), ((), ())), preferred_element_type=f32)
    rows = KV_RANK // N_DP
    p_ref[...] = scratch[pl.ds(pl.multiple_of(d_ref[0] * rows, rows), rows), :].astype(bf16)


def gram_a_body(x_ref, g_ref, full_ref, gram_ref):
    full_ref[: N_FSDP * MAIN] = x_ref[:, :, :CHUNK].reshape(N_FSDP * MAIN, CHUNK)
    tail = x_ref[:, :, CHUNK:].reshape(N_FSDP * MAIN, 128)
    rows = 2 * N_FSDP
    r = lax.broadcasted_iota(jnp.int32, (rows, N_FSDP * MAIN), 0)
    c = lax.broadcasted_iota(jnp.int32, (rows, N_FSDP * MAIN), 1)
    first = MAIN * lax.shift_right_logical(r, 1) + (r & 1)
    for k in range(GROUPS):
        pick = jnp.where(c == first + 2 * k, 1.0, 0.0).astype(bf16)
        full_ref[N_FSDP * MAIN :, 128 * k : 128 * k + 128] = jnp.dot(
            pick, tail, preferred_element_type=f32
        ).astype(bf16)
    x = full_ref[...]
    gram_ref[...] = jnp.zeros_like(gram_ref)
    gram_ref[:KVA_ROWS, :KVA_ROWS] = lax.dot_general(
        x, x, (((1,), (1,)), ((), ())), preferred_element_type=f32
    )
    for i in range(BLOCKS):
        for h in range(2):
            rows = slice(128 * i + 64 * h, 128 * i + 64 * h + 64)
            for j in range(3):
                k = (i + j) % BLOCKS
                g_ref[h, 64 * i : 64 * i + 64, 128 * j : 128 * j + 128] = gram_ref[
                    rows, 128 * k : 128 * k + 128
                ].astype(bf16)


def whole_gram(t_ref, gram_ref):
    for i in range(BLOCKS):
        for j in range(3):
            k = (i + j) % BLOCKS
            block = jnp.concatenate(
                [t_ref[h, 64 * i : 64 * i + 64, 128 * j : 128 * j + 128] for h in range(2)], axis=0
            ).astype(f32)
            gram_ref[128 * i : 128 * i + 128, 128 * k : 128 * k + 128] = block
            if j:
                gram_ref[128 * k : 128 * k + 128, 128 * i : 128 * i + 128] = block.T
    return gram_ref[:KVA_ROWS, :KVA_ROWS]


def mm(a, b):
    return jnp.dot(a.astype(bf16), b.astype(bf16), preferred_element_type=f32)


def gram_scale(gram):
    n = gram.shape[0]
    r = lax.broadcasted_iota(jnp.int32, (n, n), 0)
    c = lax.broadcasted_iota(jnp.int32, (n, n), 1)
    squares = jnp.sum(jnp.where(r == c, gram, 0.0))
    return 1.0 / (jnp.sqrt(squares) + norm_epsilon)


def two_steps(g0):
    d0 = c2 * g0 + c3 * mm(g0, g0)
    t0 = c1 * g0 + mm(d0, g0)
    g1 = c1 * t0 + mm(d0, t0)
    d1 = c2 * g1 + c3 * mm(g1, g1)
    d01 = c1 * (d0 + d1) + mm(d1, d0)
    t1 = c1 * g1 + mm(d1, g1)
    g2 = c1 * t1 + mm(d1, t1)
    return d01, g2


def finish_b_body(i_ref, g0_ref, g1_ref, g2_ref, g3_ref, y_ref, o_ref, gram_ref):
    rows = KV_RANK // 4
    for k, g_ref in enumerate((g0_ref, g1_ref, g2_ref, g3_ref)):
        first = pl.multiple_of(((i_ref[0] - k) & 3) * rows, rows)
        gram_ref[pl.ds(first, rows), :] = g_ref[...].astype(f32)
    gram = gram_ref[...]
    s = gram_scale(gram)
    d01, g2 = two_steps(gram * (s * s))
    d2 = c2 * g2 + c3 * mm(g2, g2)
    rest = c1 * d01 + c1 * c1 * d2 + mm(d2, d01)
    y = y_ref[...]
    total = s * math.sqrt(max(KVB_ROWS, KV_RANK))
    out = (c1 * c1 * c1) * y.astype(f32) + mm(y, rest)
    o_ref[...] = (out * total).astype(bf16)


def finish_a_body(f_ref, g_ref, x_ref, o_ref, gram_ref, d01_ref, g2_ref):
    f = f_ref[0]
    gram = whole_gram(g_ref, gram_ref)
    s = gram_scale(gram)
    d01, g2 = two_steps(gram * (s * s))
    d01_ref[...] = d01
    g2_ref[...] = g2
    main = pl.ds(pl.multiple_of(f * MAIN, MAIN), MAIN)
    base = N_FSDP * MAIN + 8 * lax.shift_right_logical(f, 2)
    tail = pl.ds(pl.multiple_of(base, 8), 8)

    def rows(ref):
        return jnp.concatenate([ref[main, :], ref[tail, :]], axis=0)

    g2_rows = rows(g2_ref)
    d2 = c2 * g2_rows + c3 * mm(g2_rows, g2)
    rest = c1 * rows(d01_ref) + c1 * c1 * d2 + mm(d2, d01)
    x_rows = jnp.concatenate([x_ref[main, :].astype(f32), x_ref[pl.ds(pl.multiple_of(N_FSDP * MAIN + 16 * lax.shift_right_logical(f, 3), 16), 16), :].astype(f32)], axis=0)
    total = s * math.sqrt(max(KVA_ROWS, D))
    moved = mm(rest, x_ref[...])
    out = ((c1 * c1 * c1) * x_rows[:MAIN] + moved[:MAIN]) * total
    o_main = out.astype(bf16)
    q = f & 3
    h = f & 7
    x_tail = x_rows[MAIN : MAIN + 2]
    for j in range(1, 8):
        x_tail = jnp.where(h == j, x_rows[MAIN + 2 * j : MAIN + 2 * j + 2], x_tail)
    m_tail = moved[MAIN : MAIN + 2]
    for j in range(1, 4):
        m_tail = jnp.where(q == j, moved[MAIN + 2 * j : MAIN + 2 * j + 2], m_tail)
    o_tail = tail_tile(((c1 * c1 * c1) * x_tail + m_tail) * total).astype(bf16)
    for r in range(N_DP):
        o_ref[r, :, :CHUNK] = o_main
        o_ref[r, :, CHUNK:] = o_tail


def unpack_body(u_ref, o_ref):
    for d in range(N_DP):
        o_ref[:MAIN, d * CHUNK : (d + 1) * CHUNK] = u_ref[d, :, :CHUNK]
        tail = u_ref[d, :, CHUNK:].astype(f32)
        for k in range(GROUPS):
            piece = slice(d * CHUNK + 128 * k, d * CHUNK + 128 * k + 128)
            o_ref[MAIN:, piece] = tail[2 * k : 2 * k + 2].astype(bf16)


def exchange(x, axis):
    return lax.all_to_all(x, axis, split_axis=0, concat_axis=0, tiled=True)


def total_of(x):
    return jnp.sum(x.astype(f32), axis=0)


def shift(x, axis, n, k):
    return lax.ppermute(x, axis, [(i, (i + k) % n) for i in range(n)])


def others(x, axis, n, step=1):
    return [x] + [shift(x, axis, n, k) for k in range(step, n, step)]


def sum_over(x, axis, n, step=1):
    return pair_sums(others(x, axis, n, step))


def pair_sums(terms):
    terms = [y.astype(f32) for y in terms]
    while len(terms) > 1:
        half = len(terms) // 2
        terms = [terms[k] + terms[k + half] for k in range(half)]
    return terms[0].astype(bf16)


def sum_pair(x, axis, n):
    other = lax.ppermute(x, axis, [(i, i ^ 1) for i in range(n)])
    return (x.astype(f32) + other.astype(f32)).astype(bf16)


def local(kva_parts, kvb_parts, kva_moment, kvb_moment):
    y = lax.axis_index("y").astype(jnp.int32).reshape(1)
    c = lax.axis_index("c").astype(jnp.int32).reshape(1)
    f = lax.axis_index(FSDP).astype(jnp.int32).reshape(1)
    d = y * 2 + c
    rows_b = KV_RANK // N_DP

    half = shape((kvb_parts.shape[1] // 2, KV_RANK), bf16)
    packed, send_b = call(
        pack_body,
        (shape((N_DP, MAIN, WIDE), bf16), half),
        1,
        2,
        [pltpu.VMEM(kva_parts.shape, bf16), pltpu.SemaphoreType.DMA((2,))],
        pl.ANY,
        67_000_000,
    )(c, kva_parts, kvb_parts)
    terms_a = exchange(packed, DP)
    grad_b = call(half_b_body, half, 1, 2)(c, kvb_parts, shift(send_b, "c", 2, 1))
    terms_a, grad_b = lax.optimization_barrier((terms_a, grad_b))
    grads_b = others(grad_b, "y", 4)
    grad_a, push_a = call(
        push_a_body,
        (shape((MAIN, WIDE), bf16), shape((N_FSDP, MAIN, WIDE), bf16)),
        1,
        2,
    )(d, terms_a, kva_moment)
    all_a = exchange(push_a, FSDP)

    grad_b = lax.all_gather(pair_sums(grads_b), "c", tiled=True)
    moment_b, long_b, piece_b = call(
        moment_b_body,
        (
            shape(kvb_moment.shape, f32),
            shape(kvb_moment.shape, bf16),
            shape((rows_b, KV_RANK), bf16),
        ),
        1,
        2,
        [pltpu.VMEM((KV_RANK, KV_RANK), f32)],
        flops=HINT,
    )(d, grad_b, kvb_moment)
    piece_b, grad_a = lax.optimization_barrier((piece_b, grad_a))
    piece_b = sum_pair(sum_over(piece_b, "x", 4), "z", 8)

    grads_a = others(lax.all_gather(grad_a, "c"), "y", 4)
    moment_a = call(moment_a_body, shape(kva_moment.shape, f32), 1, 5)(y, *grads_a, kva_moment)
    all_a, moment_a = lax.optimization_barrier((all_a, moment_a))

    gram_a, short_a = call(
        gram_a_body,
        (shape((2, 64 * BLOCKS, 384), bf16), shape((KVA_ROWS, CHUNK), bf16)),
        0,
        1,
        [pltpu.VMEM((128 * BLOCKS, 128 * BLOCKS), f32)],
    )(all_a)
    gram_a = lax.all_gather(gram_a, "c")
    gram_a = lax.dynamic_index_in_dim(gram_a, lax.axis_index("c"), axis=1, keepdims=False)
    gram_a = total_of(gram_a).astype(bf16)
    gram_a, piece_b = lax.optimization_barrier((gram_a, piece_b))
    gram_a = sum_over(gram_a, "y", 4)
    piece_b = sum_over(piece_b, "z", 8, 2)
    gram_a, piece_b = lax.optimization_barrier((gram_a, piece_b))
    gram_a = lax.all_gather(gram_a, "c")
    piece_b = lax.all_gather(piece_b, "c", tiled=True)

    pieces_b = others(piece_b, "y", 4)
    update_a = call(
        finish_a_body,
        shape((N_DP, MAIN, WIDE), bf16),
        1,
        2,
        [pltpu.VMEM((128 * BLOCKS, 128 * BLOCKS), f32)]
        + [pltpu.VMEM((KVA_ROWS, KVA_ROWS), f32)] * 2,
    )(f, gram_a, short_a)
    update_a, pieces_b = lax.optimization_barrier((update_a, pieces_b))
    update_a = call(unpack_body, shape(kva_moment.shape, bf16))(exchange(update_a, DP))
    update_b = call(
        finish_b_body, shape(long_b.shape, bf16), 1, 5, [pltpu.VMEM((KV_RANK, KV_RANK), f32)]
    )(y, *pieces_b, long_b)
    return (moment_a, moment_b, update_a, update_b)


def solution(mesh):
    fine = Mesh(mesh.devices.reshape(4, 2, 4, 8), DP + FSDP)
    return jax.shard_map(
        local,
        mesh=fine,
        in_specs=(P(DP, FSDP, None), P(DP, FSDP, None), P(FSDP, None), P(FSDP, None)),
        out_specs=(P(FSDP, None), P(FSDP, None), P(FSDP, None), P(FSDP, None)),
        check_vma=False,
    )
```

```python
import functools
import math

import jax
import jax.numpy as jnp
from jax import lax
from jax.experimental import pallas as pl
from jax.experimental.pallas import tpu as pltpu
from jax.sharding import Mesh, PartitionSpec as P

D = 7168
KV_RANK = 512
KVA_ROWS = 576
KVB_ROWS = 16384
DP = ("y", "c")
FSDP = ("x", "z")
N_DP = 8
N_FSDP = 32
CHUNK = D // N_DP
GROUPS = CHUNK // 128
MAIN = 16
WIDE = CHUNK + 128
BLOCKS = 5

c1 = 3.4445
c2 = -4.775
c3 = 2.0315
decay_rate = 0.95
norm_epsilon = 1e-07
f32 = jnp.float32
bf16 = jnp.bfloat16
VMEM_LIMIT = 48 * 1024 * 1024
HINT = 40_000_000_000


def call(body, out_shape, n_scalar=0, n_in=1, scratch=(), space=pltpu.VMEM, limit=VMEM_LIMIT, flops=0):
    return pl.pallas_call(
        body,
        out_shape=out_shape,
        in_specs=[pl.BlockSpec(memory_space=pltpu.SMEM)] * n_scalar
        + [pl.BlockSpec(memory_space=space)] * n_in,
        out_specs=jax.tree.map(lambda _: pl.BlockSpec(memory_space=pltpu.VMEM), out_shape),
        scratch_shapes=list(scratch),
        compiler_params=pltpu.CompilerParams(vmem_limit_bytes=limit),
        cost_estimate=pl.CostEstimate(flops=flops, bytes_accessed=0, transcendentals=0)
        if flops
        else None,
    )


def shape(dims, dtype):
    return jax.ShapeDtypeStruct(dims, dtype)


def tail_tile(rows):
    pieces = [rows[:, 128 * k : 128 * k + 128] for k in range(GROUPS)]
    return jnp.concatenate(pieces + [jnp.zeros((2, 128), f32)], axis=0)


def pack_body(c_ref, a_ref, b_ref, o_ref, send_ref, held_ref, sems):
    rows = send_ref.shape[0]
    other = pl.ds(pl.multiple_of((1 - c_ref[0]) * rows, rows), rows)
    copy_a = pltpu.make_async_copy(a_ref, held_ref, sems.at[0])
    copy_b = pltpu.make_async_copy(b_ref.at[0, other], send_ref, sems.at[1])
    copy_a.start()
    copy_b.start()
    copy_a.wait()
    for d in range(N_DP):
        lanes = slice(d * CHUNK, (d + 1) * CHUNK)
        o_ref[d, :, :CHUNK] = held_ref[0, :MAIN, lanes]
        o_ref[d, :, CHUNK:] = tail_tile(held_ref[0, MAIN:, lanes].astype(f32)).astype(bf16)
    copy_b.wait()


def push_a_body(d_ref, parts_ref, m_ref, g_ref, x_ref):
    start = pl.multiple_of(d_ref[0] * CHUNK, 128)
    grad = parts_ref[0].astype(f32)
    for r in range(1, N_DP):
        grad += parts_ref[r].astype(f32)
    g_ref[...] = grad.astype(bf16)
    m_main = m_ref[:MAIN, pl.ds(start, CHUNK)]
    m_tail = tail_tile(m_ref[MAIN:, pl.ds(start, CHUNK)])
    moment = decay_rate * jnp.concatenate([m_main, m_tail], axis=1) + grad
    push = (grad + decay_rate * moment).astype(bf16)
    for r in range(N_FSDP):
        x_ref[r] = push


def moment_a_body(i_ref, g0_ref, g1_ref, g2_ref, g3_ref, m_ref, o_ref):
    for k, g_ref in enumerate((g0_ref, g1_ref, g2_ref, g3_ref)):
        for c in range(2):
            start = (((i_ref[0] - k) & 3) * 2 + c) * CHUNK
            lanes = pl.ds(pl.multiple_of(start, 128), CHUNK)
            main = g_ref[c, :, :CHUNK].astype(f32)
            o_ref[:MAIN, lanes] = decay_rate * m_ref[:MAIN, lanes] + main
            tail = g_ref[c, :, CHUNK:].astype(f32)
            for j in range(GROUPS):
                piece = pl.ds(pl.multiple_of(start + 128 * j, 128), 128)
                o_ref[MAIN:, piece] = decay_rate * m_ref[MAIN:, piece] + tail[2 * j : 2 * j + 2]


def half_b_body(c_ref, b_ref, x_ref, o_ref):
    rows = o_ref.shape[0]
    half = b_ref[0, pl.ds(pl.multiple_of(c_ref[0] * rows, rows), rows)]
    o_ref[...] = (half.astype(f32) + x_ref[...].astype(f32)).astype(bf16)


def moment_b_body(d_ref, g_ref, m_ref, o_ref, y_ref, p_ref, scratch):
    grad = g_ref[...].astype(f32)
    moment = decay_rate * m_ref[...] + grad
    o_ref[...] = moment
    y = (grad + decay_rate * moment).astype(bf16)
    y_ref[...] = y
    scratch[...] = lax.dot_general(y, y, (((0,), (0,)), ((), ())), preferred_element_type=f32)
    rows = KV_RANK // N_DP
    p_ref[...] = scratch[pl.ds(pl.multiple_of(d_ref[0] * rows, rows), rows), :].astype(bf16)


def gram_a_body(x_ref, g_ref, full_ref, gram_ref):
    full_ref[: N_FSDP * MAIN] = x_ref[:, :, :CHUNK].reshape(N_FSDP * MAIN, CHUNK)
    tail = x_ref[:, :, CHUNK:].reshape(N_FSDP * MAIN, 128)
    rows = 2 * N_FSDP
    r = lax.broadcasted_iota(jnp.int32, (rows, N_FSDP * MAIN), 0)
    c = lax.broadcasted_iota(jnp.int32, (rows, N_FSDP * MAIN), 1)
    first = MAIN * lax.shift_right_logical(r, 1) + (r & 1)
    for k in range(GROUPS):
        pick = jnp.where(c == first + 2 * k, 1.0, 0.0).astype(bf16)
        full_ref[N_FSDP * MAIN :, 128 * k : 128 * k + 128] = jnp.dot(
            pick, tail, preferred_element_type=f32
        ).astype(bf16)
    x = full_ref[...]
    gram_ref[...] = jnp.zeros_like(gram_ref)
    gram_ref[:KVA_ROWS, :KVA_ROWS] = lax.dot_general(
        x, x, (((1,), (1,)), ((), ())), preferred_element_type=f32
    )
    for i in range(BLOCKS):
        for h in range(2):
            rows = slice(128 * i + 64 * h, 128 * i + 64 * h + 64)
            for j in range(3):
                k = (i + j) % BLOCKS
                g_ref[h, 64 * i : 64 * i + 64, 128 * j : 128 * j + 128] = gram_ref[
                    rows, 128 * k : 128 * k + 128
                ].astype(bf16)


def whole_gram(t_ref, gram_ref):
    for i in range(BLOCKS):
        for j in range(3):
            k = (i + j) % BLOCKS
            block = jnp.concatenate(
                [t_ref[h, 64 * i : 64 * i + 64, 128 * j : 128 * j + 128] for h in range(2)], axis=0
            ).astype(f32)
            gram_ref[128 * i : 128 * i + 128, 128 * k : 128 * k + 128] = block
            if j:
                gram_ref[128 * k : 128 * k + 128, 128 * i : 128 * i + 128] = block.T
    return gram_ref[:KVA_ROWS, :KVA_ROWS]


def mm(a, b):
    return jnp.dot(a.astype(bf16), b.astype(bf16), preferred_element_type=f32)


def gram_scale(gram):
    n = gram.shape[0]
    r = lax.broadcasted_iota(jnp.int32, (n, n), 0)
    c = lax.broadcasted_iota(jnp.int32, (n, n), 1)
    squares = jnp.sum(jnp.where(r == c, gram, 0.0))
    return 1.0 / (jnp.sqrt(squares) + norm_epsilon)


def two_steps(g0):
    d0 = c2 * g0 + c3 * mm(g0, g0)
    t0 = c1 * g0 + mm(d0, g0)
    g1 = c1 * t0 + mm(d0, t0)
    d1 = c2 * g1 + c3 * mm(g1, g1)
    d01 = c1 * (d0 + d1) + mm(d1, d0)
    t1 = c1 * g1 + mm(d1, g1)
    g2 = c1 * t1 + mm(d1, t1)
    return d01, g2


def finish_b_body(i_ref, g0_ref, g1_ref, g2_ref, g3_ref, y_ref, o_ref, gram_ref):
    rows = KV_RANK // 4
    for k, g_ref in enumerate((g0_ref, g1_ref, g2_ref, g3_ref)):
        first = pl.multiple_of(((i_ref[0] - k) & 3) * rows, rows)
        gram_ref[pl.ds(first, rows), :] = g_ref[...].astype(f32)
    gram = gram_ref[...]
    s = gram_scale(gram)
    d01, g2 = two_steps(gram * (s * s))
    d2 = c2 * g2 + c3 * mm(g2, g2)
    rest = c1 * d01 + c1 * c1 * d2 + mm(d2, d01)
    y = y_ref[...]
    total = s * math.sqrt(max(KVB_ROWS, KV_RANK))
    out = (c1 * c1 * c1) * y.astype(f32) + mm(y, rest)
    o_ref[...] = (out * total).astype(bf16)


def finish_a_body(f_ref, g_ref, x_ref, o_ref, gram_ref, d01_ref, g2_ref):
    f = f_ref[0]
    gram = whole_gram(g_ref, gram_ref)
    s = gram_scale(gram)
    d01, g2 = two_steps(gram * (s * s))
    d01_ref[...] = d01
    g2_ref[...] = g2
    main = pl.ds(pl.multiple_of(f * MAIN, MAIN), MAIN)
    base = N_FSDP * MAIN + 8 * lax.shift_right_logical(f, 2)
    tail = pl.ds(pl.multiple_of(base, 8), 8)

    def rows(ref):
        return jnp.concatenate([ref[main, :], ref[tail, :]], axis=0)

    g2_rows = rows(g2_ref)
    d2 = c2 * g2_rows + c3 * mm(g2_rows, g2)
    rest = c1 * rows(d01_ref) + c1 * c1 * d2 + mm(d2, d01)
    x_rows = jnp.concatenate([x_ref[main, :].astype(f32), x_ref[pl.ds(pl.multiple_of(N_FSDP * MAIN + 16 * lax.shift_right_logical(f, 3), 16), 16), :].astype(f32)], axis=0)
    total = s * math.sqrt(max(KVA_ROWS, D))
    moved = mm(rest, x_ref[...])
    out = ((c1 * c1 * c1) * x_rows[:MAIN] + moved[:MAIN]) * total
    o_main = out.astype(bf16)
    q = f & 3
    h = f & 7
    x_tail = x_rows[MAIN : MAIN + 2]
    for j in range(1, 8):
        x_tail = jnp.where(h == j, x_rows[MAIN + 2 * j : MAIN + 2 * j + 2], x_tail)
    m_tail = moved[MAIN : MAIN + 2]
    for j in range(1, 4):
        m_tail = jnp.where(q == j, moved[MAIN + 2 * j : MAIN + 2 * j + 2], m_tail)
    o_tail = tail_tile(((c1 * c1 * c1) * x_tail + m_tail) * total).astype(bf16)
    for r in range(N_DP):
        o_ref[r, :, :CHUNK] = o_main
        o_ref[r, :, CHUNK:] = o_tail


def unpack_body(u_ref, o_ref):
    for d in range(N_DP):
        o_ref[:MAIN, d * CHUNK : (d + 1) * CHUNK] = u_ref[d, :, :CHUNK]
        tail = u_ref[d, :, CHUNK:].astype(f32)
        for k in range(GROUPS):
            piece = slice(d * CHUNK + 128 * k, d * CHUNK + 128 * k + 128)
            o_ref[MAIN:, piece] = tail[2 * k : 2 * k + 2].astype(bf16)


def exchange(x, axis):
    return lax.all_to_all(x, axis, split_axis=0, concat_axis=0, tiled=True)


def total_of(x):
    return jnp.sum(x.astype(f32), axis=0)


def shift(x, axis, n, k):
    return lax.ppermute(x, axis, [(i, (i + k) % n) for i in range(n)])


def others(x, axis, n, step=1):
    return [x] + [shift(x, axis, n, k) for k in range(step, n, step)]


def sum_over(x, axis, n, step=1):
    return pair_sums(others(x, axis, n, step))


def pair_sums(terms):
    terms = [y.astype(f32) for y in terms]
    while len(terms) > 1:
        half = len(terms) // 2
        terms = [terms[k] + terms[k + half] for k in range(half)]
    return terms[0].astype(bf16)


def sum_pair(x, axis, n):
    other = lax.ppermute(x, axis, [(i, i ^ 1) for i in range(n)])
    return (x.astype(f32) + other.astype(f32)).astype(bf16)


def local(kva_parts, kvb_parts, kva_moment, kvb_moment):
    y = lax.axis_index("y").astype(jnp.int32).reshape(1)
    c = lax.axis_index("c").astype(jnp.int32).reshape(1)
    f = lax.axis_index(FSDP).astype(jnp.int32).reshape(1)
    d = y * 2 + c
    rows_b = KV_RANK // N_DP

    half = shape((kvb_parts.shape[1] // 2, KV_RANK), bf16)
    packed, send_b = call(
        pack_body,
        (shape((N_DP, MAIN, WIDE), bf16), half),
        1,
        2,
        [pltpu.VMEM(kva_parts.shape, bf16), pltpu.SemaphoreType.DMA((2,))],
        pl.ANY,
        67_000_000,
    )(c, kva_parts, kvb_parts)
    terms_a = exchange(packed, DP)
    grad_b = call(half_b_body, half, 1, 2)(c, kvb_parts, shift(send_b, "c", 2, 1))
    terms_a, grad_b = lax.optimization_barrier((terms_a, grad_b))
    grads_b = others(grad_b, "y", 4)
    grad_a, push_a = call(
        push_a_body,
        (shape((MAIN, WIDE), bf16), shape((N_FSDP, MAIN, WIDE), bf16)),
        1,
        2,
    )(d, terms_a, kva_moment)
    all_a = exchange(push_a, FSDP)

    grad_b = lax.all_gather(pair_sums(grads_b), "c", tiled=True)
    moment_b, long_b, piece_b = call(
        moment_b_body,
        (
            shape(kvb_moment.shape, f32),
            shape(kvb_moment.shape, bf16),
            shape((rows_b, KV_RANK), bf16),
        ),
        1,
        2,
        [pltpu.VMEM((KV_RANK, KV_RANK), f32)],
        flops=HINT,
    )(d, grad_b, kvb_moment)
    piece_b, grad_a = lax.optimization_barrier((piece_b, grad_a))
    piece_b = sum_over(sum_over(piece_b, "x", 4), "z", 8, 2)

    grads_a = others(lax.all_gather(grad_a, "c"), "y", 4)
    moment_a = call(moment_a_body, shape(kva_moment.shape, f32), 1, 5)(y, *grads_a, kva_moment)
    all_a, moment_a = lax.optimization_barrier((all_a, moment_a))

    gram_a, short_a = call(
        gram_a_body,
        (shape((2, 64 * BLOCKS, 384), bf16), shape((KVA_ROWS, CHUNK), bf16)),
        0,
        1,
        [pltpu.VMEM((128 * BLOCKS, 128 * BLOCKS), f32)],
    )(all_a)
    gram_a = lax.all_gather(gram_a, "c")
    gram_a = lax.dynamic_index_in_dim(gram_a, lax.axis_index("c"), axis=1, keepdims=False)
    gram_a = total_of(gram_a).astype(bf16)
    gram_a, piece_b = lax.optimization_barrier((gram_a, piece_b))
    gram_a = lax.all_gather(sum_over(gram_a, "y", 4), "c")
    piece_b = lax.all_gather(sum_pair(piece_b, "z", 8), "c", tiled=True)

    pieces_b = others(piece_b, "y", 4)
    update_a = call(
        finish_a_body,
        shape((N_DP, MAIN, WIDE), bf16),
        1,
        2,
        [pltpu.VMEM((128 * BLOCKS, 128 * BLOCKS), f32)]
        + [pltpu.VMEM((KVA_ROWS, KVA_ROWS), f32)] * 2,
    )(f, gram_a, short_a)
    update_a, pieces_b = lax.optimization_barrier((update_a, pieces_b))
    update_a = call(unpack_body, shape(kva_moment.shape, bf16))(exchange(update_a, DP))
    update_b = call(
        finish_b_body, shape(long_b.shape, bf16), 1, 5, [pltpu.VMEM((KV_RANK, KV_RANK), f32)]
    )(y, *pieces_b, long_b)
    return (moment_a, moment_b, update_a, update_b)


def solution(mesh):
    fine = Mesh(mesh.devices.reshape(4, 2, 4, 8), DP + FSDP)
    return jax.shard_map(
        local,
        mesh=fine,
        in_specs=(P(DP, FSDP, None), P(DP, FSDP, None), P(FSDP, None), P(FSDP, None)),
        out_specs=(P(FSDP, None), P(FSDP, None), P(FSDP, None), P(FSDP, None)),
        check_vma=False,
    )
```

```python
import functools
import math

import jax
import jax.numpy as jnp
from jax import lax
from jax.experimental import pallas as pl
from jax.experimental.pallas import tpu as pltpu
from jax.sharding import Mesh, PartitionSpec as P

D = 7168
KV_RANK = 512
KVA_ROWS = 576
KVB_ROWS = 16384
DP = ("y", "c")
FSDP = ("x", "z")
N_DP = 8
N_FSDP = 32
CHUNK = D // N_DP
GROUPS = CHUNK // 128
MAIN = 16
WIDE = CHUNK + 128
BLOCKS = 5

c1 = 3.4445
c2 = -4.775
c3 = 2.0315
decay_rate = 0.95
norm_epsilon = 1e-07
f32 = jnp.float32
bf16 = jnp.bfloat16
VMEM_LIMIT = 48 * 1024 * 1024
HINT = 40_000_000_000


def call(body, out_shape, n_scalar=0, n_in=1, scratch=(), space=pltpu.VMEM, limit=VMEM_LIMIT, flops=0):
    return pl.pallas_call(
        body,
        out_shape=out_shape,
        in_specs=[pl.BlockSpec(memory_space=pltpu.SMEM)] * n_scalar
        + [pl.BlockSpec(memory_space=space)] * n_in,
        out_specs=jax.tree.map(lambda _: pl.BlockSpec(memory_space=pltpu.VMEM), out_shape),
        scratch_shapes=list(scratch),
        compiler_params=pltpu.CompilerParams(vmem_limit_bytes=limit),
        cost_estimate=pl.CostEstimate(flops=flops, bytes_accessed=0, transcendentals=0)
        if flops
        else None,
    )


def shape(dims, dtype):
    return jax.ShapeDtypeStruct(dims, dtype)


def tail_tile(rows):
    pieces = [rows[:, 128 * k : 128 * k + 128] for k in range(GROUPS)]
    return jnp.concatenate(pieces + [jnp.zeros((2, 128), f32)], axis=0)


def pack_body(c_ref, a_ref, b_ref, o_ref, send_ref, held_ref, sems):
    rows = send_ref.shape[0]
    other = pl.ds(pl.multiple_of((1 - c_ref[0]) * rows, rows), rows)
    copy_a = pltpu.make_async_copy(a_ref, held_ref, sems.at[0])
    copy_b = pltpu.make_async_copy(b_ref.at[0, other], send_ref, sems.at[1])
    copy_a.start()
    copy_b.start()
    copy_a.wait()
    for d in range(N_DP):
        lanes = slice(d * CHUNK, (d + 1) * CHUNK)
        o_ref[d, :, :CHUNK] = held_ref[0, :MAIN, lanes]
        o_ref[d, :, CHUNK:] = tail_tile(held_ref[0, MAIN:, lanes].astype(f32)).astype(bf16)
    copy_b.wait()


def push_a_body(d_ref, parts_ref, m_ref, g_ref, x_ref):
    start = pl.multiple_of(d_ref[0] * CHUNK, 128)
    grad = parts_ref[0].astype(f32)
    for r in range(1, N_DP):
        grad += parts_ref[r].astype(f32)
    g_ref[...] = grad.astype(bf16)
    m_main = m_ref[:MAIN, pl.ds(start, CHUNK)]
    m_tail = tail_tile(m_ref[MAIN:, pl.ds(start, CHUNK)])
    moment = decay_rate * jnp.concatenate([m_main, m_tail], axis=1) + grad
    push = (grad + decay_rate * moment).astype(bf16)
    for r in range(N_FSDP):
        x_ref[r] = push


def moment_a_body(i_ref, g0_ref, g1_ref, g2_ref, g3_ref, m_ref, o_ref):
    for k, g_ref in enumerate((g0_ref, g1_ref, g2_ref, g3_ref)):
        for c in range(2):
            start = (((i_ref[0] - k) & 3) * 2 + c) * CHUNK
            lanes = pl.ds(pl.multiple_of(start, 128), CHUNK)
            main = g_ref[c, :, :CHUNK].astype(f32)
            o_ref[:MAIN, lanes] = decay_rate * m_ref[:MAIN, lanes] + main
            tail = g_ref[c, :, CHUNK:].astype(f32)
            for j in range(GROUPS):
                piece = pl.ds(pl.multiple_of(start + 128 * j, 128), 128)
                o_ref[MAIN:, piece] = decay_rate * m_ref[MAIN:, piece] + tail[2 * j : 2 * j + 2]


def half_b_body(c_ref, b_ref, x_ref, o_ref):
    rows = o_ref.shape[0]
    half = b_ref[0, pl.ds(pl.multiple_of(c_ref[0] * rows, rows), rows)]
    o_ref[...] = (half.astype(f32) + x_ref[...].astype(f32)).astype(bf16)


def moment_b_body(d_ref, g_ref, m_ref, o_ref, y_ref, p_ref, scratch):
    grad = g_ref[...].astype(f32)
    moment = decay_rate * m_ref[...] + grad
    o_ref[...] = moment
    y = (grad + decay_rate * moment).astype(bf16)
    y_ref[...] = y
    scratch[...] = lax.dot_general(y, y, (((0,), (0,)), ((), ())), preferred_element_type=f32)
    rows = KV_RANK // N_DP
    p_ref[...] = scratch[pl.ds(pl.multiple_of(d_ref[0] * rows, rows), rows), :].astype(bf16)


def gram_a_body(x_ref, g_ref, full_ref, gram_ref):
    full_ref[: N_FSDP * MAIN] = x_ref[:, :, :CHUNK].reshape(N_FSDP * MAIN, CHUNK)
    tail = x_ref[:, :, CHUNK:].reshape(N_FSDP * MAIN, 128)
    rows = 2 * N_FSDP
    r = lax.broadcasted_iota(jnp.int32, (rows, N_FSDP * MAIN), 0)
    c = lax.broadcasted_iota(jnp.int32, (rows, N_FSDP * MAIN), 1)
    first = MAIN * lax.shift_right_logical(r, 1) + (r & 1)
    for k in range(GROUPS):
        pick = jnp.where(c == first + 2 * k, 1.0, 0.0).astype(bf16)
        full_ref[N_FSDP * MAIN :, 128 * k : 128 * k + 128] = jnp.dot(
            pick, tail, preferred_element_type=f32
        ).astype(bf16)
    x = full_ref[...]
    gram_ref[...] = jnp.zeros_like(gram_ref)
    gram_ref[:KVA_ROWS, :KVA_ROWS] = lax.dot_general(
        x, x, (((1,), (1,)), ((), ())), preferred_element_type=f32
    )
    for i in range(BLOCKS):
        for h in range(2):
            rows = slice(128 * i + 64 * h, 128 * i + 64 * h + 64)
            for j in range(3):
                k = (i + j) % BLOCKS
                g_ref[h, 64 * i : 64 * i + 64, 128 * j : 128 * j + 128] = gram_ref[
                    rows, 128 * k : 128 * k + 128
                ].astype(bf16)


def whole_gram(t_ref, gram_ref):
    for i in range(BLOCKS):
        for j in range(3):
            k = (i + j) % BLOCKS
            block = jnp.concatenate(
                [t_ref[h, 64 * i : 64 * i + 64, 128 * j : 128 * j + 128] for h in range(2)], axis=0
            ).astype(f32)
            gram_ref[128 * i : 128 * i + 128, 128 * k : 128 * k + 128] = block
            if j:
                gram_ref[128 * k : 128 * k + 128, 128 * i : 128 * i + 128] = block.T
    return gram_ref[:KVA_ROWS, :KVA_ROWS]


def mm(a, b):
    return jnp.dot(a.astype(bf16), b.astype(bf16), preferred_element_type=f32)


def gram_scale(gram):
    n = gram.shape[0]
    r = lax.broadcasted_iota(jnp.int32, (n, n), 0)
    c = lax.broadcasted_iota(jnp.int32, (n, n), 1)
    squares = jnp.sum(jnp.where(r == c, gram, 0.0))
    return 1.0 / (jnp.sqrt(squares) + norm_epsilon)


def two_steps(g0):
    d0 = c2 * g0 + c3 * mm(g0, g0)
    t0 = c1 * g0 + mm(d0, g0)
    g1 = c1 * t0 + mm(d0, t0)
    d1 = c2 * g1 + c3 * mm(g1, g1)
    d01 = c1 * (d0 + d1) + mm(d1, d0)
    t1 = c1 * g1 + mm(d1, g1)
    g2 = c1 * t1 + mm(d1, t1)
    return d01, g2


def finish_b_body(i_ref, g0_ref, g1_ref, g2_ref, g3_ref, y_ref, o_ref, gram_ref):
    rows = KV_RANK // 4
    for k, g_ref in enumerate((g0_ref, g1_ref, g2_ref, g3_ref)):
        first = pl.multiple_of(((i_ref[0] - k) & 3) * rows, rows)
        gram_ref[pl.ds(first, rows), :] = g_ref[...].astype(f32)
    gram = gram_ref[...]
    s = gram_scale(gram)
    d01, g2 = two_steps(gram * (s * s))
    d2 = c2 * g2 + c3 * mm(g2, g2)
    rest = c1 * d01 + c1 * c1 * d2 + mm(d2, d01)
    y = y_ref[...]
    total = s * math.sqrt(max(KVB_ROWS, KV_RANK))
    out = (c1 * c1 * c1) * y.astype(f32) + mm(y, rest)
    o_ref[...] = (out * total).astype(bf16)


def finish_a_body(f_ref, g_ref, x_ref, o_ref, gram_ref, d01_ref, g2_ref):
    f = f_ref[0]
    gram = whole_gram(g_ref, gram_ref)
    s = gram_scale(gram)
    d01, g2 = two_steps(gram * (s * s))
    d01_ref[...] = d01
    g2_ref[...] = g2
    main = pl.ds(pl.multiple_of(f * MAIN, MAIN), MAIN)
    base = N_FSDP * MAIN + 8 * lax.shift_right_logical(f, 2)
    tail = pl.ds(pl.multiple_of(base, 8), 8)

    def rows(ref):
        return jnp.concatenate([ref[main, :], ref[tail, :]], axis=0)

    g2_rows = rows(g2_ref)
    d2 = c2 * g2_rows + c3 * mm(g2_rows, g2)
    rest = c1 * rows(d01_ref) + c1 * c1 * d2 + mm(d2, d01)
    x_rows = jnp.concatenate([x_ref[main, :].astype(f32), x_ref[pl.ds(pl.multiple_of(N_FSDP * MAIN + 16 * lax.shift_right_logical(f, 3), 16), 16), :].astype(f32)], axis=0)
    total = s * math.sqrt(max(KVA_ROWS, D))
    moved = mm(rest, x_ref[...])
    out = ((c1 * c1 * c1) * x_rows[:MAIN] + moved[:MAIN]) * total
    o_main = out.astype(bf16)
    q = f & 3
    h = f & 7
    x_tail = x_rows[MAIN : MAIN + 2]
    for j in range(1, 8):
        x_tail = jnp.where(h == j, x_rows[MAIN + 2 * j : MAIN + 2 * j + 2], x_tail)
    m_tail = moved[MAIN : MAIN + 2]
    for j in range(1, 4):
        m_tail = jnp.where(q == j, moved[MAIN + 2 * j : MAIN + 2 * j + 2], m_tail)
    o_tail = tail_tile(((c1 * c1 * c1) * x_tail + m_tail) * total).astype(bf16)
    for r in range(N_DP):
        o_ref[r, :, :CHUNK] = o_main
        o_ref[r, :, CHUNK:] = o_tail


def unpack_body(u_ref, o_ref):
    for d in range(N_DP):
        o_ref[:MAIN, d * CHUNK : (d + 1) * CHUNK] = u_ref[d, :, :CHUNK]
        tail = u_ref[d, :, CHUNK:].astype(f32)
        for k in range(GROUPS):
            piece = slice(d * CHUNK + 128 * k, d * CHUNK + 128 * k + 128)
            o_ref[MAIN:, piece] = tail[2 * k : 2 * k + 2].astype(bf16)


def exchange(x, axis):
    return lax.all_to_all(x, axis, split_axis=0, concat_axis=0, tiled=True)


def total_of(x):
    return jnp.sum(x.astype(f32), axis=0)


def shift(x, axis, n, k):
    return lax.ppermute(x, axis, [(i, (i + k) % n) for i in range(n)])


def others(x, axis, n, step=1):
    return [x] + [shift(x, axis, n, k) for k in range(step, n, step)]


def sum_over(x, axis, n, step=1):
    return pair_sums(others(x, axis, n, step))


def pair_sums(terms):
    terms = [y.astype(f32) for y in terms]
    while len(terms) > 1:
        half = len(terms) // 2
        terms = [terms[k] + terms[k + half] for k in range(half)]
    return terms[0].astype(bf16)


def sum_pair(x, axis, n):
    other = lax.ppermute(x, axis, [(i, i ^ 1) for i in range(n)])
    return (x.astype(f32) + other.astype(f32)).astype(bf16)


def local(kva_parts, kvb_parts, kva_moment, kvb_moment):
    y = lax.axis_index("y").astype(jnp.int32).reshape(1)
    c = lax.axis_index("c").astype(jnp.int32).reshape(1)
    f = lax.axis_index(FSDP).astype(jnp.int32).reshape(1)
    d = y * 2 + c
    rows_b = KV_RANK // N_DP

    half = shape((kvb_parts.shape[1] // 2, KV_RANK), bf16)
    packed, send_b = call(
        pack_body,
        (shape((N_DP, MAIN, WIDE), bf16), half),
        1,
        2,
        [pltpu.VMEM(kva_parts.shape, bf16), pltpu.SemaphoreType.DMA((2,))],
        pl.ANY,
        67_000_000,
    )(c, kva_parts, kvb_parts)
    terms_a = exchange(packed, DP)
    grad_b = call(half_b_body, half, 1, 2)(c, kvb_parts, shift(send_b, "c", 2, 1))
    terms_a, grad_b = lax.optimization_barrier((terms_a, grad_b))
    grads_b = others(grad_b, "y", 4)
    grad_a, push_a = call(
        push_a_body,
        (shape((MAIN, WIDE), bf16), shape((N_FSDP, MAIN, WIDE), bf16)),
        1,
        2,
    )(d, terms_a, kva_moment)
    all_a = exchange(push_a, FSDP)

    grad_b = lax.all_gather(pair_sums(grads_b), "c", tiled=True)
    moment_b, long_b, piece_b = call(
        moment_b_body,
        (
            shape(kvb_moment.shape, f32),
            shape(kvb_moment.shape, bf16),
            shape((rows_b, KV_RANK), bf16),
        ),
        1,
        2,
        [pltpu.VMEM((KV_RANK, KV_RANK), f32)],
        flops=HINT,
    )(d, grad_b, kvb_moment)
    piece_b, grad_a = lax.optimization_barrier((piece_b, grad_a))
    terms_b = others(sum_over(piece_b, "x", 4), "z", 8, 2)

    grads_a = others(lax.all_gather(grad_a, "c"), "y", 4)
    moment_a = call(moment_a_body, shape(kva_moment.shape, f32), 1, 5)(y, *grads_a, kva_moment)
    all_a, moment_a = lax.optimization_barrier((all_a, moment_a))

    gram_a, short_a = call(
        gram_a_body,
        (shape((2, 64 * BLOCKS, 384), bf16), shape((KVA_ROWS, CHUNK), bf16)),
        0,
        1,
        [pltpu.VMEM((128 * BLOCKS, 128 * BLOCKS), f32)],
    )(all_a)
    gram_a = lax.all_gather(gram_a, "c")
    gram_a = lax.dynamic_index_in_dim(gram_a, lax.axis_index("c"), axis=1, keepdims=False)
    gram_a = total_of(gram_a).astype(bf16)
    _, terms_b = lax.optimization_barrier((gram_a, terms_b))
    piece_b = pair_sums(terms_b)
    gram_a = lax.all_gather(sum_over(gram_a, "y", 4), "c")
    piece_b = lax.all_gather(sum_pair(piece_b, "z", 8), "c", tiled=True)

    pieces_b = others(piece_b, "y", 4)
    update_a = call(
        finish_a_body,
        shape((N_DP, MAIN, WIDE), bf16),
        1,
        2,
        [pltpu.VMEM((128 * BLOCKS, 128 * BLOCKS), f32)]
        + [pltpu.VMEM((KVA_ROWS, KVA_ROWS), f32)] * 2,
    )(f, gram_a, short_a)
    update_a, pieces_b = lax.optimization_barrier((update_a, pieces_b))
    update_a = call(unpack_body, shape(kva_moment.shape, bf16))(exchange(update_a, DP))
    update_b = call(
        finish_b_body, shape(long_b.shape, bf16), 1, 5, [pltpu.VMEM((KV_RANK, KV_RANK), f32)]
    )(y, *pieces_b, long_b)
    return (moment_a, moment_b, update_a, update_b)


def solution(mesh):
    fine = Mesh(mesh.devices.reshape(4, 2, 4, 8), DP + FSDP)
    return jax.shard_map(
        local,
        mesh=fine,
        in_specs=(P(DP, FSDP, None), P(DP, FSDP, None), P(FSDP, None), P(FSDP, None)),
        out_specs=(P(FSDP, None), P(FSDP, None), P(FSDP, None), P(FSDP, None)),
        check_vma=False,
    )
```

```python
import functools
import math

import jax
import jax.numpy as jnp
from jax import lax
from jax.experimental import pallas as pl
from jax.experimental.pallas import tpu as pltpu
from jax.sharding import Mesh, PartitionSpec as P

D = 7168
KV_RANK = 512
KVA_ROWS = 576
KVB_ROWS = 16384
DP = ("y", "c")
FSDP = ("x", "z")
N_DP = 8
N_FSDP = 32
CHUNK = D // N_DP
GROUPS = CHUNK // 128
MAIN = 16
WIDE = CHUNK + 128
BLOCKS = 5

c1 = 3.4445
c2 = -4.775
c3 = 2.0315
decay_rate = 0.95
norm_epsilon = 1e-07
f32 = jnp.float32
bf16 = jnp.bfloat16
VMEM_LIMIT = 48 * 1024 * 1024
HINT = 40_000_000_000


def call(body, out_shape, n_scalar=0, n_in=1, scratch=(), space=pltpu.VMEM, limit=VMEM_LIMIT, flops=0):
    return pl.pallas_call(
        body,
        out_shape=out_shape,
        in_specs=[pl.BlockSpec(memory_space=pltpu.SMEM)] * n_scalar
        + [pl.BlockSpec(memory_space=space)] * n_in,
        out_specs=jax.tree.map(lambda _: pl.BlockSpec(memory_space=pltpu.VMEM), out_shape),
        scratch_shapes=list(scratch),
        compiler_params=pltpu.CompilerParams(vmem_limit_bytes=limit),
        cost_estimate=pl.CostEstimate(flops=flops, bytes_accessed=0, transcendentals=0)
        if flops
        else None,
    )


def shape(dims, dtype):
    return jax.ShapeDtypeStruct(dims, dtype)


def tail_tile(rows):
    pieces = [rows[:, 128 * k : 128 * k + 128] for k in range(GROUPS)]
    return jnp.concatenate(pieces + [jnp.zeros((2, 128), f32)], axis=0)


def pack_body(c_ref, a_ref, b_ref, o_ref, send_ref, held_ref, sems):
    rows = send_ref.shape[0]
    other = pl.ds(pl.multiple_of((1 - c_ref[0]) * rows, rows), rows)
    copy_a = pltpu.make_async_copy(a_ref, held_ref, sems.at[0])
    copy_b = pltpu.make_async_copy(b_ref.at[0, other], send_ref, sems.at[1])
    copy_a.start()
    copy_b.start()
    copy_a.wait()
    for d in range(N_DP):
        lanes = slice(d * CHUNK, (d + 1) * CHUNK)
        o_ref[d, :, :CHUNK] = held_ref[0, :MAIN, lanes]
        o_ref[d, :, CHUNK:] = tail_tile(held_ref[0, MAIN:, lanes].astype(f32)).astype(bf16)
    copy_b.wait()


def push_a_body(d_ref, parts_ref, m_ref, g_ref, x_ref):
    start = pl.multiple_of(d_ref[0] * CHUNK, 128)
    grad = parts_ref[0].astype(f32)
    for r in range(1, N_DP):
        grad += parts_ref[r].astype(f32)
    g_ref[:MAIN] = grad[:, :KV_RANK].astype(bf16)
    g_ref[MAIN:] = grad[:, KV_RANK:].astype(bf16)
    m_main = m_ref[:MAIN, pl.ds(start, CHUNK)]
    m_tail = tail_tile(m_ref[MAIN:, pl.ds(start, CHUNK)])
    moment = decay_rate * jnp.concatenate([m_main, m_tail], axis=1) + grad
    push = (grad + decay_rate * moment).astype(bf16)
    for r in range(x_ref.shape[0]):
        x_ref[r] = push


def moment_a_body(i_ref, g0_ref, g1_ref, g2_ref, g3_ref, m_ref, o_ref):
    for k, g_ref in enumerate((g0_ref, g1_ref, g2_ref, g3_ref)):
        for c in range(2):
            start = (((i_ref[0] - k) & 3) * 2 + c) * CHUNK
            lanes = pl.ds(pl.multiple_of(start, 128), CHUNK)
            grad = jnp.concatenate([g_ref[c, :MAIN], g_ref[c, MAIN:]], axis=1).astype(f32)
            main = grad[:, :CHUNK]
            o_ref[:MAIN, lanes] = decay_rate * m_ref[:MAIN, lanes] + main
            tail = grad[:, CHUNK:]
            for j in range(GROUPS):
                piece = pl.ds(pl.multiple_of(start + 128 * j, 128), 128)
                o_ref[MAIN:, piece] = decay_rate * m_ref[MAIN:, piece] + tail[2 * j : 2 * j + 2]


def half_b_body(c_ref, b_ref, x_ref, o_ref):
    rows = o_ref.shape[0]
    half = b_ref[0, pl.ds(pl.multiple_of(c_ref[0] * rows, rows), rows)]
    o_ref[...] = (half.astype(f32) + x_ref[...].astype(f32)).astype(bf16)


def sum_b_body(b0_ref, b1_ref, b2_ref, b3_ref, g_ref, o_ref):
    rows = b0_ref.shape[0]
    first = b0_ref[...].astype(f32) + b2_ref[...].astype(f32)
    second = b1_ref[...].astype(f32) + b3_ref[...].astype(f32)
    o_ref[:rows] = (first + second).astype(bf16)
    o_ref[rows:] = g_ref[...]


def moment_b_body(d_ref, g_ref, m_ref, o_ref, y_ref, p_ref, a_ref, scratch):
    rows = m_ref.shape[0] // 2
    a_ref[...] = g_ref[:, rows:]
    grad = jnp.concatenate([g_ref[0, :rows], g_ref[1, :rows]], axis=0).astype(f32)
    moment = decay_rate * m_ref[...] + grad
    o_ref[...] = moment
    y = (grad + decay_rate * moment).astype(bf16)
    y_ref[...] = y
    scratch[...] = lax.dot_general(y, y, (((0,), (0,)), ((), ())), preferred_element_type=f32)
    rows = KV_RANK // N_DP
    p_ref[...] = scratch[pl.ds(pl.multiple_of(d_ref[0] * rows, rows), rows), :].astype(bf16)


def gram_a_body(x0_ref, x1_ref, x2_ref, x3_ref, g_ref, full_ref, gram_ref):
    tails = []
    for k, x_ref in enumerate((x0_ref, x1_ref, x2_ref, x3_ref)):
        full_ref[128 * k : 128 * k + 128] = x_ref[:, :, :CHUNK].reshape(128, CHUNK)
        tails.append(x_ref[:, :, CHUNK:].reshape(128, 128))
    tail = jnp.concatenate(tails, axis=0)
    rows = 2 * N_FSDP
    r = lax.broadcasted_iota(jnp.int32, (rows, N_FSDP * MAIN), 0)
    c = lax.broadcasted_iota(jnp.int32, (rows, N_FSDP * MAIN), 1)
    first = MAIN * lax.shift_right_logical(r, 1) + (r & 1)
    for k in range(GROUPS):
        pick = jnp.where(c == first + 2 * k, 1.0, 0.0).astype(bf16)
        full_ref[N_FSDP * MAIN :, 128 * k : 128 * k + 128] = jnp.dot(
            pick, tail, preferred_element_type=f32
        ).astype(bf16)
    x = full_ref[...]
    gram_ref[...] = jnp.zeros_like(gram_ref)
    gram_ref[:KVA_ROWS, :KVA_ROWS] = lax.dot_general(
        x, x, (((1,), (1,)), ((), ())), preferred_element_type=f32
    )
    for i in range(BLOCKS):
        for h in range(2):
            rows = slice(128 * i + 64 * h, 128 * i + 64 * h + 64)
            for j in range(3):
                k = (i + j) % BLOCKS
                g_ref[h, 64 * i : 64 * i + 64, 128 * j : 128 * j + 128] = gram_ref[
                    rows, 128 * k : 128 * k + 128
                ].astype(bf16)


def whole_gram(t_ref, gram_ref):
    for i in range(BLOCKS):
        for j in range(3):
            k = (i + j) % BLOCKS
            block = jnp.concatenate(
                [t_ref[h, 64 * i : 64 * i + 64, 128 * j : 128 * j + 128] for h in range(2)], axis=0
            ).astype(f32)
            gram_ref[128 * i : 128 * i + 128, 128 * k : 128 * k + 128] = block
            if j:
                gram_ref[128 * k : 128 * k + 128, 128 * i : 128 * i + 128] = block.T
    return gram_ref[:KVA_ROWS, :KVA_ROWS]


def mm(a, b):
    return jnp.dot(a.astype(bf16), b.astype(bf16), preferred_element_type=f32)


def gram_scale(gram):
    n = gram.shape[0]
    r = lax.broadcasted_iota(jnp.int32, (n, n), 0)
    c = lax.broadcasted_iota(jnp.int32, (n, n), 1)
    squares = jnp.sum(jnp.where(r == c, gram, 0.0))
    return 1.0 / (jnp.sqrt(squares) + norm_epsilon)


def two_steps(g0):
    d0 = c2 * g0 + c3 * mm(g0, g0)
    t0 = c1 * g0 + mm(d0, g0)
    g1 = c1 * t0 + mm(d0, t0)
    d1 = c2 * g1 + c3 * mm(g1, g1)
    d01 = c1 * (d0 + d1) + mm(d1, d0)
    t1 = c1 * g1 + mm(d1, g1)
    g2 = c1 * t1 + mm(d1, t1)
    return d01, g2


def finish_b_body(i_ref, g0_ref, g1_ref, g2_ref, g3_ref, y_ref, o_ref, gram_ref):
    rows = KV_RANK // 4
    for k, g_ref in enumerate((g0_ref, g1_ref, g2_ref, g3_ref)):
        first = pl.multiple_of(((i_ref[0] - k) & 3) * rows, rows)
        gram_ref[pl.ds(first, rows), :] = g_ref[...].astype(f32)
    gram = gram_ref[...]
    s = gram_scale(gram)
    d01, g2 = two_steps(gram * (s * s))
    d2 = c2 * g2 + c3 * mm(g2, g2)
    rest = c1 * d01 + c1 * c1 * d2 + mm(d2, d01)
    y = y_ref[...]
    total = s * math.sqrt(max(KVB_ROWS, KV_RANK))
    out = (c1 * c1 * c1) * y.astype(f32) + mm(y, rest)
    o_ref[...] = (out * total).astype(bf16)


def finish_a_body(f_ref, g_ref, x_ref, o_ref, gram_ref, d01_ref, g2_ref):
    f = f_ref[0]
    gram = whole_gram(g_ref, gram_ref)
    s = gram_scale(gram)
    d01, g2 = two_steps(gram * (s * s))
    d01_ref[...] = d01
    g2_ref[...] = g2
    main = pl.ds(pl.multiple_of(f * MAIN, MAIN), MAIN)
    base = N_FSDP * MAIN + 8 * lax.shift_right_logical(f, 2)
    tail = pl.ds(pl.multiple_of(base, 8), 8)

    def rows(ref):
        return jnp.concatenate([ref[main, :], ref[tail, :]], axis=0)

    g2_rows = rows(g2_ref)
    d2 = c2 * g2_rows + c3 * mm(g2_rows, g2)
    rest = c1 * rows(d01_ref) + c1 * c1 * d2 + mm(d2, d01)
    x_rows = jnp.concatenate([x_ref[main, :].astype(f32), x_ref[pl.ds(pl.multiple_of(N_FSDP * MAIN + 16 * lax.shift_right_logical(f, 3), 16), 16), :].astype(f32)], axis=0)
    total = s * math.sqrt(max(KVA_ROWS, D))
    moved = mm(rest, x_ref[...])
    out = ((c1 * c1 * c1) * x_rows[:MAIN] + moved[:MAIN]) * total
    o_main = out.astype(bf16)
    q = f & 3
    h = f & 7
    x_tail = x_rows[MAIN : MAIN + 2]
    for j in range(1, 8):
        x_tail = jnp.where(h == j, x_rows[MAIN + 2 * j : MAIN + 2 * j + 2], x_tail)
    m_tail = moved[MAIN : MAIN + 2]
    for j in range(1, 4):
        m_tail = jnp.where(q == j, moved[MAIN + 2 * j : MAIN + 2 * j + 2], m_tail)
    o_tail = tail_tile(((c1 * c1 * c1) * x_tail + m_tail) * total).astype(bf16)
    for r in range(N_DP):
        o_ref[r, :, :CHUNK] = o_main
        o_ref[r, :, CHUNK:] = o_tail


def unpack_body(u_ref, o_ref):
    for d in range(N_DP):
        o_ref[:MAIN, d * CHUNK : (d + 1) * CHUNK] = u_ref[d, :, :CHUNK]
        tail = u_ref[d, :, CHUNK:].astype(f32)
        for k in range(GROUPS):
            piece = slice(d * CHUNK + 128 * k, d * CHUNK + 128 * k + 128)
            o_ref[MAIN:, piece] = tail[2 * k : 2 * k + 2].astype(bf16)


def exchange(x, axis):
    return lax.all_to_all(x, axis, split_axis=0, concat_axis=0, tiled=True)


def total_of(x):
    return jnp.sum(x.astype(f32), axis=0)


def shift(x, axis, n, k):
    return lax.ppermute(x, axis, [(i, (i + k) % n) for i in range(n)])


def others(x, axis, n, step=1):
    return [x] + [shift(x, axis, n, k) for k in range(step, n, step)]


def sum_over(x, axis, n, step=1):
    return pair_sums(others(x, axis, n, step))


def pair_sums(terms):
    terms = [y.astype(f32) for y in terms]
    while len(terms) > 1:
        half = len(terms) // 2
        terms = [terms[k] + terms[k + half] for k in range(half)]
    return terms[0].astype(bf16)


def sum_pair(x, axis, n):
    other = lax.ppermute(x, axis, [(i, i ^ 1) for i in range(n)])
    return (x.astype(f32) + other.astype(f32)).astype(bf16)


def local(kva_parts, kvb_parts, kva_moment, kvb_moment):
    y = lax.axis_index("y").astype(jnp.int32).reshape(1)
    c = lax.axis_index("c").astype(jnp.int32).reshape(1)
    z = lax.axis_index("z").astype(jnp.int32).reshape(1)
    d = y * 2 + c
    rows_b = KV_RANK // N_DP

    half = shape((kvb_parts.shape[1] // 2, KV_RANK), bf16)
    packed, send_b = call(
        pack_body,
        (shape((N_DP, MAIN, WIDE), bf16), half),
        1,
        2,
        [pltpu.VMEM(kva_parts.shape, bf16), pltpu.SemaphoreType.DMA((2,))],
        pl.ANY,
        67_000_000,
    )(c, kva_parts, kvb_parts)
    terms_a = exchange(packed, DP)
    grad_b = call(half_b_body, half, 1, 2)(c, kvb_parts, shift(send_b, "c", 2, 1))
    terms_a, grad_b = lax.optimization_barrier((terms_a, grad_b))
    grads_b = others(grad_b, "y", 4)
    grad_a, push_a = call(
        push_a_body,
        (shape((2 * MAIN, KV_RANK), bf16), shape((8, MAIN, WIDE), bf16)),
        1,
        2,
    )(d, terms_a, kva_moment)
    all_z = exchange(push_a, "z")

    rows = half.shape[0]
    both = call(sum_b_body, shape((rows + 2 * MAIN, KV_RANK), bf16), 0, 5, flops=HINT)(
        *grads_b, grad_a
    )
    both = lax.all_gather(both, "c")
    all_z, both = lax.optimization_barrier((all_z, both))
    all_a = others(all_z, "x", 4)
    moment_b, long_b, piece_b, grad_a = call(
        moment_b_body,
        (
            shape(kvb_moment.shape, f32),
            shape(kvb_moment.shape, bf16),
            shape((rows_b, KV_RANK), bf16),
            shape((2, 2 * MAIN, KV_RANK), bf16),
        ),
        1,
        2,
        [pltpu.VMEM((KV_RANK, KV_RANK), f32)],
    )(d, both, kvb_moment)
    terms_b = others(sum_pair(piece_b, "z", 8), "z", 8, 2)

    grads_a = others(grad_a, "y", 4)
    moment_a = call(moment_a_body, shape(kva_moment.shape, f32), 1, 5)(y, *grads_a, kva_moment)
    all_a[0], moment_a = lax.optimization_barrier((all_a[0], moment_a))

    gram_a, short_a = call(
        gram_a_body,
        (shape((2, 64 * BLOCKS, 384), bf16), shape((KVA_ROWS, CHUNK), bf16)),
        0,
        4,
        [pltpu.VMEM((128 * BLOCKS, 128 * BLOCKS), f32)],
    )(*all_a)
    gram_a = lax.all_gather(gram_a, "c")
    gram_a = lax.dynamic_index_in_dim(gram_a, lax.axis_index("c"), axis=1, keepdims=False)
    gram_a = total_of(gram_a).astype(bf16)
    _, terms_b = lax.optimization_barrier((gram_a, terms_b))
    piece_b = pair_sums(terms_b)
    gram_a = lax.all_gather(sum_over(gram_a, "y", 4), "c")
    piece_b = lax.all_gather(sum_over(piece_b, "x", 4), "c", tiled=True)

    pieces_b = others(piece_b, "y", 4)
    update_a = call(
        finish_a_body,
        shape((N_DP, MAIN, WIDE), bf16),
        1,
        2,
        [pltpu.VMEM((128 * BLOCKS, 128 * BLOCKS), f32)]
        + [pltpu.VMEM((KVA_ROWS, KVA_ROWS), f32)] * 2,
    )(z, gram_a, short_a)
    update_a, pieces_b = lax.optimization_barrier((update_a, pieces_b))
    update_a = call(unpack_body, shape(kva_moment.shape, bf16))(exchange(update_a, DP))
    update_b = call(
        finish_b_body, shape(long_b.shape, bf16), 1, 5, [pltpu.VMEM((KV_RANK, KV_RANK), f32)]
    )(y, *pieces_b, long_b)
    return (moment_a, moment_b, update_a, update_b)


def solution(mesh):
    fine = Mesh(mesh.devices.reshape(4, 2, 4, 8), DP + FSDP)
    return jax.shard_map(
        local,
        mesh=fine,
        in_specs=(P(DP, FSDP, None), P(DP, FSDP, None), P(FSDP, None), P(FSDP, None)),
        out_specs=(P(FSDP, None), P(FSDP, None), P(FSDP, None), P(FSDP, None)),
        check_vma=False,
    )
```

```python
import functools
import math

import jax
import jax.numpy as jnp
from jax import lax
from jax.experimental import pallas as pl
from jax.experimental.pallas import tpu as pltpu
from jax.sharding import Mesh, PartitionSpec as P

D = 7168
KV_RANK = 512
KVA_ROWS = 576
KVB_ROWS = 16384
DP = ("y", "c")
FSDP = ("x", "z")
N_DP = 8
N_FSDP = 32
CHUNK = D // N_DP
GROUPS = CHUNK // 128
MAIN = 16
WIDE = CHUNK + 128
BLOCKS = 5

c1 = 3.4445
c2 = -4.775
c3 = 2.0315
decay_rate = 0.95
norm_epsilon = 1e-07
f32 = jnp.float32
bf16 = jnp.bfloat16
VMEM_LIMIT = 48 * 1024 * 1024
HINT = 40_000_000_000


def call(body, out_shape, n_scalar=0, n_in=1, scratch=(), space=pltpu.VMEM, limit=VMEM_LIMIT, flops=0):
    return pl.pallas_call(
        body,
        out_shape=out_shape,
        in_specs=[pl.BlockSpec(memory_space=pltpu.SMEM)] * n_scalar
        + [pl.BlockSpec(memory_space=space)] * n_in,
        out_specs=jax.tree.map(lambda _: pl.BlockSpec(memory_space=pltpu.VMEM), out_shape),
        scratch_shapes=list(scratch),
        compiler_params=pltpu.CompilerParams(vmem_limit_bytes=limit),
        cost_estimate=pl.CostEstimate(flops=flops, bytes_accessed=0, transcendentals=0)
        if flops
        else None,
    )


def shape(dims, dtype):
    return jax.ShapeDtypeStruct(dims, dtype)


def tail_tile(rows):
    pieces = [rows[:, 128 * k : 128 * k + 128] for k in range(GROUPS)]
    return jnp.concatenate(pieces + [jnp.zeros((2, 128), f32)], axis=0)


def pack_body(c_ref, a_ref, b_ref, o_ref, send_ref, held_ref, sems):
    rows = send_ref.shape[0]
    other = pl.ds(pl.multiple_of((1 - c_ref[0]) * rows, rows), rows)
    copy_a = pltpu.make_async_copy(a_ref, held_ref, sems.at[0])
    copy_b = pltpu.make_async_copy(b_ref.at[0, other], send_ref, sems.at[1])
    copy_a.start()
    copy_b.start()
    copy_a.wait()
    for d in range(N_DP):
        lanes = slice(d * CHUNK, (d + 1) * CHUNK)
        o_ref[d, :, :CHUNK] = held_ref[0, :MAIN, lanes]
        o_ref[d, :, CHUNK:] = tail_tile(held_ref[0, MAIN:, lanes].astype(f32)).astype(bf16)
    copy_b.wait()


def push_a_body(d_ref, parts_ref, m_ref, g_ref, x_ref):
    start = pl.multiple_of(d_ref[0] * CHUNK, 128)
    grad = parts_ref[0].astype(f32)
    for r in range(1, N_DP):
        grad += parts_ref[r].astype(f32)
    g_ref[:MAIN] = grad[:, :KV_RANK].astype(bf16)
    g_ref[MAIN:] = grad[:, KV_RANK:].astype(bf16)
    m_main = m_ref[:MAIN, pl.ds(start, CHUNK)]
    m_tail = tail_tile(m_ref[MAIN:, pl.ds(start, CHUNK)])
    moment = decay_rate * jnp.concatenate([m_main, m_tail], axis=1) + grad
    push = (grad + decay_rate * moment).astype(bf16)
    for r in range(x_ref.shape[0]):
        x_ref[r] = push


def moment_a_body(i_ref, g0_ref, g1_ref, g2_ref, g3_ref, m_ref, o_ref):
    for k, g_ref in enumerate((g0_ref, g1_ref, g2_ref, g3_ref)):
        for c in range(2):
            start = (((i_ref[0] - k) & 3) * 2 + c) * CHUNK
            lanes = pl.ds(pl.multiple_of(start, 128), CHUNK)
            first = KV_RANK // 4 + 2 * MAIN * c
            low = g_ref[first : first + MAIN]
            high = g_ref[first + MAIN : first + 2 * MAIN]
            grad = jnp.concatenate([low, high], axis=1).astype(f32)
            main = grad[:, :CHUNK]
            o_ref[:MAIN, lanes] = decay_rate * m_ref[:MAIN, lanes] + main
            tail = grad[:, CHUNK:]
            for j in range(GROUPS):
                piece = pl.ds(pl.multiple_of(start + 128 * j, 128), 128)
                o_ref[MAIN:, piece] = decay_rate * m_ref[MAIN:, piece] + tail[2 * j : 2 * j + 2]


def half_b_body(c_ref, b_ref, x_ref, o_ref):
    rows = o_ref.shape[0]
    half = b_ref[0, pl.ds(pl.multiple_of(c_ref[0] * rows, rows), rows)]
    o_ref[...] = (half.astype(f32) + x_ref[...].astype(f32)).astype(bf16)


def sum_b_body(b0_ref, b1_ref, b2_ref, b3_ref, g_ref, o_ref):
    rows = b0_ref.shape[0]
    first = b0_ref[...].astype(f32) + b2_ref[...].astype(f32)
    second = b1_ref[...].astype(f32) + b3_ref[...].astype(f32)
    o_ref[:rows] = (first + second).astype(bf16)
    o_ref[rows:] = g_ref[...]


def moment_b_body(d_ref, g_ref, m_ref, o_ref, y_ref, p_ref, a_ref, scratch):
    rows = m_ref.shape[0] // 2
    a_ref[...] = g_ref[:, rows:]
    grad = jnp.concatenate([g_ref[0, :rows], g_ref[1, :rows]], axis=0).astype(f32)
    moment = decay_rate * m_ref[...] + grad
    o_ref[...] = moment
    y = (grad + decay_rate * moment).astype(bf16)
    y_ref[...] = y
    scratch[...] = lax.dot_general(y, y, (((0,), (0,)), ((), ())), preferred_element_type=f32)
    rows = KV_RANK // N_DP
    p_ref[...] = scratch[pl.ds(pl.multiple_of(d_ref[0] * rows, rows), rows), :].astype(bf16)


def gram_a_body(c_ref, x0_ref, x1_ref, x2_ref, x3_ref, own_ref, send_ref, full_ref, gram_ref):
    tails = []
    for k, x_ref in enumerate((x0_ref, x1_ref, x2_ref, x3_ref)):
        full_ref[128 * k : 128 * k + 128] = x_ref[:, :, :CHUNK].reshape(128, CHUNK)
        tails.append(x_ref[:, :, CHUNK:].reshape(128, 128))
    tail = jnp.concatenate(tails, axis=0)
    rows = 2 * N_FSDP
    r = lax.broadcasted_iota(jnp.int32, (rows, N_FSDP * MAIN), 0)
    c = lax.broadcasted_iota(jnp.int32, (rows, N_FSDP * MAIN), 1)
    first = MAIN * lax.shift_right_logical(r, 1) + (r & 1)
    for k in range(GROUPS):
        pick = jnp.where(c == first + 2 * k, 1.0, 0.0).astype(bf16)
        full_ref[N_FSDP * MAIN :, 128 * k : 128 * k + 128] = jnp.dot(
            pick, tail, preferred_element_type=f32
        ).astype(bf16)
    x = full_ref[...]
    gram_ref[...] = jnp.zeros_like(gram_ref)
    gram_ref[:KVA_ROWS, :KVA_ROWS] = lax.dot_general(
        x, x, (((1,), (1,)), ((), ())), preferred_element_type=f32
    )
    for h, o_ref in ((c_ref[0], own_ref), (1 - c_ref[0], send_ref)):
        for i in range(BLOCKS):
            rows = pl.ds(pl.multiple_of(128 * i + 64 * h, 64), 64)
            for j in range(3):
                k = (i + j) % BLOCKS
                o_ref[64 * i : 64 * i + 64, 128 * j : 128 * j + 128] = gram_ref[
                    rows, 128 * k : 128 * k + 128
                ].astype(bf16)


def whole_gram(t_ref, gram_ref):
    for i in range(BLOCKS):
        for j in range(3):
            k = (i + j) % BLOCKS
            block = jnp.concatenate(
                [t_ref[h, 64 * i : 64 * i + 64, 128 * j : 128 * j + 128] for h in range(2)], axis=0
            ).astype(f32)
            gram_ref[128 * i : 128 * i + 128, 128 * k : 128 * k + 128] = block
            if j:
                gram_ref[128 * k : 128 * k + 128, 128 * i : 128 * i + 128] = block.T
    return gram_ref[:KVA_ROWS, :KVA_ROWS]


def mm(a, b):
    return jnp.dot(a.astype(bf16), b.astype(bf16), preferred_element_type=f32)


def gram_scale(gram):
    n = gram.shape[0]
    r = lax.broadcasted_iota(jnp.int32, (n, n), 0)
    c = lax.broadcasted_iota(jnp.int32, (n, n), 1)
    squares = jnp.sum(jnp.where(r == c, gram, 0.0))
    return 1.0 / (jnp.sqrt(squares) + norm_epsilon)


def two_steps(g0):
    d0 = c2 * g0 + c3 * mm(g0, g0)
    t0 = c1 * g0 + mm(d0, g0)
    g1 = c1 * t0 + mm(d0, t0)
    d1 = c2 * g1 + c3 * mm(g1, g1)
    d01 = c1 * (d0 + d1) + mm(d1, d0)
    t1 = c1 * g1 + mm(d1, g1)
    g2 = c1 * t1 + mm(d1, t1)
    return d01, g2


def finish_b_body(i_ref, g0_ref, g1_ref, g2_ref, g3_ref, y_ref, o_ref, gram_ref):
    rows = KV_RANK // 4
    for k, g_ref in enumerate((g0_ref, g1_ref, g2_ref, g3_ref)):
        first = pl.multiple_of(((i_ref[0] - k) & 3) * rows, rows)
        gram_ref[pl.ds(first, rows), :] = g_ref[:rows].astype(f32)
    gram = gram_ref[...]
    s = gram_scale(gram)
    d01, g2 = two_steps(gram * (s * s))
    d2 = c2 * g2 + c3 * mm(g2, g2)
    rest = c1 * d01 + c1 * c1 * d2 + mm(d2, d01)
    y = y_ref[...]
    total = s * math.sqrt(max(KVB_ROWS, KV_RANK))
    out = (c1 * c1 * c1) * y.astype(f32) + mm(y, rest)
    o_ref[...] = (out * total).astype(bf16)


def finish_a_body(f_ref, g_ref, x_ref, o_ref, gram_ref, d01_ref, g2_ref):
    f = f_ref[0]
    gram = whole_gram(g_ref, gram_ref)
    s = gram_scale(gram)
    d01, g2 = two_steps(gram * (s * s))
    d01_ref[...] = d01
    g2_ref[...] = g2
    main = pl.ds(pl.multiple_of(f * MAIN, MAIN), MAIN)
    base = N_FSDP * MAIN + 8 * lax.shift_right_logical(f, 2)
    tail = pl.ds(pl.multiple_of(base, 8), 8)

    def rows(ref):
        return jnp.concatenate([ref[main, :], ref[tail, :]], axis=0)

    g2_rows = rows(g2_ref)
    d2 = c2 * g2_rows + c3 * mm(g2_rows, g2)
    rest = c1 * rows(d01_ref) + c1 * c1 * d2 + mm(d2, d01)
    x_rows = jnp.concatenate([x_ref[main, :].astype(f32), x_ref[pl.ds(pl.multiple_of(N_FSDP * MAIN + 16 * lax.shift_right_logical(f, 3), 16), 16), :].astype(f32)], axis=0)
    total = s * math.sqrt(max(KVA_ROWS, D))
    moved = mm(rest, x_ref[...])
    out = ((c1 * c1 * c1) * x_rows[:MAIN] + moved[:MAIN]) * total
    o_main = out.astype(bf16)
    q = f & 3
    h = f & 7
    x_tail = x_rows[MAIN : MAIN + 2]
    for j in range(1, 8):
        x_tail = jnp.where(h == j, x_rows[MAIN + 2 * j : MAIN + 2 * j + 2], x_tail)
    m_tail = moved[MAIN : MAIN + 2]
    for j in range(1, 4):
        m_tail = jnp.where(q == j, moved[MAIN + 2 * j : MAIN + 2 * j + 2], m_tail)
    o_tail = tail_tile(((c1 * c1 * c1) * x_tail + m_tail) * total).astype(bf16)
    for r in range(N_DP):
        o_ref[r, :, :CHUNK] = o_main
        o_ref[r, :, CHUNK:] = o_tail


def unpack_body(u_ref, o_ref):
    for d in range(N_DP):
        o_ref[:MAIN, d * CHUNK : (d + 1) * CHUNK] = u_ref[d, :, :CHUNK]
        tail = u_ref[d, :, CHUNK:].astype(f32)
        for k in range(GROUPS):
            piece = slice(d * CHUNK + 128 * k, d * CHUNK + 128 * k + 128)
            o_ref[MAIN:, piece] = tail[2 * k : 2 * k + 2].astype(bf16)


def exchange(x, axis):
    return lax.all_to_all(x, axis, split_axis=0, concat_axis=0, tiled=True)


def total_of(x):
    return jnp.sum(x.astype(f32), axis=0)


def shift(x, axis, n, k):
    return lax.ppermute(x, axis, [(i, (i + k) % n) for i in range(n)])


def others(x, axis, n, step=1):
    return [x] + [shift(x, axis, n, k) for k in range(step, n, step)]


def sum_over(x, axis, n, step=1):
    return pair_sums(others(x, axis, n, step))


def pair_sums(terms):
    terms = [y.astype(f32) for y in terms]
    while len(terms) > 1:
        half = len(terms) // 2
        terms = [terms[k] + terms[k + half] for k in range(half)]
    return terms[0].astype(bf16)


def sum_pair(x, axis, n):
    other = lax.ppermute(x, axis, [(i, i ^ 1) for i in range(n)])
    return (x.astype(f32) + other.astype(f32)).astype(bf16)


def local(kva_parts, kvb_parts, kva_moment, kvb_moment):
    y = lax.axis_index("y").astype(jnp.int32).reshape(1)
    c = lax.axis_index("c").astype(jnp.int32).reshape(1)
    z = lax.axis_index("z").astype(jnp.int32).reshape(1)
    d = y * 2 + c
    rows_b = KV_RANK // N_DP

    half = shape((kvb_parts.shape[1] // 2, KV_RANK), bf16)
    packed, send_b = call(
        pack_body,
        (shape((N_DP, MAIN, WIDE), bf16), half),
        1,
        2,
        [pltpu.VMEM(kva_parts.shape, bf16), pltpu.SemaphoreType.DMA((2,))],
        pl.ANY,
        67_000_000,
    )(c, kva_parts, kvb_parts)
    terms_a = exchange(packed, DP)
    grad_b = call(half_b_body, half, 1, 2)(c, kvb_parts, shift(send_b, "c", 2, 1))
    terms_a, grad_b = lax.optimization_barrier((terms_a, grad_b))
    grads_b = others(grad_b, "y", 4)
    grad_a, push_a = call(
        push_a_body,
        (shape((2 * MAIN, KV_RANK), bf16), shape((8, MAIN, WIDE), bf16)),
        1,
        2,
    )(d, terms_a, kva_moment)
    all_z = exchange(push_a, "z")

    rows = half.shape[0]
    both = call(sum_b_body, shape((rows + 2 * MAIN, KV_RANK), bf16), 0, 5, flops=HINT)(
        *grads_b, grad_a
    )
    both = lax.all_gather(both, "c")
    all_z, both = lax.optimization_barrier((all_z, both))
    all_a = others(all_z, "x", 4)
    moment_b, long_b, piece_b, grad_a = call(
        moment_b_body,
        (
            shape(kvb_moment.shape, f32),
            shape(kvb_moment.shape, bf16),
            shape((rows_b, KV_RANK), bf16),
            shape((2, 2 * MAIN, KV_RANK), bf16),
        ),
        1,
        2,
        [pltpu.VMEM((KV_RANK, KV_RANK), f32)],
    )(d, both, kvb_moment)
    terms_b = others(sum_pair(piece_b, "z", 8), "z", 8, 2)

    part = shape((64 * BLOCKS, 384), bf16)
    gram_a, send_a, short_a = call(
        gram_a_body,
        (part, part, shape((KVA_ROWS, CHUNK), bf16)),
        1,
        4,
        [pltpu.VMEM((128 * BLOCKS, 128 * BLOCKS), f32)],
    )(c, *all_a)
    send_a, terms_b = lax.optimization_barrier((send_a, terms_b))
    piece_b = pair_sums(terms_b)
    gram_a = pair_sums([gram_a, shift(send_a, "c", 2, 1)])
    gram_a = lax.all_gather(sum_over(gram_a, "y", 4), "c")
    piece_b = lax.all_gather(sum_over(piece_b, "x", 4), "c", tiled=True)

    pieces_b = others(jnp.concatenate([piece_b, grad_a.reshape(-1, KV_RANK)]), "y", 4)
    update_a = call(
        finish_a_body,
        shape((N_DP, MAIN, WIDE), bf16),
        1,
        2,
        [pltpu.VMEM((128 * BLOCKS, 128 * BLOCKS), f32)]
        + [pltpu.VMEM((KVA_ROWS, KVA_ROWS), f32)] * 2,
    )(z, gram_a, short_a)
    update_a, pieces_b = lax.optimization_barrier((update_a, pieces_b))
    moment_a = call(moment_a_body, shape(kva_moment.shape, f32), 1, 5)(y, *pieces_b, kva_moment)
    update_a = call(unpack_body, shape(kva_moment.shape, bf16))(exchange(update_a, DP))
    update_b = call(
        finish_b_body, shape(long_b.shape, bf16), 1, 5, [pltpu.VMEM((KV_RANK, KV_RANK), f32)]
    )(y, *pieces_b, long_b)
    return (moment_a, moment_b, update_a, update_b)


def solution(mesh):
    fine = Mesh(mesh.devices.reshape(4, 2, 4, 8), DP + FSDP)
    return jax.shard_map(
        local,
        mesh=fine,
        in_specs=(P(DP, FSDP, None), P(DP, FSDP, None), P(FSDP, None), P(FSDP, None)),
        out_specs=(P(FSDP, None), P(FSDP, None), P(FSDP, None), P(FSDP, None)),
        check_vma=False,
    )
```

```python
import functools
import math

import jax
import jax.numpy as jnp
from jax import lax
from jax.experimental import pallas as pl
from jax.experimental.pallas import tpu as pltpu
from jax.sharding import Mesh, PartitionSpec as P

D = 7168
KV_RANK = 512
KVA_ROWS = 576
KVB_ROWS = 16384
DP = ("y", "c")
FSDP = ("x", "z")
N_DP = 8
N_FSDP = 32
CHUNK = D // N_DP
GROUPS = CHUNK // 128
MAIN = 16
WIDE = CHUNK + 128
BLOCKS = 5

c1 = 3.4445
c2 = -4.775
c3 = 2.0315
decay_rate = 0.95
norm_epsilon = 1e-07
f32 = jnp.float32
bf16 = jnp.bfloat16
VMEM_LIMIT = 48 * 1024 * 1024
HINT = 40_000_000_000


def call(body, out_shape, n_scalar=0, n_in=1, scratch=(), space=pltpu.VMEM, limit=VMEM_LIMIT, flops=0):
    return pl.pallas_call(
        body,
        out_shape=out_shape,
        in_specs=[pl.BlockSpec(memory_space=pltpu.SMEM)] * n_scalar
        + [pl.BlockSpec(memory_space=space)] * n_in,
        out_specs=jax.tree.map(lambda _: pl.BlockSpec(memory_space=pltpu.VMEM), out_shape),
        scratch_shapes=list(scratch),
        compiler_params=pltpu.CompilerParams(vmem_limit_bytes=limit),
        cost_estimate=pl.CostEstimate(flops=flops, bytes_accessed=0, transcendentals=0)
        if flops
        else None,
    )


def shape(dims, dtype):
    return jax.ShapeDtypeStruct(dims, dtype)


def tail_tile(rows):
    pieces = [rows[:, 128 * k : 128 * k + 128] for k in range(GROUPS)]
    return jnp.concatenate(pieces + [jnp.zeros((2, 128), f32)], axis=0)


def pack_body(c_ref, a_ref, b_ref, o_ref, send_ref, held_ref, sems):
    rows = send_ref.shape[0]
    other = pl.ds(pl.multiple_of((1 - c_ref[0]) * rows, rows), rows)
    copy_a = pltpu.make_async_copy(a_ref, held_ref, sems.at[0])
    copy_b = pltpu.make_async_copy(b_ref.at[0, other], send_ref, sems.at[1])
    copy_a.start()
    copy_b.start()
    copy_a.wait()
    for d in range(N_DP):
        lanes = slice(d * CHUNK, (d + 1) * CHUNK)
        o_ref[d, :, :CHUNK] = held_ref[0, :MAIN, lanes]
        o_ref[d, :, CHUNK:] = tail_tile(held_ref[0, MAIN:, lanes].astype(f32)).astype(bf16)
    copy_b.wait()


def push_a_body(d_ref, parts_ref, m_ref, g_ref, x_ref):
    start = pl.multiple_of(d_ref[0] * CHUNK, 128)
    grad = parts_ref[0].astype(f32)
    for r in range(1, N_DP):
        grad += parts_ref[r].astype(f32)
    g_ref[:MAIN] = grad[:, :KV_RANK].astype(bf16)
    g_ref[MAIN:] = grad[:, KV_RANK:].astype(bf16)
    m_main = m_ref[:MAIN, pl.ds(start, CHUNK)]
    m_tail = tail_tile(m_ref[MAIN:, pl.ds(start, CHUNK)])
    moment = decay_rate * jnp.concatenate([m_main, m_tail], axis=1) + grad
    push = (grad + decay_rate * moment).astype(bf16)
    for r in range(x_ref.shape[0]):
        x_ref[r] = push


def moment_a_body(i_ref, g0_ref, g1_ref, g2_ref, g3_ref, m_ref, o_ref):
    for k, g_ref in enumerate((g0_ref, g1_ref, g2_ref, g3_ref)):
        for c in range(2):
            start = (((i_ref[0] - k) & 3) * 2 + c) * CHUNK
            lanes = pl.ds(pl.multiple_of(start, 128), CHUNK)
            first = KV_RANK // 4 + 2 * MAIN * c
            low = g_ref[first : first + MAIN]
            high = g_ref[first + MAIN : first + 2 * MAIN]
            grad = jnp.concatenate([low, high], axis=1).astype(f32)
            main = grad[:, :CHUNK]
            o_ref[:MAIN, lanes] = decay_rate * m_ref[:MAIN, lanes] + main
            tail = grad[:, CHUNK:]
            for j in range(GROUPS):
                piece = pl.ds(pl.multiple_of(start + 128 * j, 128), 128)
                o_ref[MAIN:, piece] = decay_rate * m_ref[MAIN:, piece] + tail[2 * j : 2 * j + 2]


def half_b_body(c_ref, b_ref, x_ref, o_ref):
    rows = o_ref.shape[0]
    half = b_ref[0, pl.ds(pl.multiple_of(c_ref[0] * rows, rows), rows)]
    o_ref[...] = (half.astype(f32) + x_ref[...].astype(f32)).astype(bf16)


def sum_b_body(b0_ref, b1_ref, b2_ref, b3_ref, g_ref, o_ref):
    rows = b0_ref.shape[0]
    first = b0_ref[...].astype(f32) + b2_ref[...].astype(f32)
    second = b1_ref[...].astype(f32) + b3_ref[...].astype(f32)
    o_ref[:rows] = (first + second).astype(bf16)
    o_ref[rows:] = g_ref[...]


def moment_b_body(d_ref, g_ref, m_ref, o_ref, y_ref, p_ref, a_ref, scratch):
    rows = m_ref.shape[0] // 2
    a_ref[...] = g_ref[:, rows:]
    grad = jnp.concatenate([g_ref[0, :rows], g_ref[1, :rows]], axis=0).astype(f32)
    moment = decay_rate * m_ref[...] + grad
    o_ref[...] = moment
    y = (grad + decay_rate * moment).astype(bf16)
    y_ref[...] = y
    scratch[...] = lax.dot_general(y, y, (((0,), (0,)), ((), ())), preferred_element_type=f32)
    rows = KV_RANK // N_DP
    p_ref[...] = scratch[pl.ds(pl.multiple_of(d_ref[0] * rows, rows), rows), :].astype(bf16)


def gram_a_body(c_ref, x0_ref, x1_ref, x2_ref, x3_ref, own_ref, send_ref, full_ref, gram_ref):
    tails = []
    for k, x_ref in enumerate((x0_ref, x1_ref, x2_ref, x3_ref)):
        full_ref[128 * k : 128 * k + 128] = x_ref[:, :, :CHUNK].reshape(128, CHUNK)
        tails.append(x_ref[:, :, CHUNK:].reshape(128, 128))
    tail = jnp.concatenate(tails, axis=0)
    rows = 2 * N_FSDP
    r = lax.broadcasted_iota(jnp.int32, (rows, N_FSDP * MAIN), 0)
    c = lax.broadcasted_iota(jnp.int32, (rows, N_FSDP * MAIN), 1)
    first = MAIN * lax.shift_right_logical(r, 1) + (r & 1)
    for k in range(GROUPS):
        pick = jnp.where(c == first + 2 * k, 1.0, 0.0).astype(bf16)
        full_ref[N_FSDP * MAIN :, 128 * k : 128 * k + 128] = jnp.dot(
            pick, tail, preferred_element_type=f32
        ).astype(bf16)
    x = full_ref[...]
    gram_ref[...] = jnp.zeros_like(gram_ref)
    gram_ref[:KVA_ROWS, :KVA_ROWS] = lax.dot_general(
        x, x, (((1,), (1,)), ((), ())), preferred_element_type=f32
    )
    for h, o_ref in ((c_ref[0], own_ref), (1 - c_ref[0], send_ref)):
        for i in range(BLOCKS):
            rows = pl.ds(pl.multiple_of(128 * i + 64 * h, 64), 64)
            for j in range(3):
                k = (i + j) % BLOCKS
                o_ref[64 * i : 64 * i + 64, 128 * j : 128 * j + 128] = gram_ref[
                    rows, 128 * k : 128 * k + 128
                ].astype(bf16)


def whole_gram(t_ref, gram_ref):
    for i in range(BLOCKS):
        for j in range(3):
            k = (i + j) % BLOCKS
            block = jnp.concatenate(
                [t_ref[h, 64 * i : 64 * i + 64, 128 * j : 128 * j + 128] for h in range(2)], axis=0
            ).astype(f32)
            gram_ref[128 * i : 128 * i + 128, 128 * k : 128 * k + 128] = block
            if j:
                gram_ref[128 * k : 128 * k + 128, 128 * i : 128 * i + 128] = block.T
    return gram_ref[:KVA_ROWS, :KVA_ROWS]


def mm(a, b):
    return jnp.dot(a.astype(bf16), b.astype(bf16), preferred_element_type=f32)


def gram_scale(gram):
    n = gram.shape[0]
    r = lax.broadcasted_iota(jnp.int32, (n, n), 0)
    c = lax.broadcasted_iota(jnp.int32, (n, n), 1)
    squares = jnp.sum(jnp.where(r == c, gram, 0.0))
    return 1.0 / (jnp.sqrt(squares) + norm_epsilon)


def two_steps(g0):
    d0 = c2 * g0 + c3 * mm(g0, g0)
    t0 = c1 * g0 + mm(d0, g0)
    g1 = c1 * t0 + mm(d0, t0)
    d1 = c2 * g1 + c3 * mm(g1, g1)
    d01 = c1 * (d0 + d1) + mm(d1, d0)
    t1 = c1 * g1 + mm(d1, g1)
    g2 = c1 * t1 + mm(d1, t1)
    return d01, g2


def finish_b_body(i_ref, g0_ref, g1_ref, g2_ref, g3_ref, y_ref, o_ref, gram_ref):
    rows = KV_RANK // 4
    for k, g_ref in enumerate((g0_ref, g1_ref, g2_ref, g3_ref)):
        first = pl.multiple_of(((i_ref[0] - k) & 3) * rows, rows)
        gram_ref[pl.ds(first, rows), :] = g_ref[:rows].astype(f32)
    gram = gram_ref[...]
    s = gram_scale(gram)
    d01, g2 = two_steps(gram * (s * s))
    d2 = c2 * g2 + c3 * mm(g2, g2)
    rest = c1 * d01 + c1 * c1 * d2 + mm(d2, d01)
    y = y_ref[...]
    total = s * math.sqrt(max(KVB_ROWS, KV_RANK))
    out = (c1 * c1 * c1) * y.astype(f32) + mm(y, rest)
    o_ref[...] = (out * total).astype(bf16)


def finish_a_body(f_ref, g_ref, x_ref, o_ref, gram_ref, d01_ref, g2_ref):
    f = f_ref[0]
    gram = whole_gram(g_ref, gram_ref)
    s = gram_scale(gram)
    d01, g2 = two_steps(gram * (s * s))
    d01_ref[...] = d01
    g2_ref[...] = g2
    main = pl.ds(pl.multiple_of(f * MAIN, MAIN), MAIN)
    base = N_FSDP * MAIN + 8 * lax.shift_right_logical(f, 2)
    tail = pl.ds(pl.multiple_of(base, 8), 8)

    def rows(ref):
        return jnp.concatenate([ref[main, :], ref[tail, :]], axis=0)

    g2_rows = rows(g2_ref)
    d2 = c2 * g2_rows + c3 * mm(g2_rows, g2)
    rest = c1 * rows(d01_ref) + c1 * c1 * d2 + mm(d2, d01)
    x_rows = jnp.concatenate([x_ref[main, :].astype(f32), x_ref[pl.ds(pl.multiple_of(N_FSDP * MAIN + 16 * lax.shift_right_logical(f, 3), 16), 16), :].astype(f32)], axis=0)
    total = s * math.sqrt(max(KVA_ROWS, D))
    moved = mm(rest, x_ref[...])
    out = ((c1 * c1 * c1) * x_rows[:MAIN] + moved[:MAIN]) * total
    o_main = out.astype(bf16)
    q = f & 3
    h = f & 7
    x_tail = x_rows[MAIN : MAIN + 2]
    for j in range(1, 8):
        x_tail = jnp.where(h == j, x_rows[MAIN + 2 * j : MAIN + 2 * j + 2], x_tail)
    m_tail = moved[MAIN : MAIN + 2]
    for j in range(1, 4):
        m_tail = jnp.where(q == j, moved[MAIN + 2 * j : MAIN + 2 * j + 2], m_tail)
    o_tail = tail_tile(((c1 * c1 * c1) * x_tail + m_tail) * total).astype(bf16)
    for r in range(N_DP):
        o_ref[r, :, :CHUNK] = o_main
        o_ref[r, :, CHUNK:] = o_tail


def unpack_body(u_ref, o_ref):
    for d in range(N_DP):
        o_ref[:MAIN, d * CHUNK : (d + 1) * CHUNK] = u_ref[d, :, :CHUNK]
        tail = u_ref[d, :, CHUNK:].astype(f32)
        for k in range(GROUPS):
            piece = slice(d * CHUNK + 128 * k, d * CHUNK + 128 * k + 128)
            o_ref[MAIN:, piece] = tail[2 * k : 2 * k + 2].astype(bf16)


def exchange(x, axis):
    return lax.all_to_all(x, axis, split_axis=0, concat_axis=0, tiled=True)


def total_of(x):
    return jnp.sum(x.astype(f32), axis=0)


def shift(x, axis, n, k):
    return lax.ppermute(x, axis, [(i, (i + k) % n) for i in range(n)])


def others(x, axis, n, step=1):
    return [x] + [shift(x, axis, n, k) for k in range(step, n, step)]


def sum_over(x, axis, n, step=1):
    return pair_sums(others(x, axis, n, step))


def pair_sums(terms):
    terms = [y.astype(f32) for y in terms]
    while len(terms) > 1:
        half = len(terms) // 2
        terms = [terms[k] + terms[k + half] for k in range(half)]
    return terms[0].astype(bf16)


def sum_pair(x, axis, n):
    other = lax.ppermute(x, axis, [(i, i ^ 1) for i in range(n)])
    return (x.astype(f32) + other.astype(f32)).astype(bf16)


def local(kva_parts, kvb_parts, kva_moment, kvb_moment):
    y = lax.axis_index("y").astype(jnp.int32).reshape(1)
    c = lax.axis_index("c").astype(jnp.int32).reshape(1)
    z = lax.axis_index("z").astype(jnp.int32).reshape(1)
    d = y * 2 + c
    rows_b = KV_RANK // N_DP

    half = shape((kvb_parts.shape[1] // 2, KV_RANK), bf16)
    packed, send_b = call(
        pack_body,
        (shape((N_DP, MAIN, WIDE), bf16), half),
        1,
        2,
        [pltpu.VMEM(kva_parts.shape, bf16), pltpu.SemaphoreType.DMA((2,))],
        pl.ANY,
        67_000_000,
    )(c, kva_parts, kvb_parts)
    terms_a = exchange(packed, DP)
    grad_b = call(half_b_body, half, 1, 2)(c, kvb_parts, shift(send_b, "c", 2, 1))
    terms_a, grad_b = lax.optimization_barrier((terms_a, grad_b))
    grads_b = others(grad_b, "y", 4)
    grad_a, push_a = call(
        push_a_body,
        (shape((2 * MAIN, KV_RANK), bf16), shape((8, MAIN, WIDE), bf16)),
        1,
        2,
    )(d, terms_a, kva_moment)
    all_z = exchange(push_a, "z")

    rows = half.shape[0]
    both = call(sum_b_body, shape((rows + 2 * MAIN, KV_RANK), bf16), 0, 5, flops=HINT)(
        *grads_b, grad_a
    )
    both = lax.all_gather(both, "c")
    all_z, both = lax.optimization_barrier((all_z, both))
    all_a = others(all_z, "x", 4)
    moment_b, long_b, piece_b, grad_a = call(
        moment_b_body,
        (
            shape(kvb_moment.shape, f32),
            shape(kvb_moment.shape, bf16),
            shape((rows_b, KV_RANK), bf16),
            shape((2, 2 * MAIN, KV_RANK), bf16),
        ),
        1,
        2,
        [pltpu.VMEM((KV_RANK, KV_RANK), f32)],
    )(d, both, kvb_moment)
    terms_b = others(sum_pair(piece_b, "z", 8), "z", 8, 2)

    part = shape((64 * BLOCKS, 384), bf16)
    gram_a, send_a, short_a = call(
        gram_a_body,
        (part, part, shape((KVA_ROWS, CHUNK), bf16)),
        1,
        4,
        [pltpu.VMEM((128 * BLOCKS, 128 * BLOCKS), f32)],
    )(c, *all_a)
    send_a, terms_b = lax.optimization_barrier((send_a, terms_b))
    piece_b = pair_sums(terms_b)
    gram_a = pair_sums([gram_a, shift(send_a, "c", 2, 1)])
    gram_a = sum_over(gram_a, "y", 4)
    piece_b = lax.all_gather(sum_over(piece_b, "x", 4), "c", tiled=True)

    piece_b = jnp.concatenate([piece_b, grad_a.reshape(-1, KV_RANK)])
    gram_a, piece_b = lax.optimization_barrier((gram_a, piece_b))
    gram_a = lax.all_gather(gram_a, "c")
    pieces_b = others(piece_b, "y", 4)
    update_a = call(
        finish_a_body,
        shape((N_DP, MAIN, WIDE), bf16),
        1,
        2,
        [pltpu.VMEM((128 * BLOCKS, 128 * BLOCKS), f32)]
        + [pltpu.VMEM((KVA_ROWS, KVA_ROWS), f32)] * 2,
    )(z, gram_a, short_a)
    update_a, pieces_b = lax.optimization_barrier((update_a, pieces_b))
    moment_a = call(moment_a_body, shape(kva_moment.shape, f32), 1, 5)(y, *pieces_b, kva_moment)
    update_a = call(unpack_body, shape(kva_moment.shape, bf16))(exchange(update_a, DP))
    update_b = call(
        finish_b_body, shape(long_b.shape, bf16), 1, 5, [pltpu.VMEM((KV_RANK, KV_RANK), f32)]
    )(y, *pieces_b, long_b)
    return (moment_a, moment_b, update_a, update_b)


def solution(mesh):
    fine = Mesh(mesh.devices.reshape(4, 2, 4, 8), DP + FSDP)
    return jax.shard_map(
        local,
        mesh=fine,
        in_specs=(P(DP, FSDP, None), P(DP, FSDP, None), P(FSDP, None), P(FSDP, None)),
        out_specs=(P(FSDP, None), P(FSDP, None), P(FSDP, None), P(FSDP, None)),
        check_vma=False,
    )
```

```python
import functools
import math

import jax
import jax.numpy as jnp
from jax import lax
from jax.experimental import pallas as pl
from jax.experimental.pallas import tpu as pltpu
from jax.sharding import Mesh, PartitionSpec as P

D = 7168
KV_RANK = 512
KVA_ROWS = 576
KVB_ROWS = 16384
DP = ("y", "c")
FSDP = ("x", "z")
N_DP = 8
N_FSDP = 32
CHUNK = D // N_DP
GROUPS = CHUNK // 128
MAIN = 16
WIDE = CHUNK + 128
BLOCKS = 5

c1 = 3.4445
c2 = -4.775
c3 = 2.0315
decay_rate = 0.95
norm_epsilon = 1e-07
f32 = jnp.float32
bf16 = jnp.bfloat16
VMEM_LIMIT = 48 * 1024 * 1024
HINT = 40_000_000_000


def call(body, out_shape, n_scalar=0, n_in=1, scratch=(), space=pltpu.VMEM, limit=VMEM_LIMIT, flops=0):
    return pl.pallas_call(
        body,
        out_shape=out_shape,
        in_specs=[pl.BlockSpec(memory_space=pltpu.SMEM)] * n_scalar
        + [pl.BlockSpec(memory_space=space)] * n_in,
        out_specs=jax.tree.map(lambda _: pl.BlockSpec(memory_space=pltpu.VMEM), out_shape),
        scratch_shapes=list(scratch),
        compiler_params=pltpu.CompilerParams(vmem_limit_bytes=limit),
        cost_estimate=pl.CostEstimate(flops=flops, bytes_accessed=0, transcendentals=0)
        if flops
        else None,
    )


def shape(dims, dtype):
    return jax.ShapeDtypeStruct(dims, dtype)


def tail_tile(rows):
    pieces = [rows[:, 128 * k : 128 * k + 128] for k in range(GROUPS)]
    return jnp.concatenate(pieces + [jnp.zeros((2, 128), f32)], axis=0)


def pack_body(c_ref, a_ref, b_ref, o_ref, send_ref, held_ref, sems):
    rows = send_ref.shape[0]
    other = pl.ds(pl.multiple_of((1 - c_ref[0]) * rows, rows), rows)
    copy_a = pltpu.make_async_copy(a_ref, held_ref, sems.at[0])
    copy_b = pltpu.make_async_copy(b_ref.at[0, other], send_ref, sems.at[1])
    copy_a.start()
    copy_b.start()
    copy_a.wait()
    for d in range(N_DP):
        lanes = slice(d * CHUNK, (d + 1) * CHUNK)
        o_ref[d, :, :CHUNK] = held_ref[0, :MAIN, lanes]
        o_ref[d, :, CHUNK:] = tail_tile(held_ref[0, MAIN:, lanes].astype(f32)).astype(bf16)
    copy_b.wait()


def push_a_body(d_ref, parts_ref, m_ref, g_ref, x_ref):
    start = pl.multiple_of(d_ref[0] * CHUNK, 128)
    grad = parts_ref[0].astype(f32)
    for r in range(1, N_DP):
        grad += parts_ref[r].astype(f32)
    g_ref[:MAIN] = grad[:, :KV_RANK].astype(bf16)
    g_ref[MAIN:] = grad[:, KV_RANK:].astype(bf16)
    m_main = m_ref[:MAIN, pl.ds(start, CHUNK)]
    m_tail = tail_tile(m_ref[MAIN:, pl.ds(start, CHUNK)])
    moment = decay_rate * jnp.concatenate([m_main, m_tail], axis=1) + grad
    push = (grad + decay_rate * moment).astype(bf16)
    for r in range(x_ref.shape[0]):
        x_ref[r] = push


def moment_a_body(i_ref, g0_ref, g1_ref, g2_ref, g3_ref, m_ref, o_ref):
    for k, g_ref in enumerate((g0_ref, g1_ref, g2_ref, g3_ref)):
        for c in range(2):
            start = (((i_ref[0] - k) & 3) * 2 + c) * CHUNK
            lanes = pl.ds(pl.multiple_of(start, 128), CHUNK)
            first = KV_RANK // 4 + 2 * MAIN * c
            low = g_ref[first : first + MAIN]
            high = g_ref[first + MAIN : first + 2 * MAIN]
            grad = jnp.concatenate([low, high], axis=1).astype(f32)
            main = grad[:, :CHUNK]
            o_ref[:MAIN, lanes] = decay_rate * m_ref[:MAIN, lanes] + main
            tail = grad[:, CHUNK:]
            for j in range(GROUPS):
                piece = pl.ds(pl.multiple_of(start + 128 * j, 128), 128)
                o_ref[MAIN:, piece] = decay_rate * m_ref[MAIN:, piece] + tail[2 * j : 2 * j + 2]


def half_b_body(c_ref, b_ref, x_ref, o_ref):
    rows = o_ref.shape[0]
    half = b_ref[0, pl.ds(pl.multiple_of(c_ref[0] * rows, rows), rows)]
    o_ref[...] = (half.astype(f32) + x_ref[...].astype(f32)).astype(bf16)


def sum_b_body(b0_ref, b1_ref, b2_ref, b3_ref, g_ref, o_ref):
    rows = b0_ref.shape[0]
    first = b0_ref[...].astype(f32) + b2_ref[...].astype(f32)
    second = b1_ref[...].astype(f32) + b3_ref[...].astype(f32)
    o_ref[:rows] = (first + second).astype(bf16)
    o_ref[rows:] = g_ref[...]


def moment_b_body(d_ref, g_ref, m_ref, o_ref, y_ref, p_ref, a_ref, scratch):
    rows = m_ref.shape[0] // 2
    a_ref[...] = g_ref[:, rows:]
    grad = jnp.concatenate([g_ref[0, :rows], g_ref[1, :rows]], axis=0).astype(f32)
    moment = decay_rate * m_ref[...] + grad
    o_ref[...] = moment
    y = (grad + decay_rate * moment).astype(bf16)
    y_ref[...] = y
    scratch[...] = lax.dot_general(y, y, (((0,), (0,)), ((), ())), preferred_element_type=f32)
    rows = KV_RANK // N_DP
    p_ref[...] = scratch[pl.ds(pl.multiple_of(d_ref[0] * rows, rows), rows), :].astype(bf16)


def gram_a_body(c_ref, x0_ref, x1_ref, x2_ref, x3_ref, own_ref, send_ref, full_ref, gram_ref):
    tails = []
    for k, x_ref in enumerate((x0_ref, x1_ref, x2_ref, x3_ref)):
        full_ref[128 * k : 128 * k + 128] = x_ref[:, :, :CHUNK].reshape(128, CHUNK)
        tails.append(x_ref[:, :, CHUNK:].reshape(128, 128))
    tail = jnp.concatenate(tails, axis=0)
    rows = 2 * N_FSDP
    r = lax.broadcasted_iota(jnp.int32, (rows, N_FSDP * MAIN), 0)
    c = lax.broadcasted_iota(jnp.int32, (rows, N_FSDP * MAIN), 1)
    first = MAIN * lax.shift_right_logical(r, 1) + (r & 1)
    for k in range(GROUPS):
        pick = jnp.where(c == first + 2 * k, 1.0, 0.0).astype(bf16)
        full_ref[N_FSDP * MAIN :, 128 * k : 128 * k + 128] = jnp.dot(
            pick, tail, preferred_element_type=f32
        ).astype(bf16)
    x = full_ref[...]
    gram_ref[...] = jnp.zeros_like(gram_ref)
    gram_ref[:KVA_ROWS, :KVA_ROWS] = lax.dot_general(
        x, x, (((1,), (1,)), ((), ())), preferred_element_type=f32
    )
    for h, o_ref in ((c_ref[0], own_ref), (1 - c_ref[0], send_ref)):
        for i in range(BLOCKS):
            rows = pl.ds(pl.multiple_of(128 * i + 64 * h, 64), 64)
            for j in range(3):
                k = (i + j) % BLOCKS
                o_ref[64 * i : 64 * i + 64, 128 * j : 128 * j + 128] = gram_ref[
                    rows, 128 * k : 128 * k + 128
                ].astype(bf16)


def whole_gram(t_ref, gram_ref):
    for i in range(BLOCKS):
        for j in range(3):
            k = (i + j) % BLOCKS
            block = jnp.concatenate(
                [t_ref[h, 64 * i : 64 * i + 64, 128 * j : 128 * j + 128] for h in range(2)], axis=0
            ).astype(f32)
            gram_ref[128 * i : 128 * i + 128, 128 * k : 128 * k + 128] = block
            if j:
                gram_ref[128 * k : 128 * k + 128, 128 * i : 128 * i + 128] = block.T
    return gram_ref[:KVA_ROWS, :KVA_ROWS]


def mm(a, b):
    return jnp.dot(a.astype(bf16), b.astype(bf16), preferred_element_type=f32)


def symmetric_mm(a, b):
    a, b = a.astype(bf16), b.astype(bf16)
    cut = a.shape[0] // 256 * 256
    if cut == a.shape[0]:
        return jnp.dot(a, b, preferred_element_type=f32)
    left = jnp.dot(a, b[:, :cut], preferred_element_type=f32)
    corner = jnp.dot(a[cut:], b[:, cut:], preferred_element_type=f32)
    right = jnp.concatenate([left[cut:].T, corner], axis=0)
    return jnp.concatenate([left, right], axis=1)


def gram_scale(gram_ref):
    r = lax.broadcasted_iota(jnp.int32, (128, 128), 0)
    c = lax.broadcasted_iota(jnp.int32, (128, 128), 1)
    total = jnp.zeros((128, 128), f32)
    for i in range(gram_ref.shape[0] // 128):
        total += gram_ref[128 * i : 128 * i + 128, 128 * i : 128 * i + 128]
    squares = jnp.sum(jnp.where(r == c, total, 0.0))
    return 1.0 / (jnp.sqrt(squares) + norm_epsilon)


def two_steps(g0):
    d0 = c2 * g0 + c3 * symmetric_mm(g0, g0)
    t0 = c1 * g0 + symmetric_mm(d0, g0)
    g1 = c1 * t0 + symmetric_mm(d0, t0)
    d1 = c2 * g1 + c3 * symmetric_mm(g1, g1)
    d01 = c1 * (d0 + d1) + symmetric_mm(d1, d0)
    t1 = c1 * g1 + symmetric_mm(d1, g1)
    g2 = c1 * t1 + symmetric_mm(d1, t1)
    return d01, g2


def finish_b_body(i_ref, g0_ref, g1_ref, g2_ref, g3_ref, y_ref, o_ref, gram_ref):
    rows = KV_RANK // 4
    for k, g_ref in enumerate((g0_ref, g1_ref, g2_ref, g3_ref)):
        first = pl.multiple_of(((i_ref[0] - k) & 3) * rows, rows)
        gram_ref[pl.ds(first, rows), :] = g_ref[:rows].astype(f32)
    gram = gram_ref[...]
    s = gram_scale(gram_ref)
    d01, g2 = two_steps(gram * (s * s))
    d2 = c2 * g2 + c3 * mm(g2, g2)
    rest = c1 * d01 + c1 * c1 * d2 + mm(d2, d01)
    y = y_ref[...]
    total = s * math.sqrt(max(KVB_ROWS, KV_RANK))
    out = (c1 * c1 * c1) * y.astype(f32) + mm(y, rest)
    o_ref[...] = (out * total).astype(bf16)


def finish_a_body(
    f_ref, c_ref, own_ref, other_ref, x_ref, o_ref, halves_ref, gram_ref, d01_ref, g2_ref
):
    f = f_ref[0]
    halves_ref[c_ref[0]] = own_ref[...]
    halves_ref[1 - c_ref[0]] = other_ref[...]
    gram = whole_gram(halves_ref, gram_ref)
    s = gram_scale(gram_ref)
    d01, g2 = two_steps(gram * (s * s))
    d01_ref[...] = d01
    g2_ref[...] = g2
    main = pl.ds(pl.multiple_of(f * MAIN, MAIN), MAIN)
    base = N_FSDP * MAIN + 8 * lax.shift_right_logical(f, 2)
    tail = pl.ds(pl.multiple_of(base, 8), 8)

    def rows(ref):
        return jnp.concatenate([ref[main, :], ref[tail, :]], axis=0)

    g2_rows = rows(g2_ref)
    d2 = c2 * g2_rows + c3 * mm(g2_rows, g2)
    rest = c1 * rows(d01_ref) + c1 * c1 * d2 + mm(d2, d01)
    x_rows = jnp.concatenate([x_ref[main, :].astype(f32), x_ref[pl.ds(pl.multiple_of(N_FSDP * MAIN + 16 * lax.shift_right_logical(f, 3), 16), 16), :].astype(f32)], axis=0)
    total = s * math.sqrt(max(KVA_ROWS, D))
    moved = mm(rest, x_ref[...])
    out = ((c1 * c1 * c1) * x_rows[:MAIN] + moved[:MAIN]) * total
    o_main = out.astype(bf16)
    q = f & 3
    h = f & 7
    x_tail = x_rows[MAIN : MAIN + 2]
    for j in range(1, 8):
        x_tail = jnp.where(h == j, x_rows[MAIN + 2 * j : MAIN + 2 * j + 2], x_tail)
    m_tail = moved[MAIN : MAIN + 2]
    for j in range(1, 4):
        m_tail = jnp.where(q == j, moved[MAIN + 2 * j : MAIN + 2 * j + 2], m_tail)
    o_tail = tail_tile(((c1 * c1 * c1) * x_tail + m_tail) * total).astype(bf16)
    for r in range(N_DP):
        o_ref[r, :, :CHUNK] = o_main
        o_ref[r, :, CHUNK:] = o_tail


def unpack_body(u_ref, o_ref):
    for d in range(N_DP):
        o_ref[:MAIN, d * CHUNK : (d + 1) * CHUNK] = u_ref[d, :, :CHUNK]
        tail = u_ref[d, :, CHUNK:].astype(f32)
        for k in range(GROUPS):
            piece = slice(d * CHUNK + 128 * k, d * CHUNK + 128 * k + 128)
            o_ref[MAIN:, piece] = tail[2 * k : 2 * k + 2].astype(bf16)


def exchange(x, axis):
    return lax.all_to_all(x, axis, split_axis=0, concat_axis=0, tiled=True)


def total_of(x):
    return jnp.sum(x.astype(f32), axis=0)


def shift(x, axis, n, k):
    return lax.ppermute(x, axis, [(i, (i + k) % n) for i in range(n)])


def others(x, axis, n, step=1):
    return [x] + [shift(x, axis, n, k) for k in range(step, n, step)]


def sum_over(x, axis, n, step=1):
    return pair_sums(others(x, axis, n, step))


def pair_sums(terms):
    terms = [y.astype(f32) for y in terms]
    while len(terms) > 1:
        half = len(terms) // 2
        terms = [terms[k] + terms[k + half] for k in range(half)]
    return terms[0].astype(bf16)


def sum_pair(x, axis, n):
    other = lax.ppermute(x, axis, [(i, i ^ 1) for i in range(n)])
    return (x.astype(f32) + other.astype(f32)).astype(bf16)


def local(kva_parts, kvb_parts, kva_moment, kvb_moment):
    y = lax.axis_index("y").astype(jnp.int32).reshape(1)
    c = lax.axis_index("c").astype(jnp.int32).reshape(1)
    z = lax.axis_index("z").astype(jnp.int32).reshape(1)
    d = y * 2 + c
    rows_b = KV_RANK // N_DP

    half = shape((kvb_parts.shape[1] // 2, KV_RANK), bf16)
    packed, send_b = call(
        pack_body,
        (shape((N_DP, MAIN, WIDE), bf16), half),
        1,
        2,
        [pltpu.VMEM(kva_parts.shape, bf16), pltpu.SemaphoreType.DMA((2,))],
        pl.ANY,
        67_000_000,
    )(c, kva_parts, kvb_parts)
    terms_a = exchange(packed, DP)
    grad_b = call(half_b_body, half, 1, 2)(c, kvb_parts, shift(send_b, "c", 2, 1))
    terms_a, grad_b = lax.optimization_barrier((terms_a, grad_b))
    grads_b = others(grad_b, "y", 4)
    grad_a, push_a = call(
        push_a_body,
        (shape((2 * MAIN, KV_RANK), bf16), shape((8, MAIN, WIDE), bf16)),
        1,
        2,
    )(d, terms_a, kva_moment)
    all_z = exchange(push_a, "z")

    rows = half.shape[0]
    both = call(sum_b_body, shape((rows + 2 * MAIN, KV_RANK), bf16), 0, 5, flops=HINT)(
        *grads_b, grad_a
    )
    both = lax.all_gather(both, "c")
    all_z, both = lax.optimization_barrier((all_z, both))
    all_a = others(all_z, "x", 4)
    moment_b, long_b, piece_b, grad_a = call(
        moment_b_body,
        (
            shape(kvb_moment.shape, f32),
            shape(kvb_moment.shape, bf16),
            shape((rows_b, KV_RANK), bf16),
            shape((2, 2 * MAIN, KV_RANK), bf16),
        ),
        1,
        2,
        [pltpu.VMEM((KV_RANK, KV_RANK), f32)],
    )(d, both, kvb_moment)
    terms_b = others(sum_pair(piece_b, "z", 8), "z", 8, 2)

    part = shape((64 * BLOCKS, 384), bf16)
    gram_a, send_a, short_a = call(
        gram_a_body,
        (part, part, shape((KVA_ROWS, CHUNK), bf16)),
        1,
        4,
        [pltpu.VMEM((128 * BLOCKS, 128 * BLOCKS), f32)],
    )(c, *all_a)
    send_a, terms_b = lax.optimization_barrier((send_a, terms_b))
    piece_b = pair_sums(terms_b)
    gram_a = pair_sums([gram_a, shift(send_a, "c", 2, 1)])
    gram_a = sum_over(gram_a, "y", 4)
    piece_b = lax.all_gather(sum_over(piece_b, "x", 4), "c", tiled=True)

    piece_b = jnp.concatenate([piece_b, grad_a.reshape(-1, KV_RANK)])
    gram_a, piece_b = lax.optimization_barrier((gram_a, piece_b))
    other_a = shift(gram_a, "c", 2, 1)
    pieces_b = others(piece_b, "y", 4)
    update_a = call(
        finish_a_body,
        shape((N_DP, MAIN, WIDE), bf16),
        2,
        3,
        [pltpu.VMEM((2,) + part.shape, bf16), pltpu.VMEM((128 * BLOCKS, 128 * BLOCKS), f32)]
        + [pltpu.VMEM((KVA_ROWS, KVA_ROWS), f32)] * 2,
    )(z, c, gram_a, other_a, short_a)
    update_a, pieces_b = lax.optimization_barrier((update_a, pieces_b))
    moment_a = call(moment_a_body, shape(kva_moment.shape, f32), 1, 5)(y, *pieces_b, kva_moment)
    update_a = call(unpack_body, shape(kva_moment.shape, bf16))(exchange(update_a, DP))
    update_b = call(
        finish_b_body, shape(long_b.shape, bf16), 1, 5, [pltpu.VMEM((KV_RANK, KV_RANK), f32)]
    )(y, *pieces_b, long_b)
    return (moment_a, moment_b, update_a, update_b)


def solution(mesh):
    fine = Mesh(mesh.devices.reshape(4, 2, 4, 8), DP + FSDP)
    return jax.shard_map(
        local,
        mesh=fine,
        in_specs=(P(DP, FSDP, None), P(DP, FSDP, None), P(FSDP, None), P(FSDP, None)),
        out_specs=(P(FSDP, None), P(FSDP, None), P(FSDP, None), P(FSDP, None)),
        check_vma=False,
    )
```

```python
import functools
import math

import jax
import jax.numpy as jnp
from jax import lax
from jax.experimental import pallas as pl
from jax.experimental.pallas import tpu as pltpu
from jax.sharding import Mesh, PartitionSpec as P

D = 7168
KV_RANK = 512
KVA_ROWS = 576
KVB_ROWS = 16384
DP = ("y", "c")
FSDP = ("x", "z")
N_DP = 8
N_FSDP = 32
CHUNK = D // N_DP
GROUPS = CHUNK // 128
MAIN = 16
WIDE = CHUNK + 128
BLOCKS = 5

c1 = 3.4445
c2 = -4.775
c3 = 2.0315
decay_rate = 0.95
norm_epsilon = 1e-07
f32 = jnp.float32
bf16 = jnp.bfloat16
VMEM_LIMIT = 48 * 1024 * 1024
HINT = 40_000_000_000


def call(body, out_shape, n_scalar=0, n_in=1, scratch=(), space=pltpu.VMEM, limit=VMEM_LIMIT, flops=0):
    return pl.pallas_call(
        body,
        out_shape=out_shape,
        in_specs=[pl.BlockSpec(memory_space=pltpu.SMEM)] * n_scalar
        + [pl.BlockSpec(memory_space=space)] * n_in,
        out_specs=jax.tree.map(lambda _: pl.BlockSpec(memory_space=pltpu.VMEM), out_shape),
        scratch_shapes=list(scratch),
        compiler_params=pltpu.CompilerParams(vmem_limit_bytes=limit),
        cost_estimate=pl.CostEstimate(flops=flops, bytes_accessed=0, transcendentals=0)
        if flops
        else None,
    )


def shape(dims, dtype):
    return jax.ShapeDtypeStruct(dims, dtype)


def tail_tile(rows):
    pieces = [rows[:, 128 * k : 128 * k + 128] for k in range(GROUPS)]
    return jnp.concatenate(pieces + [jnp.zeros((2, 128), f32)], axis=0)


def pack_body(c_ref, a_ref, b_ref, o_ref, send_ref, held_ref, sems):
    rows = send_ref.shape[0]
    other = pl.ds(pl.multiple_of((1 - c_ref[0]) * rows, rows), rows)
    copy_a = pltpu.make_async_copy(a_ref, held_ref, sems.at[0])
    copy_b = pltpu.make_async_copy(b_ref.at[0, other], send_ref, sems.at[1])
    copy_a.start()
    copy_b.start()
    copy_a.wait()
    for d in range(N_DP):
        lanes = slice(d * CHUNK, (d + 1) * CHUNK)
        o_ref[d, :, :CHUNK] = held_ref[0, :MAIN, lanes]
        o_ref[d, :, CHUNK:] = tail_tile(held_ref[0, MAIN:, lanes].astype(f32)).astype(bf16)
    copy_b.wait()


def push_a_body(d_ref, parts_ref, m_ref, g_ref, x_ref):
    start = pl.multiple_of(d_ref[0] * CHUNK, 128)
    grad = parts_ref[0].astype(f32)
    for r in range(1, N_DP):
        grad += parts_ref[r].astype(f32)
    g_ref[:MAIN] = grad[:, :KV_RANK].astype(bf16)
    g_ref[MAIN:] = grad[:, KV_RANK:].astype(bf16)
    m_main = m_ref[:MAIN, pl.ds(start, CHUNK)]
    m_tail = tail_tile(m_ref[MAIN:, pl.ds(start, CHUNK)])
    moment = decay_rate * jnp.concatenate([m_main, m_tail], axis=1) + grad
    push = (grad + decay_rate * moment).astype(bf16)
    for r in range(x_ref.shape[0]):
        x_ref[r] = push


def moment_a_body(i_ref, g0_ref, g1_ref, g2_ref, g3_ref, m_ref, o_ref):
    for k, g_ref in enumerate((g0_ref, g1_ref, g2_ref, g3_ref)):
        for c in range(2):
            start = (((i_ref[0] - k) & 3) * 2 + c) * CHUNK
            lanes = pl.ds(pl.multiple_of(start, 128), CHUNK)
            first = KV_RANK // 4 + 2 * MAIN * c
            low = g_ref[first : first + MAIN]
            high = g_ref[first + MAIN : first + 2 * MAIN]
            grad = jnp.concatenate([low, high], axis=1).astype(f32)
            main = grad[:, :CHUNK]
            o_ref[:MAIN, lanes] = decay_rate * m_ref[:MAIN, lanes] + main
            tail = grad[:, CHUNK:]
            for j in range(GROUPS):
                piece = pl.ds(pl.multiple_of(start + 128 * j, 128), 128)
                o_ref[MAIN:, piece] = decay_rate * m_ref[MAIN:, piece] + tail[2 * j : 2 * j + 2]


def half_b_body(c_ref, b_ref, x_ref, o_ref):
    rows = o_ref.shape[0]
    half = b_ref[0, pl.ds(pl.multiple_of(c_ref[0] * rows, rows), rows)]
    o_ref[...] = (half.astype(f32) + x_ref[...].astype(f32)).astype(bf16)


def sum_b_body(b0_ref, b1_ref, b2_ref, b3_ref, g_ref, o_ref):
    rows = b0_ref.shape[0]
    first = b0_ref[...].astype(f32) + b2_ref[...].astype(f32)
    second = b1_ref[...].astype(f32) + b3_ref[...].astype(f32)
    o_ref[:rows] = (first + second).astype(bf16)
    o_ref[rows:] = g_ref[...]


def moment_b_body(d_ref, g_ref, m_ref, o_ref, y_ref, p_ref, a_ref, scratch):
    rows = m_ref.shape[0] // 2
    a_ref[...] = g_ref[:, rows:]
    grad = jnp.concatenate([g_ref[0, :rows], g_ref[1, :rows]], axis=0).astype(f32)
    moment = decay_rate * m_ref[...] + grad
    o_ref[...] = moment
    y = (grad + decay_rate * moment).astype(bf16)
    y_ref[...] = y
    scratch[...] = lax.dot_general(y, y, (((0,), (0,)), ((), ())), preferred_element_type=f32)
    rows = KV_RANK // N_DP
    p_ref[...] = scratch[pl.ds(pl.multiple_of(d_ref[0] * rows, rows), rows), :].astype(bf16)


def gram_a_body(c_ref, x0_ref, x1_ref, x2_ref, x3_ref, own_ref, send_ref, full_ref, gram_ref):
    tails = []
    for k, x_ref in enumerate((x0_ref, x1_ref, x2_ref, x3_ref)):
        full_ref[128 * k : 128 * k + 128] = x_ref[:, :, :CHUNK].reshape(128, CHUNK)
        tails.append(x_ref[:, :, CHUNK:].reshape(128, 128))
    tail = jnp.concatenate(tails, axis=0)
    rows = 2 * N_FSDP
    r = lax.broadcasted_iota(jnp.int32, (rows, N_FSDP * MAIN), 0)
    c = lax.broadcasted_iota(jnp.int32, (rows, N_FSDP * MAIN), 1)
    first = MAIN * lax.shift_right_logical(r, 1) + (r & 1)
    for k in range(GROUPS):
        pick = jnp.where(c == first + 2 * k, 1.0, 0.0).astype(bf16)
        full_ref[N_FSDP * MAIN :, 128 * k : 128 * k + 128] = jnp.dot(
            pick, tail, preferred_element_type=f32
        ).astype(bf16)
    x = full_ref[...]
    gram_ref[...] = jnp.zeros_like(gram_ref)
    gram_ref[:KVA_ROWS, :KVA_ROWS] = lax.dot_general(
        x, x, (((1,), (1,)), ((), ())), preferred_element_type=f32
    )
    for h, o_ref in ((c_ref[0], own_ref), (1 - c_ref[0], send_ref)):
        for i in range(BLOCKS):
            rows = pl.ds(pl.multiple_of(128 * i + 64 * h, 64), 64)
            for j in range(3):
                k = (i + j) % BLOCKS
                o_ref[64 * i : 64 * i + 64, 128 * j : 128 * j + 128] = gram_ref[
                    rows, 128 * k : 128 * k + 128
                ].astype(bf16)


def whole_gram(t_ref, gram_ref):
    for i in range(BLOCKS):
        for j in range(3):
            k = (i + j) % BLOCKS
            block = jnp.concatenate(
                [t_ref[h, 64 * i : 64 * i + 64, 128 * j : 128 * j + 128] for h in range(2)], axis=0
            ).astype(f32)
            gram_ref[128 * i : 128 * i + 128, 128 * k : 128 * k + 128] = block
            if j:
                gram_ref[128 * k : 128 * k + 128, 128 * i : 128 * i + 128] = block.T
    return gram_ref[:KVA_ROWS, :KVA_ROWS]


def mm(a, b):
    return jnp.dot(a.astype(bf16), b.astype(bf16), preferred_element_type=f32)


def symmetric_mm(a, b):
    a, b = a.astype(bf16), b.astype(bf16)
    cut = a.shape[0] // 256 * 256
    if cut == a.shape[0]:
        return jnp.dot(a, b, preferred_element_type=f32)
    left = jnp.dot(a, b[:, :cut], preferred_element_type=f32)
    corner = jnp.dot(a[cut:], b[:, cut:], preferred_element_type=f32)
    right = jnp.concatenate([left[cut:].T, corner], axis=0)
    return jnp.concatenate([left, right], axis=1)


def gram_scale(gram_ref):
    r = lax.broadcasted_iota(jnp.int32, (128, 128), 0)
    c = lax.broadcasted_iota(jnp.int32, (128, 128), 1)
    total = jnp.zeros((128, 128), f32)
    for i in range(gram_ref.shape[0] // 128):
        total += gram_ref[128 * i : 128 * i + 128, 128 * i : 128 * i + 128]
    squares = jnp.sum(jnp.where(r == c, total, 0.0))
    return 1.0 / (jnp.sqrt(squares) + norm_epsilon)


def two_steps(g0):
    d0 = c2 * g0 + c3 * symmetric_mm(g0, g0)
    t0 = c1 * g0 + symmetric_mm(d0, g0)
    g1 = c1 * t0 + symmetric_mm(d0, t0)
    d1 = c2 * g1 + c3 * symmetric_mm(g1, g1)
    d01 = c1 * (d0 + d1) + symmetric_mm(d1, d0)
    t1 = c1 * g1 + symmetric_mm(d1, g1)
    g2 = c1 * t1 + symmetric_mm(d1, t1)
    return d01, g2


def finish_b_body(i_ref, g0_ref, g1_ref, g2_ref, g3_ref, y_ref, o_ref, gram_ref):
    rows = KV_RANK // 4
    for k, g_ref in enumerate((g0_ref, g1_ref, g2_ref, g3_ref)):
        first = pl.multiple_of(((i_ref[0] - k) & 3) * rows, rows)
        gram_ref[pl.ds(first, rows), :] = g_ref[:rows].astype(f32)
    gram = gram_ref[...]
    s = gram_scale(gram_ref)
    d01, g2 = two_steps(gram * (s * s))
    d2 = c2 * g2 + c3 * mm(g2, g2)
    rest = c1 * d01 + c1 * c1 * d2 + mm(d2, d01)
    y = y_ref[...]
    total = s * math.sqrt(max(KVB_ROWS, KV_RANK))
    out = (c1 * c1 * c1) * y.astype(f32) + mm(y, rest)
    o_ref[...] = (out * total).astype(bf16)


def finish_a_body(
    f_ref, c_ref, own_ref, other_ref, x_ref, o_ref, halves_ref, gram_ref, d01_ref, g2_ref
):
    f = f_ref[0]
    halves_ref[c_ref[0]] = own_ref[...]
    halves_ref[1 - c_ref[0]] = other_ref[...]
    gram = whole_gram(halves_ref, gram_ref)
    s = gram_scale(gram_ref)
    d01, g2 = two_steps(gram * (s * s))
    d01_ref[...] = d01
    g2_ref[...] = g2
    main = pl.ds(pl.multiple_of(f * MAIN, MAIN), MAIN)
    base = N_FSDP * MAIN + 8 * lax.shift_right_logical(f, 2)
    tail = pl.ds(pl.multiple_of(base, 8), 8)

    def rows(ref):
        return jnp.concatenate([ref[main, :], ref[tail, :]], axis=0)

    g2_rows = rows(g2_ref)
    d2 = c2 * g2_rows + c3 * mm(g2_rows, g2)
    rest = c1 * rows(d01_ref) + c1 * c1 * d2 + mm(d2, d01)
    x_rows = jnp.concatenate([x_ref[main, :].astype(f32), x_ref[pl.ds(pl.multiple_of(N_FSDP * MAIN + 16 * lax.shift_right_logical(f, 3), 16), 16), :].astype(f32)], axis=0)
    total = s * math.sqrt(max(KVA_ROWS, D))
    moved = mm(rest, x_ref[...])
    out = ((c1 * c1 * c1) * x_rows[:MAIN] + moved[:MAIN]) * total
    o_main = out.astype(bf16)
    q = f & 3
    h = f & 7
    x_tail = x_rows[MAIN : MAIN + 2]
    for j in range(1, 8):
        x_tail = jnp.where(h == j, x_rows[MAIN + 2 * j : MAIN + 2 * j + 2], x_tail)
    m_tail = moved[MAIN : MAIN + 2]
    for j in range(1, 4):
        m_tail = jnp.where(q == j, moved[MAIN + 2 * j : MAIN + 2 * j + 2], m_tail)
    o_tail = tail_tile(((c1 * c1 * c1) * x_tail + m_tail) * total).astype(bf16)
    for r in range(N_DP):
        o_ref[r, :, :CHUNK] = o_main
        o_ref[r, :, CHUNK:] = o_tail


def unpack_body(u_ref, o_ref):
    for d in range(N_DP):
        o_ref[:MAIN, d * CHUNK : (d + 1) * CHUNK] = u_ref[d, :, :CHUNK]
        tail = u_ref[d, :, CHUNK:].astype(f32)
        for k in range(GROUPS):
            piece = slice(d * CHUNK + 128 * k, d * CHUNK + 128 * k + 128)
            o_ref[MAIN:, piece] = tail[2 * k : 2 * k + 2].astype(bf16)


def exchange(x, axis):
    return lax.all_to_all(x, axis, split_axis=0, concat_axis=0, tiled=True)


def total_of(x):
    return jnp.sum(x.astype(f32), axis=0)


def shift(x, axis, n, k):
    return lax.ppermute(x, axis, [(i, (i + k) % n) for i in range(n)])


def others(x, axis, n, step=1):
    return [x] + [shift(x, axis, n, k) for k in range(step, n, step)]


def sum_over(x, axis, n, step=1):
    return pair_sums(others(x, axis, n, step))


def pair_sums(terms):
    terms = [y.astype(f32) for y in terms]
    while len(terms) > 1:
        half = len(terms) // 2
        terms = [terms[k] + terms[k + half] for k in range(half)]
    return terms[0].astype(bf16)


def sum_pair(x, axis, n):
    other = lax.ppermute(x, axis, [(i, i ^ 1) for i in range(n)])
    return (x.astype(f32) + other.astype(f32)).astype(bf16)


def local(kva_parts, kvb_parts, kva_moment, kvb_moment):
    y = lax.axis_index("y").astype(jnp.int32).reshape(1)
    c = lax.axis_index("c").astype(jnp.int32).reshape(1)
    z = lax.axis_index("z").astype(jnp.int32).reshape(1)
    d = y * 2 + c
    rows_b = KV_RANK // N_DP

    half = shape((kvb_parts.shape[1] // 2, KV_RANK), bf16)
    packed, send_b = call(
        pack_body,
        (shape((N_DP, MAIN, WIDE), bf16), half),
        1,
        2,
        [pltpu.VMEM(kva_parts.shape, bf16), pltpu.SemaphoreType.DMA((2,))],
        pl.ANY,
        67_000_000,
    )(c, kva_parts, kvb_parts)
    terms_a = exchange(packed, DP)
    grad_b = call(half_b_body, half, 1, 2)(c, kvb_parts, shift(send_b, "c", 2, 1))
    terms_a, grad_b = lax.optimization_barrier((terms_a, grad_b))
    grads_b = others(grad_b, "y", 4)
    grad_a, push_a = call(
        push_a_body,
        (shape((2 * MAIN, KV_RANK), bf16), shape((8, MAIN, WIDE), bf16)),
        1,
        2,
    )(d, terms_a, kva_moment)
    all_z = exchange(push_a, "z")

    rows = half.shape[0]
    both = call(sum_b_body, shape((rows + 2 * MAIN, KV_RANK), bf16), 0, 5, flops=HINT)(
        *grads_b, grad_a
    )
    both = lax.all_gather(both, "c")
    all_z, both = lax.optimization_barrier((all_z, both))
    all_a = others(all_z, "x", 4)
    moment_b, long_b, piece_b, grad_a = call(
        moment_b_body,
        (
            shape(kvb_moment.shape, f32),
            shape(kvb_moment.shape, bf16),
            shape((rows_b, KV_RANK), bf16),
            shape((2, 2 * MAIN, KV_RANK), bf16),
        ),
        1,
        2,
        [pltpu.VMEM((KV_RANK, KV_RANK), f32)],
    )(d, both, kvb_moment)
    terms_b = others(sum_pair(piece_b, "z", 8), "z", 8, 2)

    part = shape((64 * BLOCKS, 384), bf16)
    gram_a, send_a, short_a = call(
        gram_a_body,
        (part, part, shape((KVA_ROWS, CHUNK), bf16)),
        1,
        4,
        [pltpu.VMEM((128 * BLOCKS, 128 * BLOCKS), f32)],
    )(c, *all_a)
    send_a, terms_b = lax.optimization_barrier((send_a, terms_b))
    piece_b = pair_sums(terms_b)
    gram_a = pair_sums([gram_a, shift(send_a, "c", 2, 1)])
    gram_a = sum_over(gram_a, "y", 4)
    piece_b = lax.all_gather(sum_over(piece_b, "x", 4), "c", tiled=True)

    piece_b = jnp.concatenate([piece_b, grad_a.reshape(-1, KV_RANK)])
    gram_a, piece_b = lax.optimization_barrier((gram_a, piece_b))
    other_a = shift(gram_a, "c", 2, 1)
    pieces_b = others(piece_b, "y", 4)
    update_a = call(
        finish_a_body,
        shape((N_DP, MAIN, WIDE), bf16),
        2,
        3,
        [pltpu.VMEM((2,) + part.shape, bf16), pltpu.VMEM((128 * BLOCKS, 128 * BLOCKS), f32)]
        + [pltpu.VMEM((KVA_ROWS, KVA_ROWS), f32)] * 2,
        flops=HINT,
    )(z, c, gram_a, other_a, short_a)
    moment_a = call(moment_a_body, shape(kva_moment.shape, f32), 1, 5)(y, *pieces_b, kva_moment)
    update_a = call(unpack_body, shape(kva_moment.shape, bf16))(exchange(update_a, DP))
    update_b = call(
        finish_b_body,
        shape(long_b.shape, bf16),
        1,
        5,
        [pltpu.VMEM((KV_RANK, KV_RANK), f32)],
        flops=HINT,
    )(y, *pieces_b, long_b)
    return (moment_a, moment_b, update_a, update_b)


def solution(mesh):
    fine = Mesh(mesh.devices.reshape(4, 2, 4, 8), DP + FSDP)
    return jax.shard_map(
        local,
        mesh=fine,
        in_specs=(P(DP, FSDP, None), P(DP, FSDP, None), P(FSDP, None), P(FSDP, None)),
        out_specs=(P(FSDP, None), P(FSDP, None), P(FSDP, None), P(FSDP, None)),
        check_vma=False,
    )
```

```python
import functools
import math

import jax
import jax.numpy as jnp
from jax import lax
from jax.experimental import pallas as pl
from jax.experimental.pallas import tpu as pltpu
from jax.sharding import Mesh, PartitionSpec as P

D = 7168
KV_RANK = 512
KVA_ROWS = 576
KVB_ROWS = 16384
DP = ("y", "c")
FSDP = ("x", "z")
N_DP = 8
N_FSDP = 32
CHUNK = D // N_DP
GROUPS = CHUNK // 128
MAIN = 16
WIDE = CHUNK + 128
BLOCKS = 5

c1 = 3.4445
c2 = -4.775
c3 = 2.0315
decay_rate = 0.95
norm_epsilon = 1e-07
f32 = jnp.float32
bf16 = jnp.bfloat16
VMEM_LIMIT = 48 * 1024 * 1024
HINT = 40_000_000_000


def call(body, out_shape, n_scalar=0, n_in=1, scratch=(), space=pltpu.VMEM, limit=VMEM_LIMIT, flops=0):
    return pl.pallas_call(
        body,
        out_shape=out_shape,
        in_specs=[pl.BlockSpec(memory_space=pltpu.SMEM)] * n_scalar
        + [pl.BlockSpec(memory_space=space)] * n_in,
        out_specs=jax.tree.map(lambda _: pl.BlockSpec(memory_space=pltpu.VMEM), out_shape),
        scratch_shapes=list(scratch),
        compiler_params=pltpu.CompilerParams(vmem_limit_bytes=limit),
        cost_estimate=pl.CostEstimate(flops=flops, bytes_accessed=0, transcendentals=0)
        if flops
        else None,
    )


def shape(dims, dtype):
    return jax.ShapeDtypeStruct(dims, dtype)


def tail_tile(rows):
    pieces = [rows[:, 128 * k : 128 * k + 128] for k in range(GROUPS)]
    return jnp.concatenate(pieces + [jnp.zeros((2, 128), f32)], axis=0)


def pack_body(c_ref, a_ref, b_ref, o_ref, send_ref, held_ref, sems):
    rows = send_ref.shape[0]
    other = pl.ds(pl.multiple_of((1 - c_ref[0]) * rows, rows), rows)
    copy_a = pltpu.make_async_copy(a_ref, held_ref, sems.at[0])
    copy_b = pltpu.make_async_copy(b_ref.at[0, other], send_ref, sems.at[1])
    copy_a.start()
    copy_b.start()
    copy_a.wait()
    for d in range(N_DP):
        lanes = slice(d * CHUNK, (d + 1) * CHUNK)
        o_ref[d, :, :CHUNK] = held_ref[0, :MAIN, lanes]
        o_ref[d, :, CHUNK:] = tail_tile(held_ref[0, MAIN:, lanes].astype(f32)).astype(bf16)
    copy_b.wait()


def push_a_body(d_ref, parts_ref, m_ref, g_ref, x_ref):
    start = pl.multiple_of(d_ref[0] * CHUNK, 128)
    grad = parts_ref[0].astype(f32)
    for r in range(1, N_DP):
        grad += parts_ref[r].astype(f32)
    g_ref[:MAIN] = grad[:, :KV_RANK].astype(bf16)
    g_ref[MAIN:] = grad[:, KV_RANK:].astype(bf16)
    m_main = m_ref[:MAIN, pl.ds(start, CHUNK)]
    m_tail = tail_tile(m_ref[MAIN:, pl.ds(start, CHUNK)])
    moment = decay_rate * jnp.concatenate([m_main, m_tail], axis=1) + grad
    push = (grad + decay_rate * moment).astype(bf16)
    for r in range(x_ref.shape[0]):
        x_ref[r] = push


def moment_a_body(i_ref, g0_ref, g1_ref, g2_ref, g3_ref, m_ref, o_ref):
    for k, g_ref in enumerate((g0_ref, g1_ref, g2_ref, g3_ref)):
        for c in range(2):
            start = (((i_ref[0] + k) & 3) * 2 + c) * CHUNK
            lanes = pl.ds(pl.multiple_of(start, 128), CHUNK)
            first = KV_RANK // 4 + 2 * MAIN * c
            low = g_ref[first : first + MAIN]
            high = g_ref[first + MAIN : first + 2 * MAIN]
            grad = jnp.concatenate([low, high], axis=1).astype(f32)
            main = grad[:, :CHUNK]
            o_ref[:MAIN, lanes] = decay_rate * m_ref[:MAIN, lanes] + main
            tail = grad[:, CHUNK:]
            for j in range(GROUPS):
                piece = pl.ds(pl.multiple_of(start + 128 * j, 128), 128)
                o_ref[MAIN:, piece] = decay_rate * m_ref[MAIN:, piece] + tail[2 * j : 2 * j + 2]


def half_b_body(c_ref, b_ref, x_ref, o_ref):
    rows = o_ref.shape[0]
    half = b_ref[0, pl.ds(pl.multiple_of(c_ref[0] * rows, rows), rows)]
    o_ref[...] = (half.astype(f32) + x_ref[...].astype(f32)).astype(bf16)


def sum_b_body(b0_ref, b1_ref, b2_ref, b3_ref, g_ref, o_ref):
    rows = b0_ref.shape[0]
    first = b0_ref[...].astype(f32) + b2_ref[...].astype(f32)
    second = b1_ref[...].astype(f32) + b3_ref[...].astype(f32)
    o_ref[:rows] = (first + second).astype(bf16)
    o_ref[rows:] = g_ref[...]


def moment_b_body(d_ref, g_ref, m_ref, o_ref, y_ref, p_ref, a_ref, scratch):
    rows = m_ref.shape[0] // 2
    a_ref[...] = g_ref[:, rows:]
    grad = jnp.concatenate([g_ref[0, :rows], g_ref[1, :rows]], axis=0).astype(f32)
    moment = decay_rate * m_ref[...] + grad
    o_ref[...] = moment
    y = (grad + decay_rate * moment).astype(bf16)
    y_ref[...] = y
    scratch[...] = lax.dot_general(y, y, (((0,), (0,)), ((), ())), preferred_element_type=f32)
    rows = KV_RANK // N_DP
    p_ref[...] = scratch[pl.ds(pl.multiple_of(d_ref[0] * rows, rows), rows), :].astype(bf16)


def gram_a_body(c_ref, x0_ref, x1_ref, x2_ref, x3_ref, own_ref, send_ref, full_ref, gram_ref):
    tails = []
    for k, x_ref in enumerate((x0_ref, x1_ref, x2_ref, x3_ref)):
        full_ref[128 * k : 128 * k + 128] = x_ref[:, :, :CHUNK].reshape(128, CHUNK)
        tails.append(x_ref[:, :, CHUNK:].reshape(128, 128))
    tail = jnp.concatenate(tails, axis=0)
    rows = 2 * N_FSDP
    r = lax.broadcasted_iota(jnp.int32, (rows, N_FSDP * MAIN), 0)
    c = lax.broadcasted_iota(jnp.int32, (rows, N_FSDP * MAIN), 1)
    first = MAIN * lax.shift_right_logical(r, 1) + (r & 1)
    for k in range(GROUPS):
        pick = jnp.where(c == first + 2 * k, 1.0, 0.0).astype(bf16)
        full_ref[N_FSDP * MAIN :, 128 * k : 128 * k + 128] = jnp.dot(
            pick, tail, preferred_element_type=f32
        ).astype(bf16)
    x = full_ref[...]
    gram_ref[...] = jnp.zeros_like(gram_ref)
    gram_ref[:KVA_ROWS, :KVA_ROWS] = lax.dot_general(
        x, x, (((1,), (1,)), ((), ())), preferred_element_type=f32
    )
    for h, o_ref in ((c_ref[0], own_ref), (1 - c_ref[0], send_ref)):
        for i in range(BLOCKS):
            rows = pl.ds(pl.multiple_of(128 * i + 64 * h, 64), 64)
            for j in range(3):
                k = (i + j) % BLOCKS
                o_ref[64 * i : 64 * i + 64, 128 * j : 128 * j + 128] = gram_ref[
                    rows, 128 * k : 128 * k + 128
                ].astype(bf16)


def whole_gram(t_ref, gram_ref):
    for i in range(BLOCKS):
        for j in range(3):
            k = (i + j) % BLOCKS
            block = jnp.concatenate(
                [t_ref[h, 64 * i : 64 * i + 64, 128 * j : 128 * j + 128] for h in range(2)], axis=0
            ).astype(f32)
            gram_ref[128 * i : 128 * i + 128, 128 * k : 128 * k + 128] = block
            if j:
                gram_ref[128 * k : 128 * k + 128, 128 * i : 128 * i + 128] = block.T
    return gram_ref[:KVA_ROWS, :KVA_ROWS]


def mm(a, b):
    return jnp.dot(a.astype(bf16), b.astype(bf16), preferred_element_type=f32)


def symmetric_mm(a, b):
    a, b = a.astype(bf16), b.astype(bf16)
    cut = a.shape[0] // 256 * 256
    if cut == a.shape[0]:
        return jnp.dot(a, b, preferred_element_type=f32)
    left = jnp.dot(a, b[:, :cut], preferred_element_type=f32)
    corner = jnp.dot(a[cut:], b[:, cut:], preferred_element_type=f32)
    right = jnp.concatenate([left[cut:].T, corner], axis=0)
    return jnp.concatenate([left, right], axis=1)


def gram_scale(gram_ref):
    r = lax.broadcasted_iota(jnp.int32, (128, 128), 0)
    c = lax.broadcasted_iota(jnp.int32, (128, 128), 1)
    total = jnp.zeros((128, 128), f32)
    for i in range(gram_ref.shape[0] // 128):
        total += gram_ref[128 * i : 128 * i + 128, 128 * i : 128 * i + 128]
    squares = jnp.sum(jnp.where(r == c, total, 0.0))
    return 1.0 / (jnp.sqrt(squares) + norm_epsilon)


def two_steps(g0):
    d0 = c2 * g0 + c3 * symmetric_mm(g0, g0)
    t0 = c1 * g0 + symmetric_mm(d0, g0)
    g1 = c1 * t0 + symmetric_mm(d0, t0)
    d1 = c2 * g1 + c3 * symmetric_mm(g1, g1)
    d01 = c1 * (d0 + d1) + symmetric_mm(d1, d0)
    t1 = c1 * g1 + symmetric_mm(d1, g1)
    g2 = c1 * t1 + symmetric_mm(d1, t1)
    return d01, g2


def finish_b_body(i_ref, g0_ref, g1_ref, g2_ref, g3_ref, y_ref, o_ref, gram_ref):
    rows = KV_RANK // 4
    for k, g_ref in enumerate((g0_ref, g1_ref, g2_ref, g3_ref)):
        first = pl.multiple_of(((i_ref[0] + k) & 3) * rows, rows)
        gram_ref[pl.ds(first, rows), :] = g_ref[:rows].astype(f32)
    gram = gram_ref[...]
    s = gram_scale(gram_ref)
    d01, g2 = two_steps(gram * (s * s))
    d2 = c2 * g2 + c3 * mm(g2, g2)
    rest = c1 * d01 + c1 * c1 * d2 + mm(d2, d01)
    y = y_ref[...]
    total = s * math.sqrt(max(KVB_ROWS, KV_RANK))
    out = (c1 * c1 * c1) * y.astype(f32) + mm(y, rest)
    o_ref[...] = (out * total).astype(bf16)


def finish_a_body(
    f_ref, c_ref, own_ref, other_ref, x_ref, o_ref, halves_ref, gram_ref, d01_ref, g2_ref
):
    f = f_ref[0]
    halves_ref[c_ref[0]] = own_ref[...]
    halves_ref[1 - c_ref[0]] = other_ref[...]
    gram = whole_gram(halves_ref, gram_ref)
    s = gram_scale(gram_ref)
    d01, g2 = two_steps(gram * (s * s))
    d01_ref[...] = d01
    g2_ref[...] = g2
    main = pl.ds(pl.multiple_of(f * MAIN, MAIN), MAIN)
    base = N_FSDP * MAIN + 8 * lax.shift_right_logical(f, 2)
    tail = pl.ds(pl.multiple_of(base, 8), 8)

    def rows(ref):
        return jnp.concatenate([ref[main, :], ref[tail, :]], axis=0)

    g2_rows = rows(g2_ref)
    d2 = c2 * g2_rows + c3 * mm(g2_rows, g2)
    rest = c1 * rows(d01_ref) + c1 * c1 * d2 + mm(d2, d01)
    x_rows = jnp.concatenate([x_ref[main, :].astype(f32), x_ref[pl.ds(pl.multiple_of(N_FSDP * MAIN + 16 * lax.shift_right_logical(f, 3), 16), 16), :].astype(f32)], axis=0)
    total = s * math.sqrt(max(KVA_ROWS, D))
    moved = mm(rest, x_ref[...])
    out = ((c1 * c1 * c1) * x_rows[:MAIN] + moved[:MAIN]) * total
    o_main = out.astype(bf16)
    q = f & 3
    h = f & 7
    x_tail = x_rows[MAIN : MAIN + 2]
    for j in range(1, 8):
        x_tail = jnp.where(h == j, x_rows[MAIN + 2 * j : MAIN + 2 * j + 2], x_tail)
    m_tail = moved[MAIN : MAIN + 2]
    for j in range(1, 4):
        m_tail = jnp.where(q == j, moved[MAIN + 2 * j : MAIN + 2 * j + 2], m_tail)
    o_tail = tail_tile(((c1 * c1 * c1) * x_tail + m_tail) * total).astype(bf16)
    for r in range(N_DP):
        o_ref[r, :, :CHUNK] = o_main
        o_ref[r, :, CHUNK:] = o_tail


def unpack_body(u_ref, o_ref):
    for d in range(N_DP):
        o_ref[:MAIN, d * CHUNK : (d + 1) * CHUNK] = u_ref[d, :, :CHUNK]
        tail = u_ref[d, :, CHUNK:].astype(f32)
        for k in range(GROUPS):
            piece = slice(d * CHUNK + 128 * k, d * CHUNK + 128 * k + 128)
            o_ref[MAIN:, piece] = tail[2 * k : 2 * k + 2].astype(bf16)


def exchange(x, axis):
    return lax.all_to_all(x, axis, split_axis=0, concat_axis=0, tiled=True)


def total_of(x):
    return jnp.sum(x.astype(f32), axis=0)


def shift(x, axis, n, k):
    return lax.ppermute(x, axis, [(i, (i + k) % n) for i in range(n)])


def others(x, axis, n, step=1):
    return [x] + [shift(x, axis, n, n - k) for k in range(step, n, step)]


def sum_over(x, axis, n, step=1):
    return pair_sums(others(x, axis, n, step))


def pair_sums(terms):
    terms = [y.astype(f32) for y in terms]
    while len(terms) > 1:
        half = len(terms) // 2
        terms = [terms[k] + terms[k + half] for k in range(half)]
    return terms[0].astype(bf16)


def sum_pair(x, axis, n):
    other = lax.ppermute(x, axis, [(i, i ^ 1) for i in range(n)])
    return (x.astype(f32) + other.astype(f32)).astype(bf16)


def local(kva_parts, kvb_parts, kva_moment, kvb_moment):
    y = lax.axis_index("y").astype(jnp.int32).reshape(1)
    c = lax.axis_index("c").astype(jnp.int32).reshape(1)
    z = lax.axis_index("z").astype(jnp.int32).reshape(1)
    d = y * 2 + c
    rows_b = KV_RANK // N_DP

    half = shape((kvb_parts.shape[1] // 2, KV_RANK), bf16)
    packed, send_b = call(
        pack_body,
        (shape((N_DP, MAIN, WIDE), bf16), half),
        1,
        2,
        [pltpu.VMEM(kva_parts.shape, bf16), pltpu.SemaphoreType.DMA((2,))],
        pl.ANY,
        67_000_000,
    )(c, kva_parts, kvb_parts)
    terms_a = exchange(packed, DP)
    grad_b = call(half_b_body, half, 1, 2)(c, kvb_parts, shift(send_b, "c", 2, 1))
    terms_a, grad_b = lax.optimization_barrier((terms_a, grad_b))
    grads_b = others(grad_b, "y", 4)
    grad_a, push_a = call(
        push_a_body,
        (shape((2 * MAIN, KV_RANK), bf16), shape((8, MAIN, WIDE), bf16)),
        1,
        2,
    )(d, terms_a, kva_moment)
    all_z = exchange(push_a, "z")

    rows = half.shape[0]
    both = call(sum_b_body, shape((rows + 2 * MAIN, KV_RANK), bf16), 0, 5, flops=HINT)(
        *grads_b, grad_a
    )
    both = lax.all_gather(both, "c")
    all_z, both = lax.optimization_barrier((all_z, both))
    all_a = others(all_z, "x", 4)
    moment_b, long_b, piece_b, grad_a = call(
        moment_b_body,
        (
            shape(kvb_moment.shape, f32),
            shape(kvb_moment.shape, bf16),
            shape((rows_b, KV_RANK), bf16),
            shape((2, 2 * MAIN, KV_RANK), bf16),
        ),
        1,
        2,
        [pltpu.VMEM((KV_RANK, KV_RANK), f32)],
    )(d, both, kvb_moment)
    terms_b = others(sum_pair(piece_b, "z", 8), "z", 8, 2)

    part = shape((64 * BLOCKS, 384), bf16)
    gram_a, send_a, short_a = call(
        gram_a_body,
        (part, part, shape((KVA_ROWS, CHUNK), bf16)),
        1,
        4,
        [pltpu.VMEM((128 * BLOCKS, 128 * BLOCKS), f32)],
    )(c, *all_a)
    send_a, terms_b = lax.optimization_barrier((send_a, terms_b))
    piece_b = pair_sums(terms_b)
    gram_a = pair_sums([gram_a, shift(send_a, "c", 2, 1)])
    gram_a = sum_over(gram_a, "y", 4)
    piece_b = lax.all_gather(sum_over(piece_b, "x", 4), "c", tiled=True)

    piece_b = jnp.concatenate([piece_b, grad_a.reshape(-1, KV_RANK)])
    gram_a, piece_b = lax.optimization_barrier((gram_a, piece_b))
    other_a = shift(gram_a, "c", 2, 1)
    pieces_b = others(piece_b, "y", 4)
    update_a = call(
        finish_a_body,
        shape((N_DP, MAIN, WIDE), bf16),
        2,
        3,
        [pltpu.VMEM((2,) + part.shape, bf16), pltpu.VMEM((128 * BLOCKS, 128 * BLOCKS), f32)]
        + [pltpu.VMEM((KVA_ROWS, KVA_ROWS), f32)] * 2,
        flops=HINT,
    )(z, c, gram_a, other_a, short_a)
    moment_a = call(moment_a_body, shape(kva_moment.shape, f32), 1, 5)(y, *pieces_b, kva_moment)
    update_a = call(unpack_body, shape(kva_moment.shape, bf16))(exchange(update_a, DP))
    update_b = call(
        finish_b_body,
        shape(long_b.shape, bf16),
        1,
        5,
        [pltpu.VMEM((KV_RANK, KV_RANK), f32)],
        flops=HINT,
    )(y, *pieces_b, long_b)
    return (moment_a, moment_b, update_a, update_b)


def solution(mesh):
    fine = Mesh(mesh.devices.reshape(4, 2, 4, 8), DP + FSDP)
    return jax.shard_map(
        local,
        mesh=fine,
        in_specs=(P(DP, FSDP, None), P(DP, FSDP, None), P(FSDP, None), P(FSDP, None)),
        out_specs=(P(FSDP, None), P(FSDP, None), P(FSDP, None), P(FSDP, None)),
        check_vma=False,
    )
```

```python
import functools
import math

import jax
import jax.numpy as jnp
from jax import lax
from jax.experimental import pallas as pl
from jax.experimental.pallas import tpu as pltpu
from jax.sharding import Mesh, PartitionSpec as P

D = 7168
KV_RANK = 512
KVA_ROWS = 576
KVB_ROWS = 16384
DP = ("y", "c")
FSDP = ("x", "z")
N_DP = 8
N_FSDP = 32
CHUNK = D // N_DP
GROUPS = CHUNK // 128
MAIN = 16
WIDE = CHUNK + 128
BLOCKS = 5

c1 = 3.4445
c2 = -4.775
c3 = 2.0315
decay_rate = 0.95
norm_epsilon = 1e-07
f32 = jnp.float32
bf16 = jnp.bfloat16
VMEM_LIMIT = 48 * 1024 * 1024
HINT = 40_000_000_000


def call(body, out_shape, n_scalar=0, n_in=1, scratch=(), space=pltpu.VMEM, limit=VMEM_LIMIT, flops=0):
    return pl.pallas_call(
        body,
        out_shape=out_shape,
        in_specs=[pl.BlockSpec(memory_space=pltpu.SMEM)] * n_scalar
        + [pl.BlockSpec(memory_space=space)] * n_in,
        out_specs=jax.tree.map(lambda _: pl.BlockSpec(memory_space=pltpu.VMEM), out_shape),
        scratch_shapes=list(scratch),
        compiler_params=pltpu.CompilerParams(vmem_limit_bytes=limit),
        cost_estimate=pl.CostEstimate(flops=flops, bytes_accessed=0, transcendentals=0)
        if flops
        else None,
    )


def shape(dims, dtype):
    return jax.ShapeDtypeStruct(dims, dtype)


def tail_tile(rows):
    pieces = [rows[:, 128 * k : 128 * k + 128] for k in range(GROUPS)]
    return jnp.concatenate(pieces + [jnp.zeros((2, 128), f32)], axis=0)


def pack_body(c_ref, a_ref, b_ref, o_ref, send_ref, held_ref, sems):
    rows = send_ref.shape[0]
    other = pl.ds(pl.multiple_of((1 - c_ref[0]) * rows, rows), rows)
    copy_a = pltpu.make_async_copy(a_ref, held_ref, sems.at[0])
    copy_b = pltpu.make_async_copy(b_ref.at[0, other], send_ref, sems.at[1])
    copy_a.start()
    copy_b.start()
    copy_a.wait()
    for d in range(N_DP):
        lanes = slice(d * CHUNK, (d + 1) * CHUNK)
        o_ref[d, :, :CHUNK] = held_ref[0, :MAIN, lanes]
        o_ref[d, :, CHUNK:] = tail_tile(held_ref[0, MAIN:, lanes].astype(f32)).astype(bf16)
    copy_b.wait()


def push_a_body(d_ref, parts_ref, m_ref, g_ref, x_ref):
    start = pl.multiple_of(d_ref[0] * CHUNK, 128)
    grad = parts_ref[0].astype(f32)
    for r in range(1, N_DP):
        grad += parts_ref[r].astype(f32)
    g_ref[:MAIN] = grad[:, :KV_RANK].astype(bf16)
    g_ref[MAIN:] = grad[:, KV_RANK:].astype(bf16)
    m_main = m_ref[:MAIN, pl.ds(start, CHUNK)]
    m_tail = tail_tile(m_ref[MAIN:, pl.ds(start, CHUNK)])
    moment = decay_rate * jnp.concatenate([m_main, m_tail], axis=1) + grad
    push = (grad + decay_rate * moment).astype(bf16)
    for r in range(x_ref.shape[0]):
        x_ref[r] = push


def moment_a_body(i_ref, g0_ref, g1_ref, g2_ref, g3_ref, m_ref, o_ref):
    for k, g_ref in enumerate((g0_ref, g1_ref, g2_ref, g3_ref)):
        for c in range(2):
            start = (((i_ref[0] + k) & 3) * 2 + c) * CHUNK
            lanes = pl.ds(pl.multiple_of(start, 128), CHUNK)
            first = KV_RANK // 4 + 2 * MAIN * c
            low = g_ref[first : first + MAIN]
            high = g_ref[first + MAIN : first + 2 * MAIN]
            grad = jnp.concatenate([low, high], axis=1).astype(f32)
            main = grad[:, :CHUNK]
            o_ref[:MAIN, lanes] = decay_rate * m_ref[:MAIN, lanes] + main
            tail = grad[:, CHUNK:]
            for j in range(GROUPS):
                piece = pl.ds(pl.multiple_of(start + 128 * j, 128), 128)
                o_ref[MAIN:, piece] = decay_rate * m_ref[MAIN:, piece] + tail[2 * j : 2 * j + 2]


def half_b_body(c_ref, b_ref, x_ref, o_ref):
    rows = o_ref.shape[0]
    half = b_ref[0, pl.ds(pl.multiple_of(c_ref[0] * rows, rows), rows)]
    o_ref[...] = (half.astype(f32) + x_ref[...].astype(f32)).astype(bf16)


def sum_b_body(b0_ref, b1_ref, b2_ref, b3_ref, g_ref, o_ref):
    rows = b0_ref.shape[0]
    first = b0_ref[...].astype(f32) + b2_ref[...].astype(f32)
    second = b1_ref[...].astype(f32) + b3_ref[...].astype(f32)
    o_ref[:rows] = (first + second).astype(bf16)
    o_ref[rows:] = g_ref[...]


def moment_b_body(d_ref, g_ref, m_ref, o_ref, y_ref, p_ref, a_ref, scratch):
    rows = m_ref.shape[0] // 2
    a_ref[...] = g_ref[:, rows:]
    grad = jnp.concatenate([g_ref[0, :rows], g_ref[1, :rows]], axis=0).astype(f32)
    moment = decay_rate * m_ref[...] + grad
    o_ref[...] = moment
    y = (grad + decay_rate * moment).astype(bf16)
    y_ref[...] = y
    scratch[...] = lax.dot_general(y, y, (((0,), (0,)), ((), ())), preferred_element_type=f32)
    rows = KV_RANK // N_DP
    p_ref[...] = scratch[pl.ds(pl.multiple_of(d_ref[0] * rows, rows), rows), :].astype(bf16)


def gram_a_body(c_ref, x0_ref, x1_ref, x2_ref, x3_ref, own_ref, send_ref, full_ref, gram_ref):
    tails = []
    for k, x_ref in enumerate((x0_ref, x1_ref, x2_ref, x3_ref)):
        full_ref[128 * k : 128 * k + 128] = x_ref[:, :, :CHUNK].reshape(128, CHUNK)
        tails.append(x_ref[:, :, CHUNK:].reshape(128, 128))
    tail = jnp.concatenate(tails, axis=0)
    rows = 2 * N_FSDP
    r = lax.broadcasted_iota(jnp.int32, (rows, N_FSDP * MAIN), 0)
    c = lax.broadcasted_iota(jnp.int32, (rows, N_FSDP * MAIN), 1)
    first = MAIN * lax.shift_right_logical(r, 1) + (r & 1)
    for k in range(GROUPS):
        pick = jnp.where(c == first + 2 * k, 1.0, 0.0).astype(bf16)
        full_ref[N_FSDP * MAIN :, 128 * k : 128 * k + 128] = jnp.dot(
            pick, tail, preferred_element_type=f32
        ).astype(bf16)
    x = full_ref[...]
    gram_ref[...] = jnp.zeros_like(gram_ref)
    gram_ref[:KVA_ROWS, :KVA_ROWS] = lax.dot_general(
        x, x, (((1,), (1,)), ((), ())), preferred_element_type=f32
    )
    for h, o_ref in ((c_ref[0], own_ref), (1 - c_ref[0], send_ref)):
        for i in range(BLOCKS):
            rows = pl.ds(pl.multiple_of(128 * i + 64 * h, 64), 64)
            for j in range(3):
                k = (i + j) % BLOCKS
                o_ref[64 * i : 64 * i + 64, 128 * j : 128 * j + 128] = gram_ref[
                    rows, 128 * k : 128 * k + 128
                ].astype(bf16)


def whole_gram(t_ref, gram_ref):
    for i in range(BLOCKS):
        for j in range(3):
            k = (i + j) % BLOCKS
            block = jnp.concatenate(
                [t_ref[h, 64 * i : 64 * i + 64, 128 * j : 128 * j + 128] for h in range(2)], axis=0
            ).astype(f32)
            gram_ref[128 * i : 128 * i + 128, 128 * k : 128 * k + 128] = block
            if j:
                gram_ref[128 * k : 128 * k + 128, 128 * i : 128 * i + 128] = block.T
    return gram_ref[:KVA_ROWS, :KVA_ROWS]


def mm(a, b):
    return jnp.dot(a.astype(bf16), b.astype(bf16), preferred_element_type=f32)


def symmetric_mm(a, b):
    a, b = a.astype(bf16), b.astype(bf16)
    cut = a.shape[0] // 256 * 256
    if cut == a.shape[0]:
        return jnp.dot(a, b, preferred_element_type=f32)
    left = jnp.dot(a, b[:, :cut], preferred_element_type=f32)
    corner = jnp.dot(a[cut:], b[:, cut:], preferred_element_type=f32)
    right = jnp.concatenate([left[cut:].T, corner], axis=0)
    return jnp.concatenate([left, right], axis=1)


def gram_scale(gram_ref):
    r = lax.broadcasted_iota(jnp.int32, (128, 128), 0)
    c = lax.broadcasted_iota(jnp.int32, (128, 128), 1)
    total = jnp.zeros((128, 128), f32)
    for i in range(gram_ref.shape[0] // 128):
        total += gram_ref[128 * i : 128 * i + 128, 128 * i : 128 * i + 128]
    squares = jnp.sum(jnp.where(r == c, total, 0.0))
    return 1.0 / (jnp.sqrt(squares) + norm_epsilon)


def two_steps(g0):
    d0 = c2 * g0 + c3 * symmetric_mm(g0, g0)
    t0 = c1 * g0 + symmetric_mm(d0, g0)
    g1 = c1 * t0 + symmetric_mm(d0, t0)
    d1 = c2 * g1 + c3 * symmetric_mm(g1, g1)
    d01 = c1 * (d0 + d1) + symmetric_mm(d1, d0)
    t1 = c1 * g1 + symmetric_mm(d1, g1)
    g2 = c1 * t1 + symmetric_mm(d1, t1)
    return d01, g2


def finish_b_body(i_ref, g0_ref, g1_ref, g2_ref, g3_ref, y_ref, o_ref, gram_ref):
    rows = KV_RANK // 4
    for k, g_ref in enumerate((g0_ref, g1_ref, g2_ref, g3_ref)):
        first = pl.multiple_of(((i_ref[0] + k) & 3) * rows, rows)
        gram_ref[pl.ds(first, rows), :] = g_ref[:rows].astype(f32)
    gram = gram_ref[...]
    s = gram_scale(gram_ref)
    d01, g2 = two_steps(gram * (s * s))
    d2 = c2 * g2 + c3 * mm(g2, g2)
    rest = c1 * d01 + c1 * c1 * d2 + mm(d2, d01)
    y = y_ref[...]
    total = s * math.sqrt(max(KVB_ROWS, KV_RANK))
    out = (c1 * c1 * c1) * y.astype(f32) + mm(y, rest)
    o_ref[...] = (out * total).astype(bf16)


def finish_a_body(
    f_ref, c_ref, own_ref, other_ref, x_ref, o_ref, halves_ref, gram_ref, d01_ref, g2_ref
):
    f = f_ref[0]
    halves_ref[c_ref[0]] = own_ref[...]
    halves_ref[1 - c_ref[0]] = other_ref[...]
    gram = whole_gram(halves_ref, gram_ref)
    s = gram_scale(gram_ref)
    d01, g2 = two_steps(gram * (s * s))
    d01_ref[...] = d01
    g2_ref[...] = g2
    main = pl.ds(pl.multiple_of(f * MAIN, MAIN), MAIN)
    base = N_FSDP * MAIN + 8 * lax.shift_right_logical(f, 2)
    tail = pl.ds(pl.multiple_of(base, 8), 8)

    def rows(ref):
        return jnp.concatenate([ref[main, :], ref[tail, :]], axis=0)

    g2_rows = rows(g2_ref)
    d2 = c2 * g2_rows + c3 * mm(g2_rows, g2)
    rest = c1 * rows(d01_ref) + c1 * c1 * d2 + mm(d2, d01)
    x_rows = jnp.concatenate([x_ref[main, :].astype(f32), x_ref[pl.ds(pl.multiple_of(N_FSDP * MAIN + 16 * lax.shift_right_logical(f, 3), 16), 16), :].astype(f32)], axis=0)
    total = s * math.sqrt(max(KVA_ROWS, D))
    moved = mm(rest, x_ref[...])
    out = ((c1 * c1 * c1) * x_rows[:MAIN] + moved[:MAIN]) * total
    o_main = out.astype(bf16)
    q = f & 3
    h = f & 7
    x_tail = x_rows[MAIN : MAIN + 2]
    for j in range(1, 8):
        x_tail = jnp.where(h == j, x_rows[MAIN + 2 * j : MAIN + 2 * j + 2], x_tail)
    m_tail = moved[MAIN : MAIN + 2]
    for j in range(1, 4):
        m_tail = jnp.where(q == j, moved[MAIN + 2 * j : MAIN + 2 * j + 2], m_tail)
    o_tail = tail_tile(((c1 * c1 * c1) * x_tail + m_tail) * total).astype(bf16)
    for r in range(N_DP):
        o_ref[r, :, :CHUNK] = o_main
        o_ref[r, :, CHUNK:] = o_tail


def unpack_body(u_ref, o_ref):
    for d in range(N_DP):
        o_ref[:MAIN, d * CHUNK : (d + 1) * CHUNK] = u_ref[d, :, :CHUNK]
        tail = u_ref[d, :, CHUNK:].astype(f32)
        for k in range(GROUPS):
            piece = slice(d * CHUNK + 128 * k, d * CHUNK + 128 * k + 128)
            o_ref[MAIN:, piece] = tail[2 * k : 2 * k + 2].astype(bf16)


def exchange(x, axis):
    return lax.all_to_all(x, axis, split_axis=0, concat_axis=0, tiled=True)


def total_of(x):
    return jnp.sum(x.astype(f32), axis=0)


def shift(x, axis, n, k):
    return lax.ppermute(x, axis, [(i, (i + k) % n) for i in range(n)])


def others(x, axis, n, step=1):
    return [x] + [shift(x, axis, n, n - k) for k in range(step, n, step)]


def sum_over(x, axis, n, step=1):
    return pair_sums(others(x, axis, n, step))


def pair_sums(terms):
    terms = [y.astype(f32) for y in terms]
    while len(terms) > 1:
        half = len(terms) // 2
        terms = [terms[k] + terms[k + half] for k in range(half)]
    return terms[0].astype(bf16)


def sum_pair(x, axis, n):
    other = lax.ppermute(x, axis, [(i, i ^ 1) for i in range(n)])
    return (x.astype(f32) + other.astype(f32)).astype(bf16)


def local(kva_parts, kvb_parts, kva_moment, kvb_moment):
    y = lax.axis_index("y").astype(jnp.int32).reshape(1)
    c = lax.axis_index("c").astype(jnp.int32).reshape(1)
    z = lax.axis_index("z").astype(jnp.int32).reshape(1)
    d = y * 2 + c
    rows_b = KV_RANK // N_DP

    half = shape((kvb_parts.shape[1] // 2, KV_RANK), bf16)
    packed, send_b = call(
        pack_body,
        (shape((N_DP, MAIN, WIDE), bf16), half),
        1,
        2,
        [pltpu.VMEM(kva_parts.shape, bf16), pltpu.SemaphoreType.DMA((2,))],
        pl.ANY,
        67_000_000,
    )(c, kva_parts, kvb_parts)
    terms_a = exchange(packed, DP)
    grad_b = call(half_b_body, half, 1, 2)(c, kvb_parts, shift(send_b, "c", 2, 1))
    terms_a, grad_b = lax.optimization_barrier((terms_a, grad_b))
    grads_b = others(grad_b, "y", 4)
    grad_a, push_a = call(
        push_a_body,
        (shape((2 * MAIN, KV_RANK), bf16), shape((8, MAIN, WIDE), bf16)),
        1,
        2,
    )(d, terms_a, kva_moment)
    all_z = exchange(push_a, "z")

    rows = half.shape[0]
    both = call(sum_b_body, shape((rows + 2 * MAIN, KV_RANK), bf16), 0, 5, flops=HINT)(
        *grads_b, grad_a
    )
    both = lax.all_gather(both, "c")
    all_z, both = lax.optimization_barrier((all_z, both))
    all_a = others(all_z, "x", 4)
    moment_b, long_b, piece_b, grad_a = call(
        moment_b_body,
        (
            shape(kvb_moment.shape, f32),
            shape(kvb_moment.shape, bf16),
            shape((rows_b, KV_RANK), bf16),
            shape((2, 2 * MAIN, KV_RANK), bf16),
        ),
        1,
        2,
        [pltpu.VMEM((KV_RANK, KV_RANK), f32)],
    )(d, both, kvb_moment)
    terms_b = others(sum_pair(piece_b, "z", 8), "z", 8, 2)

    part = shape((64 * BLOCKS, 384), bf16)
    gram_a, send_a, short_a = call(
        gram_a_body,
        (part, part, shape((KVA_ROWS, CHUNK), bf16)),
        1,
        4,
        [pltpu.VMEM((128 * BLOCKS, 128 * BLOCKS), f32)],
    )(c, *all_a)
    _, terms_b = lax.optimization_barrier((send_a, terms_b))
    piece_b = pair_sums(terms_b)
    gram_a = pair_sums([gram_a, shift(send_a, "c", 2, 1)])
    gram_a = sum_over(gram_a, "y", 4)
    piece_b = lax.all_gather(sum_over(piece_b, "x", 4), "c", tiled=True)

    piece_b = jnp.concatenate([piece_b, grad_a.reshape(-1, KV_RANK)])
    gram_a, piece_b = lax.optimization_barrier((gram_a, piece_b))
    other_a = shift(gram_a, "c", 2, 1)
    pieces_b = others(piece_b, "y", 4)
    update_a = call(
        finish_a_body,
        shape((N_DP, MAIN, WIDE), bf16),
        2,
        3,
        [pltpu.VMEM((2,) + part.shape, bf16), pltpu.VMEM((128 * BLOCKS, 128 * BLOCKS), f32)]
        + [pltpu.VMEM((KVA_ROWS, KVA_ROWS), f32)] * 2,
        flops=HINT,
    )(z, c, gram_a, other_a, short_a)
    moment_a = call(moment_a_body, shape(kva_moment.shape, f32), 1, 5)(y, *pieces_b, kva_moment)
    update_a = call(unpack_body, shape(kva_moment.shape, bf16))(exchange(update_a, DP))
    update_b = call(
        finish_b_body,
        shape(long_b.shape, bf16),
        1,
        5,
        [pltpu.VMEM((KV_RANK, KV_RANK), f32)],
        flops=HINT,
    )(y, *pieces_b, long_b)
    return (moment_a, moment_b, update_a, update_b)


def solution(mesh):
    fine = Mesh(mesh.devices.reshape(4, 2, 4, 8), DP + FSDP)
    return jax.shard_map(
        local,
        mesh=fine,
        in_specs=(P(DP, FSDP, None), P(DP, FSDP, None), P(FSDP, None), P(FSDP, None)),
        out_specs=(P(FSDP, None), P(FSDP, None), P(FSDP, None), P(FSDP, None)),
        check_vma=False,
    )
```

```python
import functools
import math

import jax
import jax.numpy as jnp
from jax import lax
from jax.experimental import pallas as pl
from jax.experimental.pallas import tpu as pltpu
from jax.sharding import Mesh, PartitionSpec as P

D = 7168
KV_RANK = 512
KVA_ROWS = 576
KVB_ROWS = 16384
DP = ("y", "c")
FSDP = ("x", "z")
N_DP = 8
N_FSDP = 32
CHUNK = D // N_DP
GROUPS = CHUNK // 128
MAIN = 16
WIDE = CHUNK + 128
BLOCKS = 5

c1 = 3.4445
c2 = -4.775
c3 = 2.0315
decay_rate = 0.95
norm_epsilon = 1e-07
f32 = jnp.float32
bf16 = jnp.bfloat16
VMEM_LIMIT = 48 * 1024 * 1024
HINT = 40_000_000_000


def call(body, out_shape, n_scalar=0, n_in=1, scratch=(), space=pltpu.VMEM, limit=VMEM_LIMIT, flops=0):
    return pl.pallas_call(
        body,
        out_shape=out_shape,
        in_specs=[pl.BlockSpec(memory_space=pltpu.SMEM)] * n_scalar
        + [pl.BlockSpec(memory_space=space)] * n_in,
        out_specs=jax.tree.map(lambda _: pl.BlockSpec(memory_space=pltpu.VMEM), out_shape),
        scratch_shapes=list(scratch),
        compiler_params=pltpu.CompilerParams(vmem_limit_bytes=limit),
        cost_estimate=pl.CostEstimate(flops=flops, bytes_accessed=0, transcendentals=0)
        if flops
        else None,
    )


def shape(dims, dtype):
    return jax.ShapeDtypeStruct(dims, dtype)


def tail_tile(rows):
    pieces = [rows[:, 128 * k : 128 * k + 128] for k in range(GROUPS)]
    return jnp.concatenate(pieces + [jnp.zeros((2, 128), f32)], axis=0)


def pack_body(c_ref, a_ref, b_ref, o_ref, send_ref, held_ref, sems):
    rows = send_ref.shape[0]
    other = pl.ds(pl.multiple_of((1 - c_ref[0]) * rows, rows), rows)
    copy_a = pltpu.make_async_copy(a_ref, held_ref, sems.at[0])
    copy_b = pltpu.make_async_copy(b_ref.at[0, other], send_ref, sems.at[1])
    copy_a.start()
    copy_b.start()
    copy_a.wait()
    for d in range(N_DP):
        lanes = slice(d * CHUNK, (d + 1) * CHUNK)
        o_ref[d, :, :CHUNK] = held_ref[0, :MAIN, lanes]
        o_ref[d, :, CHUNK:] = tail_tile(held_ref[0, MAIN:, lanes].astype(f32)).astype(bf16)
    copy_b.wait()


def push_a_body(d_ref, parts_ref, m_ref, g_ref, x_ref):
    start = pl.multiple_of(d_ref[0] * CHUNK, 128)
    grad = parts_ref[0].astype(f32)
    for r in range(1, N_DP):
        grad += parts_ref[r].astype(f32)
    g_ref[:MAIN] = grad[:, :KV_RANK].astype(bf16)
    g_ref[MAIN:] = grad[:, KV_RANK:].astype(bf16)
    m_main = m_ref[:MAIN, pl.ds(start, CHUNK)]
    m_tail = tail_tile(m_ref[MAIN:, pl.ds(start, CHUNK)])
    moment = decay_rate * jnp.concatenate([m_main, m_tail], axis=1) + grad
    push = (grad + decay_rate * moment).astype(bf16)
    for r in range(x_ref.shape[0]):
        x_ref[r] = push


def moment_a_body(i_ref, g0_ref, g1_ref, g2_ref, g3_ref, m_ref, o_ref):
    for k, g_ref in enumerate((g0_ref, g1_ref, g2_ref, g3_ref)):
        for c in range(2):
            start = (((i_ref[0] + k) & 3) * 2 + c) * CHUNK
            lanes = pl.ds(pl.multiple_of(start, 128), CHUNK)
            first = KV_RANK // 4 + 2 * MAIN * c
            low = g_ref[first : first + MAIN]
            high = g_ref[first + MAIN : first + 2 * MAIN]
            grad = jnp.concatenate([low, high], axis=1).astype(f32)
            main = grad[:, :CHUNK]
            o_ref[:MAIN, lanes] = decay_rate * m_ref[:MAIN, lanes] + main
            tail = grad[:, CHUNK:]
            for j in range(GROUPS):
                piece = pl.ds(pl.multiple_of(start + 128 * j, 128), 128)
                o_ref[MAIN:, piece] = decay_rate * m_ref[MAIN:, piece] + tail[2 * j : 2 * j + 2]


def half_b_body(c_ref, b_ref, x_ref, o_ref):
    rows = o_ref.shape[0]
    half = b_ref[0, pl.ds(pl.multiple_of(c_ref[0] * rows, rows), rows)]
    o_ref[...] = (half.astype(f32) + x_ref[...].astype(f32)).astype(bf16)


def sum_b_body(b0_ref, b1_ref, b2_ref, b3_ref, g_ref, o_ref):
    rows = b0_ref.shape[0]
    first = b0_ref[...].astype(f32) + b2_ref[...].astype(f32)
    second = b1_ref[...].astype(f32) + b3_ref[...].astype(f32)
    o_ref[:rows] = (first + second).astype(bf16)
    o_ref[rows:] = g_ref[...]


def moment_b_body(d_ref, g_ref, m_ref, o_ref, y_ref, p_ref, a_ref, scratch):
    rows = m_ref.shape[0] // 2
    a_ref[...] = g_ref[:, rows:]
    grad = jnp.concatenate([g_ref[0, :rows], g_ref[1, :rows]], axis=0).astype(f32)
    moment = decay_rate * m_ref[...] + grad
    o_ref[...] = moment
    y = (grad + decay_rate * moment).astype(bf16)
    y_ref[...] = y
    scratch[...] = lax.dot_general(y, y, (((0,), (0,)), ((), ())), preferred_element_type=f32)
    rows = KV_RANK // N_DP
    p_ref[...] = scratch[pl.ds(pl.multiple_of(d_ref[0] * rows, rows), rows), :].astype(bf16)


def gram_a_body(c_ref, x0_ref, x1_ref, x2_ref, x3_ref, own_ref, send_ref, full_ref, gram_ref):
    tails = []
    for k, x_ref in enumerate((x0_ref, x1_ref, x2_ref, x3_ref)):
        full_ref[128 * k : 128 * k + 128] = x_ref[:, :, :CHUNK].reshape(128, CHUNK)
        tails.append(x_ref[:, :, CHUNK:].reshape(128, 128))
    tail = jnp.concatenate(tails, axis=0)
    rows = 2 * N_FSDP
    r = lax.broadcasted_iota(jnp.int32, (rows, N_FSDP * MAIN), 0)
    c = lax.broadcasted_iota(jnp.int32, (rows, N_FSDP * MAIN), 1)
    first = MAIN * lax.shift_right_logical(r, 1) + (r & 1)
    for k in range(GROUPS):
        pick = jnp.where(c == first + 2 * k, 1.0, 0.0).astype(bf16)
        full_ref[N_FSDP * MAIN :, 128 * k : 128 * k + 128] = jnp.dot(
            pick, tail, preferred_element_type=f32
        ).astype(bf16)
    x = full_ref[...]
    gram_ref[...] = jnp.zeros_like(gram_ref)
    gram_ref[:KVA_ROWS, :KVA_ROWS] = lax.dot_general(
        x, x, (((1,), (1,)), ((), ())), preferred_element_type=f32
    )
    for h, o_ref in ((c_ref[0], own_ref), (1 - c_ref[0], send_ref)):
        for i in range(BLOCKS):
            rows = pl.ds(pl.multiple_of(128 * i + 64 * h, 64), 64)
            for j in range(3):
                k = (i + j) % BLOCKS
                o_ref[64 * i : 64 * i + 64, 128 * j : 128 * j + 128] = gram_ref[
                    rows, 128 * k : 128 * k + 128
                ].astype(bf16)


def whole_gram(t_ref, gram_ref):
    for i in range(BLOCKS):
        for j in range(3):
            k = (i + j) % BLOCKS
            block = jnp.concatenate(
                [t_ref[h, 64 * i : 64 * i + 64, 128 * j : 128 * j + 128] for h in range(2)], axis=0
            ).astype(f32)
            gram_ref[128 * i : 128 * i + 128, 128 * k : 128 * k + 128] = block
            if j:
                gram_ref[128 * k : 128 * k + 128, 128 * i : 128 * i + 128] = block.T
    return gram_ref[:KVA_ROWS, :KVA_ROWS]


def mm(a, b):
    return jnp.dot(a.astype(bf16), b.astype(bf16), preferred_element_type=f32)


def symmetric_mm(a, b):
    a, b = a.astype(bf16), b.astype(bf16)
    cut = a.shape[0] // 256 * 256
    if cut == a.shape[0]:
        return jnp.dot(a, b, preferred_element_type=f32)
    left = jnp.dot(a, b[:, :cut], preferred_element_type=f32)
    corner = jnp.dot(a[cut:], b[:, cut:], preferred_element_type=f32)
    right = jnp.concatenate([left[cut:].T, corner], axis=0)
    return jnp.concatenate([left, right], axis=1)


def gram_scale(gram_ref):
    r = lax.broadcasted_iota(jnp.int32, (128, 128), 0)
    c = lax.broadcasted_iota(jnp.int32, (128, 128), 1)
    total = jnp.zeros((128, 128), f32)
    for i in range(gram_ref.shape[0] // 128):
        total += gram_ref[128 * i : 128 * i + 128, 128 * i : 128 * i + 128]
    squares = jnp.sum(jnp.where(r == c, total, 0.0))
    return 1.0 / (jnp.sqrt(squares) + norm_epsilon)


def two_steps(g0):
    d0 = c2 * g0 + c3 * symmetric_mm(g0, g0)
    t0 = c1 * g0 + symmetric_mm(d0, g0)
    g1 = c1 * t0 + symmetric_mm(d0, t0)
    d1 = c2 * g1 + c3 * symmetric_mm(g1, g1)
    d01 = c1 * (d0 + d1) + symmetric_mm(d1, d0)
    t1 = c1 * g1 + symmetric_mm(d1, g1)
    g2 = c1 * t1 + symmetric_mm(d1, t1)
    return d01, g2


def finish_b_body(i_ref, g0_ref, g1_ref, g2_ref, g3_ref, y_ref, o_ref, gram_ref):
    rows = KV_RANK // 4
    for k, g_ref in enumerate((g0_ref, g1_ref, g2_ref, g3_ref)):
        first = pl.multiple_of(((i_ref[0] + k) & 3) * rows, rows)
        gram_ref[pl.ds(first, rows), :] = g_ref[:rows].astype(f32)
    gram = gram_ref[...]
    s = gram_scale(gram_ref)
    d01, g2 = two_steps(gram * (s * s))
    d2 = c2 * g2 + c3 * mm(g2, g2)
    rest = c1 * d01 + c1 * c1 * d2 + mm(d2, d01)
    y = y_ref[...]
    total = s * math.sqrt(max(KVB_ROWS, KV_RANK))
    out = (c1 * c1 * c1) * y.astype(f32) + mm(y, rest)
    o_ref[...] = (out * total).astype(bf16)


def finish_a_body(
    f_ref, c_ref, own_ref, other_ref, x_ref, o_ref, halves_ref, gram_ref, d01_ref, g2_ref
):
    f = f_ref[0]
    halves_ref[c_ref[0]] = own_ref[...]
    halves_ref[1 - c_ref[0]] = other_ref[...]
    gram = whole_gram(halves_ref, gram_ref)
    s = gram_scale(gram_ref)
    d01, g2 = two_steps(gram * (s * s))
    d01_ref[...] = d01
    g2_ref[...] = g2
    main = pl.ds(pl.multiple_of(f * MAIN, MAIN), MAIN)
    base = N_FSDP * MAIN + 8 * lax.shift_right_logical(f, 2)
    tail = pl.ds(pl.multiple_of(base, 8), 8)

    def rows(ref):
        return jnp.concatenate([ref[main, :], ref[tail, :]], axis=0)

    g2_rows = rows(g2_ref)
    d2 = c2 * g2_rows + c3 * mm(g2_rows, g2)
    rest = c1 * rows(d01_ref) + c1 * c1 * d2 + mm(d2, d01)
    x_rows = jnp.concatenate([x_ref[main, :].astype(f32), x_ref[pl.ds(pl.multiple_of(N_FSDP * MAIN + 16 * lax.shift_right_logical(f, 3), 16), 16), :].astype(f32)], axis=0)
    total = s * math.sqrt(max(KVA_ROWS, D))
    moved = mm(rest, x_ref[...])
    out = ((c1 * c1 * c1) * x_rows[:MAIN] + moved[:MAIN]) * total
    o_main = out.astype(bf16)
    q = f & 3
    h = f & 7
    x_tail = x_rows[MAIN : MAIN + 2]
    for j in range(1, 8):
        x_tail = jnp.where(h == j, x_rows[MAIN + 2 * j : MAIN + 2 * j + 2], x_tail)
    m_tail = moved[MAIN : MAIN + 2]
    for j in range(1, 4):
        m_tail = jnp.where(q == j, moved[MAIN + 2 * j : MAIN + 2 * j + 2], m_tail)
    o_tail = tail_tile(((c1 * c1 * c1) * x_tail + m_tail) * total).astype(bf16)
    for r in range(N_DP):
        o_ref[r, :, :CHUNK] = o_main
        o_ref[r, :, CHUNK:] = o_tail


def unpack_body(u_ref, o_ref):
    for d in range(N_DP):
        o_ref[:MAIN, d * CHUNK : (d + 1) * CHUNK] = u_ref[d, :, :CHUNK]
        tail = u_ref[d, :, CHUNK:].astype(f32)
        for k in range(GROUPS):
            piece = slice(d * CHUNK + 128 * k, d * CHUNK + 128 * k + 128)
            o_ref[MAIN:, piece] = tail[2 * k : 2 * k + 2].astype(bf16)


def exchange(x, axis):
    return lax.all_to_all(x, axis, split_axis=0, concat_axis=0, tiled=True)


def total_of(x):
    return jnp.sum(x.astype(f32), axis=0)


def shift(x, axis, n, k):
    return lax.ppermute(x, axis, [(i, (i + k) % n) for i in range(n)])


def others(x, axis, n, step=1):
    return [x] + [shift(x, axis, n, n - k) for k in range(step, n, step)]


def sum_over(x, axis, n, step=1):
    return pair_sums(others(x, axis, n, step))


def pair_sums(terms):
    terms = [y.astype(f32) for y in terms]
    while len(terms) > 1:
        half = len(terms) // 2
        terms = [terms[k] + terms[k + half] for k in range(half)]
    return terms[0].astype(bf16)


def sum_pair(x, axis, n):
    other = lax.ppermute(x, axis, [(i, i ^ 1) for i in range(n)])
    return (x.astype(f32) + other.astype(f32)).astype(bf16)


def local(kva_parts, kvb_parts, kva_moment, kvb_moment):
    y = lax.axis_index("y").astype(jnp.int32).reshape(1)
    c = lax.axis_index("c").astype(jnp.int32).reshape(1)
    z = lax.axis_index("z").astype(jnp.int32).reshape(1)
    d = y * 2 + c
    rows_b = KV_RANK // N_DP

    half = shape((kvb_parts.shape[1] // 2, KV_RANK), bf16)
    packed, send_b = call(
        pack_body,
        (shape((N_DP, MAIN, WIDE), bf16), half),
        1,
        2,
        [pltpu.VMEM(kva_parts.shape, bf16), pltpu.SemaphoreType.DMA((2,))],
        pl.ANY,
        67_000_000,
    )(c, kva_parts, kvb_parts)
    terms_a = exchange(packed, DP)
    grad_b = call(half_b_body, half, 1, 2)(c, kvb_parts, shift(send_b, "c", 2, 1))
    terms_a, grad_b = lax.optimization_barrier((terms_a, grad_b))
    grads_b = others(grad_b, "y", 4)
    grad_a, push_a = call(
        push_a_body,
        (shape((2 * MAIN, KV_RANK), bf16), shape((8, MAIN, WIDE), bf16)),
        1,
        2,
    )(d, terms_a, kva_moment)
    all_z = exchange(push_a, "z")

    rows = half.shape[0]
    both = call(sum_b_body, shape((rows + 2 * MAIN, KV_RANK), bf16), 0, 5, flops=HINT)(
        *grads_b, grad_a
    )
    both = lax.all_gather(both, "c")
    _, both = lax.optimization_barrier((all_z, both))
    all_a = others(all_z, "x", 4)
    moment_b, long_b, piece_b, grad_a = call(
        moment_b_body,
        (
            shape(kvb_moment.shape, f32),
            shape(kvb_moment.shape, bf16),
            shape((rows_b, KV_RANK), bf16),
            shape((2, 2 * MAIN, KV_RANK), bf16),
        ),
        1,
        2,
        [pltpu.VMEM((KV_RANK, KV_RANK), f32)],
    )(d, both, kvb_moment)
    terms_b = others(sum_pair(piece_b, "z", 8), "z", 8, 2)

    part = shape((64 * BLOCKS, 384), bf16)
    gram_a, send_a, short_a = call(
        gram_a_body,
        (part, part, shape((KVA_ROWS, CHUNK), bf16)),
        1,
        4,
        [pltpu.VMEM((128 * BLOCKS, 128 * BLOCKS), f32)],
    )(c, *all_a)
    _, terms_b = lax.optimization_barrier((send_a, terms_b))
    piece_b = pair_sums(terms_b)
    gram_a = pair_sums([gram_a, shift(send_a, "c", 2, 1)])
    gram_a = sum_over(gram_a, "y", 4)
    piece_b = lax.all_gather(sum_over(piece_b, "x", 4), "c", tiled=True)

    piece_b = jnp.concatenate([piece_b, grad_a.reshape(-1, KV_RANK)])
    gram_a, piece_b = lax.optimization_barrier((gram_a, piece_b))
    other_a = shift(gram_a, "c", 2, 1)
    pieces_b = others(piece_b, "y", 4)
    update_a = call(
        finish_a_body,
        shape((N_DP, MAIN, WIDE), bf16),
        2,
        3,
        [pltpu.VMEM((2,) + part.shape, bf16), pltpu.VMEM((128 * BLOCKS, 128 * BLOCKS), f32)]
        + [pltpu.VMEM((KVA_ROWS, KVA_ROWS), f32)] * 2,
        flops=HINT,
    )(z, c, gram_a, other_a, short_a)
    moment_a = call(moment_a_body, shape(kva_moment.shape, f32), 1, 5)(y, *pieces_b, kva_moment)
    update_a = call(unpack_body, shape(kva_moment.shape, bf16))(exchange(update_a, DP))
    update_b = call(
        finish_b_body,
        shape(long_b.shape, bf16),
        1,
        5,
        [pltpu.VMEM((KV_RANK, KV_RANK), f32)],
        flops=HINT,
    )(y, *pieces_b, long_b)
    return (moment_a, moment_b, update_a, update_b)


def solution(mesh):
    fine = Mesh(mesh.devices.reshape(4, 2, 4, 8), DP + FSDP)
    return jax.shard_map(
        local,
        mesh=fine,
        in_specs=(P(DP, FSDP, None), P(DP, FSDP, None), P(FSDP, None), P(FSDP, None)),
        out_specs=(P(FSDP, None), P(FSDP, None), P(FSDP, None), P(FSDP, None)),
        check_vma=False,
    )
```
